32 devices in a mesh: dp: 4 (over z), seq: 4 (over y, core), mp: 2 (over x).
Axes of the slice: x: 2, y: 2, z: 4, core: 2. Of those that a mesh axis runs over, the one named last changes fastest.
Arguments:
- tokens: bfloat16 [8, 2048, 2048], P('dp', 'seq'), may hold values from -6 to 6
- lengths: int32 [8], P('dp'), may hold values from 102 to 2048, as said below
- qkv_weight: bfloat16 [3, 2048, 2048], P(None, ('dp', 'seq'), 'mp'), may hold values from -0.125 to 0.125
- out_weight: bfloat16 [2048, 2048], P('mp', ('dp', 'seq')), may hold values from -0.125 to 0.125
- in_weight: bfloat16 [2048, 8192], P(('dp', 'seq'), 'mp'), may hold values from -0.125 to 0.125
- down_weight: bfloat16 [8192, 2048], P('mp', ('dp', 'seq')), may hold values from -0.0625 to 0.0625
- gain_in: bfloat16 [2048], P(('dp', 'seq')), may hold values from 0.099609375 to 1.8984375
- gain_attn: bfloat16 [32, 64], P('mp', ('dp', 'seq')), may hold values from 0.099609375 to 1.8984375
- gain_mid: bfloat16 [2048], P(('dp', 'seq')), may hold values from 0.099609375 to 1.8984375
- gain_ffn: bfloat16 [128, 64], P('mp', ('dp', 'seq')), may hold values from 0.099609375 to 1.8984375
- out_grad: bfloat16 [8, 2048, 2048], P('dp', 'seq'), may hold values from -6 to 6
Outputs:
- result: bfloat16 [8, 2048, 2048], P('dp', 'seq')
- grad_input: bfloat16 [8, 2048, 2048], P('dp', 'seq')
- grad_qkv: float32 [3, 2048, 2048], P(None, ('dp', 'seq'), 'mp')
- grad_out: float32 [2048, 2048], P('mp', ('dp', 'seq'))
- grad_in: float32 [2048, 8192], P(('dp', 'seq'), 'mp')
- grad_down: float32 [8192, 2048], P('mp', ('dp', 'seq'))
- grad_gain_in: float32 [2048], P(('dp', 'seq'))
- grad_gain_attn: float32 [32, 64], P('mp', ('dp', 'seq'))
- grad_gain_mid: float32 [2048], P(('dp', 'seq'))
- grad_gain_ffn: float32 [128, 64], P('mp', ('dp', 'seq'))
The draws below stay inside these ranges and needn't reach their ends.
Inputs may be any that keep to these rules, and one draw needn't show every extreme that they name: `lengths`: in each aligned group of 2 sequences (those of one index of dp) one sequence, drawn, has all 2048 tokens valid.
All inputs are finite; a program needn't handle non-finite values.
Results may differ from the reference program's by a relative error of at most 0.023.
Values may be sent and summed in bfloat16 or wider, within the bound.
No kernel may reach another device: no remote copies, remote signals or barrier semaphores. Data moves between devices by JAX's collectives and lax.ppermute only.
A program may use at most 512 MiB of HBM per device.

```python
import jax
import jax.numpy as jnp
from jax import lax

D = 2048
HEADS = 32
HEAD_DIM = 64
FF = 8192
SEQ_LEN = 2048
SEQS = 2
XPOS_BASE = 512
SPAN = 512
SEQUENCES = 8


def draw_lengths(key, part):
    key = jax.random.fold_in(key, 7)
    first_key, second_key = jax.random.split(key)
    shortest = max(1, SEQ_LEN // 20)
    base_lengths = jax.random.randint(first_key, (SEQUENCES,), shortest, SEQ_LEN + 1)
    group_count = SEQUENCES // SEQS
    chosen = jax.random.randint(second_key, (group_count,), 0, SEQS)
    full_rows = jnp.arange(SEQUENCES, dtype=jnp.int32) % SEQS == jnp.repeat(chosen, SEQS)
    return jnp.where(full_rows, SEQ_LEN, base_lengths).astype(jnp.int32)


def level_of(stream_key, shape, shards, smallest, high):
    def one(position, blocks):
        heights = jax.random.uniform(jax.random.fold_in(jax.random.fold_in(stream_key, 6), position), (blocks,), jnp.float32, smallest / len(shards), high / len(shards))
        return jnp.repeat(jnp.exp(heights), shape[position] // blocks).reshape((-1,) + (1,) * (len(shape) - position - 1))

    gain = one(*shards[0])
    for cut in shards[1:]:
        gain = gain * one(*cut)
    return gain


def gaussian(stream_key, extent, width, bound, shards=(), kind=jnp.bfloat16):
    drawn = jax.random.normal(stream_key, extent, jnp.float32) * width
    if len(shards) > 0:
        drawn = level_of(stream_key, extent, shards, -0.22, 0.18) * drawn
    return jnp.clip(drawn, min=-bound, max=bound).astype(kind)


def setup_inputs(seed: int = 0) -> dict:
    key_list = jax.random.split(jax.random.key(seed), 12)
    tokens = gaussian(key_list[0], (SEQUENCES, SEQ_LEN, D), 1.0, 6.0, ((0, 4), (1, 4)))
    lengths = draw_lengths(jax.random.fold_in(key_list[11], 71), 0)
    qkv_weight = gaussian(key_list[2], (3, D, D), D ** -0.5, 0.125, ((1, 16), (2, 2)))
    out_weight = gaussian(key_list[3], (D, D), D ** -0.5, 0.125, ((0, 2), (1, 16)))
    in_weight = gaussian(key_list[4], (D, FF), D ** -0.5, 0.125, ((0, 16), (1, 2)))
    down_weight = gaussian(key_list[5], (FF, D), FF ** -0.5, 0.0625, ((0, 2), (1, 16)))
    gain_in = jnp.clip(1.0 + 0.18 * jax.random.normal(key_list[6], (D,), jnp.float32), 0.099609375, 1.8984375).astype(jnp.bfloat16)
    gain_attn = jnp.clip(1.0 + 0.18 * jax.random.normal(key_list[7], (HEADS, HEAD_DIM), jnp.float32), 0.099609375, 1.8984375).astype(jnp.bfloat16)
    gain_mid = jnp.clip(1.0 + 0.18 * jax.random.normal(key_list[8], (D,), jnp.float32), 0.099609375, 1.8984375).astype(jnp.bfloat16)
    gain_ffn = jnp.clip(1.0 + 0.18 * jax.random.normal(key_list[9], (FF // HEAD_DIM, HEAD_DIM), jnp.float32), 0.099609375, 1.8984375).astype(jnp.bfloat16)
    out_grad = gaussian(key_list[10], (SEQUENCES, SEQ_LEN, D), 1.0, 6.0, ((0, 4), (1, 4)))
    return {"tokens": tokens, "lengths": lengths, "qkv_weight": qkv_weight, "out_weight": out_weight, "in_weight": in_weight, "down_weight": down_weight, "gain_in": gain_in, "gain_attn": gain_attn, "gain_mid": gain_mid, "gain_ffn": gain_ffn, "out_grad": out_grad}


@jax.custom_vjp
def low(v):
    return lax.optimization_barrier(v.astype(jnp.bfloat16)).astype(jnp.float32)

@jax.custom_vjp
def low_back(v):
    return v

def low_keep(v):
    return (low(v), None)

def low_pass(kept, grad):
    return (grad,)

def back_keep(v):
    return (v, None)

def back_low(kept, grad):
    return (low(grad),)
low.defvjp(low_keep, low_pass)
low_back.defvjp(back_keep, back_low)
exactly = lax.Precision.HIGHEST

def layer_norm(tensor, scales):
    row_mean = lax.optimization_barrier(jnp.mean(tensor, axis=-1, keepdims=True))
    row_var = lax.optimization_barrier(jnp.mean(jnp.square(tensor - row_mean), axis=-1, keepdims=True))
    return (tensor - row_mean) * lax.rsqrt(row_var + 1e-05) * scales

def xpos_tables(count):
    positions = jnp.arange(count, dtype=jnp.float32)
    half_dim = HEAD_DIM // 2
    pair_index = jnp.arange(half_dim, dtype=jnp.float32)
    frequency = 1.0 / 10000.0 ** (2.0 * pair_index / HEAD_DIM)
    angles = positions[:, None] * frequency[None, :]
    base_ratio = (2.0 * pair_index + 0.4 * HEAD_DIM) / (1.4 * HEAD_DIM)
    growth = base_ratio[None, :] ** ((positions[:, None] - SEQ_LEN // 2) / XPOS_BASE)
    return (jnp.cos(angles), jnp.sin(angles), growth)

def rotate(tensor, cosine_table, sine_table, factor):
    half_dim = HEAD_DIM // 2
    cos_scaled = (cosine_table * factor)[:, None, :]
    sin_scaled = (sine_table * factor)[:, None, :]
    front_half = tensor[..., :half_dim]
    back_half = tensor[..., half_dim:]
    return jnp.concatenate([front_half * cos_scaled - back_half * sin_scaled, back_half * cos_scaled + front_half * sin_scaled], axis=-1)

def forward(inputs, length, qkv_weight, out_weight, in_weight, down_weight, gain_in, gain_attn, gain_mid, gain_ffn):
    normed_one = low(layer_norm(inputs, gain_in))
    projected = low_back(jnp.einsum('td,jde->jte', normed_one, qkv_weight, precision=exactly))
    shaped = projected.reshape(3, SEQ_LEN, HEADS, HEAD_DIM)
    cosine_table, sine_table, growth = xpos_tables(SEQ_LEN)
    queries = low(rotate(shaped[0], cosine_table, sine_table, growth))
    keys_all = low(rotate(shaped[1], cosine_table, sine_table, 1.0 / growth))
    values_all = low(shaped[2])
    key_pos = jnp.arange(SEQ_LEN, dtype=jnp.int32)

    def one_block(offset):
        query_rows = lax.dynamic_slice_in_dim(queries, offset, SPAN, 0)
        scores = low_back(jnp.einsum('qhe,khe->hqk', query_rows, keys_all, precision=exactly) * 0.125)
        query_pos = offset + jnp.arange(SPAN, dtype=jnp.int32)
        allowed = (key_pos[None, :] <= query_pos[:, None]) & (key_pos[None, :] < length)
        masked = jnp.where(allowed[None], scores, -1e+30)
        row_max = lax.optimization_barrier(jnp.max(masked, axis=-1, keepdims=True))
        exponent = jnp.where(allowed[None], jnp.exp(masked - row_max), 0.0)
        attn_probs = low(exponent / lax.optimization_barrier(jnp.sum(exponent, axis=-1, keepdims=True)))
        return jnp.einsum('hqk,khe->qhe', attn_probs, values_all, precision=exactly)
    offsets = jnp.arange(SEQ_LEN // SPAN, dtype=jnp.int32) * SPAN
    mixed_out = lax.map(jax.checkpoint(one_block), offsets)
    attended = low_back(mixed_out.reshape(SEQ_LEN, D))
    inner_out = low(layer_norm(attended, gain_attn.reshape(D)))
    hidden = inputs + low_back(jnp.dot(inner_out, out_weight, precision=exactly))
    normed_mid = low(layer_norm(hidden, gain_mid))
    pre_act = low_back(jnp.dot(normed_mid, in_weight, precision=exactly))
    activated = jax.nn.gelu(pre_act, approximate=False)
    ffn_normed = low(layer_norm(activated, gain_ffn.reshape(FF)))
    return hidden + low_back(jnp.dot(ffn_normed, down_weight, precision=exactly))

def reference(tokens, lengths, qkv_weight, out_weight, in_weight, down_weight, gain_in, gain_attn, gain_mid, gain_ffn, out_grad):
    weights = tuple((argument.astype(jnp.float32) for argument in (qkv_weight, out_weight, in_weight, down_weight, gain_in, gain_attn, gain_mid, gain_ffn)))

    def one_sequence(totals, sliced):
        inputs, length, cotangent = sliced

        def run_layer(inputs_float, *layer_args):
            return forward(inputs_float, length, *layer_args)
        output, pullback = jax.vjp(run_layer, inputs.astype(jnp.float32), *weights)
        gradients = pullback(cotangent.astype(jnp.float32))
        totals = tuple((total_sum + grad_part for total_sum, grad_part in zip(totals, gradients[1:])))
        return (totals, (output.astype(jnp.bfloat16), gradients[0].astype(jnp.bfloat16)))
    initial = tuple((jnp.zeros(argument.shape, jnp.float32) for argument in weights))
    totals, (outputs, grad_inputs) = lax.scan(one_sequence, initial, (tokens, lengths, out_grad))
    return (outputs, grad_inputs, totals[0], totals[1], totals[2], totals[3], totals[4], totals[5], totals[6], totals[7])
```

```python
from functools import partial

import jax
import jax.numpy as jnp
from jax import lax
from jax.experimental import pallas as pl
from jax.experimental.pallas import tpu as pltpu
from jax.sharding import PartitionSpec as P

HEAD_DIM = 64
HALF = HEAD_DIM // 2
XPOS_BASE = 512
EPSILON = 1e-05
NEGATIVE = -1e30
LOG2_E = 1.4426950408889634
SCORE_SCALE = 0.125
VMEM = 56 * 2**20
BF16 = jnp.bfloat16
F32 = jnp.float32


def params(limit=VMEM):
    return pltpu.CompilerParams(vmem_limit_bytes=limit)


def dot(left, right, left_dim, right_dim):
    return lax.dot_general(
        left, right, (((left_dim,), (right_dim,)), ((), ())), preferred_element_type=F32
    )


def swap_halves(block):
    width = block.shape[1]
    if width % 128:
        pieces = []
        for start in range(0, width, HEAD_DIM):
            pieces += [block[:, start + HALF : start + HEAD_DIM], block[:, start : start + HALF]]
        return jnp.concatenate(pieces, axis=1)
    lane = lax.broadcasted_iota(jnp.int32, (block.shape[0], 128), 1) % HEAD_DIM
    pieces = []
    for start in range(0, width, 128):
        part = block[:, start : start + 128]
        pieces.append(
            jnp.where(lane < HALF, pltpu.roll(part, 128 - HALF, 1), pltpu.roll(part, HALF, 1))
        )
    return pieces[0] if len(pieces) == 1 else jnp.concatenate(pieces, axis=1)


def turned(block, cosine, sine, sign):
    lanes = cosine.shape[1]
    pieces = []
    for start in range(0, block.shape[1], lanes):
        part = block[:, start : start + lanes]
        pieces.append(part * cosine + sign * (swap_halves(part) * sine))
    return pieces[0] if len(pieces) == 1 else jnp.concatenate(pieces, axis=1)


def project_kernel(place, rows, weight, cos_q, sin_q, cos_k, sin_k, *outs):
    step = pl.program_id(0)
    block = rows[...]
    made = [dot(block, weight[j], 1, 0) for j in range(3)]
    made[0] = turned(made[0], cos_q[...], sin_q[...], 1)
    made[1] = turned(made[1], cos_k[...], sin_k[...], 1)
    for offset, out in enumerate(outs):

        @pl.when(step == offset)
        def _(out=out):
            for j in range(3):
                out[j] = made[j].astype(BF16)


def project(place, rows, qkv_full, tables, groups):
    span, width = rows.shape
    local = qkv_full.shape[2]
    share = local // groups
    if share % 128:
        weight = qkv_full.reshape(3, width, groups, share).transpose(2, 0, 1, 3)
        weight_spec = pl.BlockSpec(
            (None, 3, width, share), lambda o, p: (jnp.bitwise_xor(o, p[0]), 0, 0, 0)
        )
    else:
        weight = qkv_full
        weight_spec = pl.BlockSpec(
            (3, width, share), lambda o, p: (0, 0, jnp.bitwise_xor(o, p[0]))
        )
    table_spec = pl.BlockSpec(tables[0].shape, lambda o, p: (0, 0))
    return pl.pallas_call(
        project_kernel,
        grid_spec=pltpu.PrefetchScalarGridSpec(
            num_scalar_prefetch=1,
            grid=(groups,),
            in_specs=[pl.BlockSpec((span, width), lambda o, p: (0, 0)), weight_spec]
            + [table_spec] * 4,
            out_specs=[pl.BlockSpec((3, span, share), lambda o, p: (0, 0, 0))] * groups,
        ),
        out_shape=[jax.ShapeDtypeStruct((3, span, share), BF16)] * groups,
        compiler_params=params(),
        cost_estimate=pl.CostEstimate(
            flops=2 * 3 * span * width * local,
            bytes_accessed=2 * 3 * width * local,
            transcendentals=0,
        ),
        name="project",
    )(place, rows, weight, *tables)


def attend_kernel(meta, *refs, groups, heads, block):
    messages, rest = refs[:groups], refs[groups:]
    outs, log_ref = rest[:groups], rest[groups]
    q_all, k_all, vt_all, o_all = rest[groups + 1 :]
    step = pl.program_id(0)
    length, place = meta[0], meta[1]
    span = messages[0].shape[1]

    @pl.when(step == 0)
    def _():
        for offset, message in enumerate(messages):
            at = pl.multiple_of(jnp.bitwise_xor(place, offset) * span, span)
            q_all[pl.ds(at, span), :] = message[0]
            k_all[pl.ds(at, span), :] = message[1]
            for h in range(heads):
                lanes = slice(h * HEAD_DIM, (h + 1) * HEAD_DIM)
                vt_all[h, :, pl.ds(at, span)] = message[2, :, lanes].T

    start = pl.multiple_of(step * block, block)
    queries = [
        q_all[pl.ds(start, block), h * HEAD_DIM : (h + 1) * HEAD_DIM] for h in range(heads)
    ]
    scale = SCORE_SCALE * LOG2_E

    def keys_block(index, carry, masked):
        at = pl.multiple_of(index * block, block)
        if masked:
            key_pos = at + lax.broadcasted_iota(jnp.int32, (block, block), 0)
            query_pos = start + lax.broadcasted_iota(jnp.int32, (block, block), 1)
            allowed = (key_pos <= query_pos) & (key_pos < length)
        new = []
        for h in range(heads):
            top, total, mixed = carry[h]
            keys = k_all[pl.ds(at, block), h * HEAD_DIM : (h + 1) * HEAD_DIM]
            scores = dot(keys, queries[h], 1, 1)
            if masked:
                scores = jnp.where(allowed, scores, NEGATIVE)
            higher = jnp.maximum(top, jnp.max(scores, axis=0, keepdims=True))
            fade = jnp.exp2((top - higher) * scale)
            weights = jnp.exp2((scores - higher) * scale)
            total = total * fade + jnp.sum(weights, axis=0, keepdims=True)
            added = dot(vt_all[h, :, pl.ds(at, block)], weights.astype(BF16), 1, 0)
            new.append((higher, total, mixed * fade + added))
        return tuple(new)

    carry = tuple(
        (
            jnp.full((1, block), NEGATIVE, F32),
            jnp.zeros((1, block), F32),
            jnp.zeros((HEAD_DIM, block), F32),
        )
        for _ in range(heads)
    )
    whole = jnp.minimum(step, length // block)
    end = jnp.minimum(step + 1, (length + block - 1) // block)
    carry = lax.fori_loop(0, whole, lambda n, c: keys_block(n, c, False), carry)
    carry = lax.fori_loop(whole, end, lambda n, c: keys_block(n, c, True), carry)
    pieces = []
    for h in range(heads):
        top, total, mixed = carry[h]
        pieces.append((mixed / total).T)
        log_ref[h : h + 1, :] = top * scale + jnp.log2(total)
    o_all[pl.ds(start, block), :] = jnp.concatenate(pieces, axis=1).astype(BF16)

    @pl.when(step == pl.num_programs(0) - 1)
    def _():
        for offset, out in enumerate(outs):
            at = pl.multiple_of(jnp.bitwise_xor(place, offset) * span, span)
            out[...] = o_all[pl.ds(at, span), :]


def attend(meta, messages):
    groups = len(messages)
    _, span, share = messages[0].shape
    heads = share // HEAD_DIM
    count = groups * span
    block = min(512, span)
    message_spec = pl.BlockSpec((3, span, share), lambda n, m: (0, 0, 0))
    out_spec = pl.BlockSpec((span, share), lambda n, m: (0, 0))
    results = pl.pallas_call(
        partial(attend_kernel, groups=groups, heads=heads, block=block),
        grid_spec=pltpu.PrefetchScalarGridSpec(
            num_scalar_prefetch=1,
            grid=(count // block,),
            in_specs=[message_spec] * groups,
            out_specs=[out_spec] * groups + [pl.BlockSpec((heads, block), lambda n, m: (0, n))],
            scratch_shapes=[
                pltpu.VMEM((count, share), BF16),
                pltpu.VMEM((count, share), BF16),
                pltpu.VMEM((heads, HEAD_DIM, count), BF16),
                pltpu.VMEM((count, share), BF16),
            ],
        ),
        out_shape=[jax.ShapeDtypeStruct((span, share), BF16)] * groups
        + [jax.ShapeDtypeStruct((heads, count), F32)],
        compiler_params=params(),
        cost_estimate=pl.CostEstimate(
            flops=8 * count * count * share, bytes_accessed=8 * count * share, transcendentals=0
        ),
        name="attend",
    )(meta, *messages)
    return results[:groups], results[groups]


def attend_back_kernel(meta, *refs, groups, heads, block):
    messages, grads, mixed = refs[:groups], refs[groups : 2 * groups], refs[2 * groups : 3 * groups]
    log_ref, cos_q, sin_q, cos_k, sin_k = refs[3 * groups : 3 * groups + 5]
    outs = refs[3 * groups + 5 : 4 * groups + 5]
    scratch = refs[4 * groups + 5 :]
    q_all, k_all, v_all, g_all, kt_all, dot_all, dqt_all, dk_sum, dv_sum, out_all = scratch
    length, place = meta[0], meta[1]
    span = messages[0].shape[1]
    count = groups * span
    scale = SCORE_SCALE * LOG2_E

    def lanes(h):
        return slice(h * HEAD_DIM, (h + 1) * HEAD_DIM)

    for offset in range(groups):
        at = pl.multiple_of(jnp.bitwise_xor(place, offset) * span, span)
        message = messages[offset]
        q_all[pl.ds(at, span), :] = message[0]
        k_all[pl.ds(at, span), :] = message[1]
        v_all[pl.ds(at, span), :] = message[2]
        g_all[pl.ds(at, span), :] = grads[offset][...]
        both = grads[offset][...].astype(F32) * mixed[offset][...].astype(F32)
        for h in range(heads):
            kt_all[h, :, pl.ds(at, span)] = message[1, :, lanes(h)].T
            dot_all[h : h + 1, pl.ds(at, span)] = jnp.sum(
                both[:, lanes(h)].T, axis=0, keepdims=True
            )
    dqt_all[...] = jnp.zeros_like(dqt_all)
    query_blocks = count // block

    def keys_block(index, _):
        key_at = pl.multiple_of(index * block, block)
        keys = [k_all[pl.ds(key_at, block), lanes(h)] for h in range(heads)]
        values = [v_all[pl.ds(key_at, block), lanes(h)] for h in range(heads)]
        dk_sum[...] = jnp.zeros_like(dk_sum)
        dv_sum[...] = jnp.zeros_like(dv_sum)

        def query_block(index, _, masked):
            at = pl.multiple_of(index * block, block)
            if masked:
                key_pos = key_at + lax.broadcasted_iota(jnp.int32, (block, block), 0)
                query_pos = at + lax.broadcasted_iota(jnp.int32, (block, block), 1)
                allowed = (key_pos <= query_pos) & (key_pos < length)
            for h in range(heads):
                query = q_all[pl.ds(at, block), lanes(h)]
                grad = g_all[pl.ds(at, block), lanes(h)]
                scores = dot(keys[h], query, 1, 1)
                weights = jnp.exp2(scores * scale - log_ref[h : h + 1, pl.ds(at, block)])
                if masked:
                    weights = jnp.where(allowed, weights, 0.0)
                grad_weights = dot(values[h], grad, 1, 1)
                grad_scores = weights * (grad_weights - dot_all[h : h + 1, pl.ds(at, block)])
                grad_scores = grad_scores.astype(BF16)
                dv_sum[h] += dot(weights.astype(BF16), grad, 1, 0)
                dk_sum[h] += dot(grad_scores, query, 1, 0)
                dqt_all[h, :, pl.ds(at, block)] += dot(
                    kt_all[h, :, pl.ds(key_at, block)], grad_scores, 1, 0
                )
            return 0

        crosses = key_at + block > length
        whole = jnp.where(crosses, query_blocks, index + 1)
        lax.fori_loop(index, whole, partial(query_block, masked=True), 0)
        lax.fori_loop(whole, query_blocks, partial(query_block, masked=False), 0)
        dk = jnp.concatenate([dk_sum[h] for h in range(heads)], axis=1) * SCORE_SCALE
        dv = jnp.concatenate([dv_sum[h] for h in range(heads)], axis=1)
        turn = (cos_k[pl.ds(key_at, block), :], sin_k[pl.ds(key_at, block), :])
        out_all[1, pl.ds(key_at, block), :] = turned(dk, *turn, -1).astype(BF16)
        out_all[2, pl.ds(key_at, block), :] = dv.astype(BF16)
        return 0

    used = (length + block - 1) // block
    lax.fori_loop(0, used, keys_block, 0)

    def no_keys(index, _):
        at = pl.multiple_of(index * block, block)
        for j in (1, 2):
            out_all[j, pl.ds(at, block), :] = jnp.zeros((block, heads * HEAD_DIM), BF16)
        return 0

    lax.fori_loop(used, query_blocks, no_keys, 0)
    for index in range(query_blocks):
        at = slice(index * block, (index + 1) * block)
        dq = jnp.concatenate([dqt_all[h, :, at].T for h in range(heads)], axis=1) * SCORE_SCALE
        out_all[0, at, :] = turned(dq, cos_q[at, :], sin_q[at, :], -1).astype(BF16)
    for offset, out in enumerate(outs):
        at = pl.multiple_of(jnp.bitwise_xor(place, offset) * span, span)
        out[...] = out_all[:, pl.ds(at, span), :]


def attend_back(meta, messages, grads, mixed, logs, tables):
    groups = len(messages)
    _, span, share = messages[0].shape
    heads = share // HEAD_DIM
    count = groups * span
    block = min(512, span)
    message_spec = pl.BlockSpec((3, span, share), lambda n, m: (0, 0, 0))
    row_spec = pl.BlockSpec((span, share), lambda n, m: (0, 0))
    table_spec = pl.BlockSpec(tables[0].shape, lambda n, m: (0, 0))
    return pl.pallas_call(
        partial(attend_back_kernel, groups=groups, heads=heads, block=block),
        grid_spec=pltpu.PrefetchScalarGridSpec(
            num_scalar_prefetch=1,
            grid=(1,),
            in_specs=[message_spec] * groups
            + [row_spec] * (2 * groups)
            + [pl.BlockSpec(logs.shape, lambda n, m: (0, 0))]
            + [table_spec] * 4,
            out_specs=[message_spec] * groups,
            scratch_shapes=[pltpu.VMEM((count, share), BF16)] * 4
            + [
                pltpu.VMEM((heads, HEAD_DIM, count), BF16),
                pltpu.VMEM((heads, count), F32),
                pltpu.VMEM((heads, HEAD_DIM, count), F32),
                pltpu.VMEM((heads, block, HEAD_DIM), F32),
                pltpu.VMEM((heads, block, HEAD_DIM), F32),
                pltpu.VMEM((3, count, share), BF16),
            ],
        ),
        out_shape=[jax.ShapeDtypeStruct((3, span, share), BF16)] * groups,
        compiler_params=params(),
        cost_estimate=pl.CostEstimate(
            flops=16 * count * count * share, bytes_accessed=16 * count * share, transcendentals=0
        ),
        name="attend_back",
    )(meta, *messages, *grads, *mixed, logs, *tables)


def weight_grad_kernel(place, *refs, sequences, devices, groups, chunk):
    lefts, rights = refs[:sequences], refs[sequences : 2 * sequences]
    away, near, own = refs[2 * sequences : 2 * sequences + 3]
    turned_left = refs[2 * sequences + 3]
    span = lefts[0].shape[0]

    @pl.when(pl.program_id(0) == 0)
    def _():
        row = 0
        for offset in (3, 1, 2, 0):
            target = jnp.bitwise_xor(place[0], offset)
            for device in range(devices):
                at = pl.multiple_of((device * groups + target) * chunk, chunk)
                for s in range(sequences):
                    turned_left[row : row + chunk, s * span : (s + 1) * span] = lefts[s][
                        :, pl.ds(at, chunk)
                    ].T
                row += chunk

    block = devices * chunk
    parts = [away.at[:block], away.at[block:], near, own]
    for n, part in enumerate(parts):
        rows = slice(n * block, (n + 1) * block)
        total = dot(turned_left[rows, :span], rights[0][...], 1, 0)
        for s in range(1, sequences):
            total += dot(turned_left[rows, s * span : (s + 1) * span], rights[s][...], 1, 0)
        part[...] = total.astype(BF16)


def weight_grad(place, lefts, rights, devices, groups):
    sequences = len(lefts)
    span, width = lefts[0].shape
    columns = rights[0].shape[1]
    chunk = width // (devices * groups)
    tile = 512 if columns % 512 == 0 else 256
    half, quarter = width // 2, width // 4
    return pl.pallas_call(
        partial(
            weight_grad_kernel, sequences=sequences, devices=devices, groups=groups, chunk=chunk
        ),
        grid_spec=pltpu.PrefetchScalarGridSpec(
            num_scalar_prefetch=1,
            grid=(columns // tile,),
            in_specs=[pl.BlockSpec((span, width), lambda n, p: (0, 0))] * sequences
            + [pl.BlockSpec((span, tile), lambda n, p: (0, n))] * sequences,
            out_specs=[
                pl.BlockSpec((half, tile), lambda n, p: (0, n)),
                pl.BlockSpec((quarter, tile), lambda n, p: (0, n)),
                pl.BlockSpec((quarter, tile), lambda n, p: (0, n)),
            ],
            scratch_shapes=[pltpu.VMEM((width, sequences * span), BF16)],
        ),
        out_shape=[
            jax.ShapeDtypeStruct((half, columns), BF16),
            jax.ShapeDtypeStruct((quarter, columns), BF16),
            jax.ShapeDtypeStruct((quarter, columns), BF16),
        ],
        compiler_params=params(),
        cost_estimate=pl.CostEstimate(
            flops=2 * sequences * span * width * columns,
            bytes_accessed=2 * width * columns,
            transcendentals=0,
        ),
        name="weight_grad",
    )(place, *lefts, *rights)


def exchange(array, axis, size, offset):
    return lax.ppermute(array, axis, [(n, n ^ offset) for n in range(size)])


def scatter_sum(parts, groups):
    away, near, own = parts
    quarter = own.shape[0]
    got = exchange(away, "seq", groups, 1)
    near = (near.astype(F32) + got[:quarter].astype(F32)).astype(BF16)
    far = exchange(near, "seq", groups, 2)
    own = own.astype(F32) + got[quarter:].astype(F32) + far.astype(F32)
    return lax.psum_scatter(own.astype(BF16), "dp", scatter_dimension=0, tiled=True).astype(F32)


def unit_sum(low, units):
    if units != 2:
        return lax.psum(low, "mp").astype(F32)
    other = exchange(low, "mp", 2, 1)
    return low.astype(F32) + other.astype(F32)


def rounded(terms):
    return lax.optimization_barrier(terms.astype(BF16))


def gathered(pieces, place, groups):
    stacked = jnp.stack(pieces)
    ordered = [
        lax.dynamic_index_in_dim(stacked, jnp.bitwise_xor(place, n), 0, False)
        for n in range(groups)
    ]
    return jnp.concatenate([piece.transpose(1, 0, 2) for piece in ordered], axis=2)


def split_up(rows, place, groups):
    share = rows.shape[1] // groups
    return [
        lax.dynamic_slice_in_dim(rows, jnp.bitwise_xor(place, n) * share, share, 1)
        for n in range(groups)
    ]


def pass_round(pieces, groups):
    return [pieces[0]] + [exchange(pieces[n], "seq", groups, n) for n in range(1, groups)]


def full_norm(inputs, scales):
    row_mean = jnp.mean(inputs, axis=-1, keepdims=True)
    centered = inputs - row_mean
    row_var = jnp.mean(centered * centered, axis=-1, keepdims=True)
    inv_std = lax.rsqrt(row_var + EPSILON)
    normal = centered * inv_std
    return (normal * scales, normal, inv_std)


def full_norm_back(grad_out, normal, inv_std, scales):
    scaled = grad_out * scales
    return inv_std * (
        scaled
        - jnp.mean(scaled, axis=-1, keepdims=True)
        - normal * jnp.mean(scaled * normal, axis=-1, keepdims=True)
    )


def across_units(first_sum, second_sum, units):
    if units != 2:
        return lax.psum((first_sum, second_sum), "mp")
    sums = jnp.stack([first_sum, second_sum])
    return sums + exchange(sums, "mp", 2, 1)


def split_norm(inputs, scales, full_width, units):
    moment_sums = across_units(
        jnp.sum(inputs, axis=-1), jnp.sum(inputs * inputs, axis=-1), units
    )
    row_mean = moment_sums[0][:, None] / full_width
    row_var = moment_sums[1][:, None] / full_width - row_mean * row_mean
    inv_std = lax.rsqrt(row_var + EPSILON)
    normal = (inputs - row_mean) * inv_std
    return (normal * scales, normal, inv_std)


def split_norm_back(grad_out, normal, inv_std, scales, full_width, units):
    scaled = grad_out * scales
    moment_sums = across_units(
        jnp.sum(scaled, axis=-1), jnp.sum(scaled * normal, axis=-1), units
    )
    grad_in = inv_std * (
        scaled
        - moment_sums[0][:, None] / full_width
        - normal * moment_sums[1][:, None] / full_width
    )
    return (grad_in, jnp.sum(grad_out * normal, axis=0))


def xpos_tables(count, lanes):
    positions = jnp.arange(count, dtype=F32)
    pair_index = jnp.arange(HALF, dtype=F32)
    frequency = 1.0 / 10000.0 ** (2.0 * pair_index / HEAD_DIM)
    angles = positions[:, None] * frequency[None, :]
    base_ratio = (2.0 * pair_index + 0.4 * HEAD_DIM) / (1.4 * HEAD_DIM)
    growth = base_ratio[None, :] ** ((positions[:, None] - count // 2) / XPOS_BASE)
    cosine, sine = jnp.cos(angles), jnp.sin(angles)
    tables = []
    for factor in (growth, 1.0 / growth):
        tables.append(jnp.tile(cosine * factor, (1, lanes // HALF)))
        tables.append(
            jnp.tile(jnp.concatenate([-sine * factor, sine * factor], axis=1), (1, lanes // HEAD_DIM))
        )
    return tables


def body(
    devices,
    groups,
    units,
    tokens,
    lengths,
    qkv_weight,
    out_weight,
    in_weight,
    down_weight,
    gain_in,
    gain_attn,
    gain_mid,
    gain_ffn,
    out_grad,
):
    sequences, span, model = tokens.shape
    each = range(sequences)
    data = ("dp", "seq")
    shards = devices * groups
    place = lax.axis_index("seq").astype(jnp.int32)
    local_width = qkv_weight.shape[2]
    heads_here = local_width // HEAD_DIM
    ffn_width = in_weight.shape[1]
    share = local_width // groups

    sizes = [gain_in.size, gain_mid.size, gain_attn.size, gain_ffn.size]
    flat = jnp.concatenate(
        [gain_in, gain_mid, gain_attn.reshape(-1), gain_ffn.reshape(-1)]
    ).reshape(1, -1)
    all_gains = lax.all_gather(flat, data, axis=0, tiled=True).astype(F32)
    cuts = [sum(sizes[:n]) for n in range(5)]
    pieces = [all_gains[:, cuts[n] : cuts[n + 1]] for n in range(4)]
    gain_one, gain_three = pieces[0].reshape(-1), pieces[1].reshape(-1)
    gain_two = pieces[2].reshape(shards, heads_here, -1).transpose(1, 0, 2).reshape(-1)
    gain_four = (
        pieces[3].reshape(shards, ffn_width // HEAD_DIM, -1).transpose(1, 0, 2).reshape(-1)
    )

    qkv_full = lax.all_gather(qkv_weight, data, axis=1, tiled=True)
    out_full = lax.all_gather(out_weight, data, axis=1, tiled=True)
    in_full = lax.all_gather(in_weight, data, axis=0, tiled=True)
    down_full = lax.all_gather(down_weight, data, axis=1, tiled=True)

    count = span * groups
    tables = xpos_tables(count, min(128, share))
    tables_here = [lax.dynamic_slice_in_dim(t, place * span, span, 0) for t in tables]
    spot = place.reshape(1)
    metas = [jnp.stack([lengths[s], place]) for s in each]

    inputs = [tokens[s].astype(F32) for s in each]
    first = [full_norm(inputs[s], gain_one) for s in each]
    first_low = [first[s][0].astype(BF16) for s in each]

    messages = []
    for s in each:
        made = project(spot, first_low[s], qkv_full, tables_here, groups)
        messages.append(pass_round(made, groups))
    mixed, logs = [], []
    hidden, second, second_low = [], [], []
    for s in each:
        outs, log = attend(metas[s], messages[s])
        mixed.append(outs)
        logs.append(log)
        back = pass_round(outs, groups)
        attended = gathered([b[None] for b in back], place, groups).reshape(span, local_width)
        normed, plain, std = split_norm(attended.astype(F32), gain_two, model, units)
        second.append((plain, std))
        second_low.append(normed.astype(BF16))
        branch = rounded(jnp.dot(second_low[s], out_full, preferred_element_type=F32))
        hidden.append(inputs[s] + unit_sum(branch, units))

    third, third_low, fourth, fourth_low, gelu_backs, results = [], [], [], [], [], []
    for s in each:
        normed, plain, std = full_norm(hidden[s], gain_three)
        third.append((plain, std))
        third_low.append(normed.astype(BF16))
        pre_act = jnp.dot(third_low[s], in_full, preferred_element_type=F32)
        activated, gelu_back = jax.vjp(partial(jax.nn.gelu, approximate=False), pre_act)
        gelu_backs.append(gelu_back)
        normed, plain, std = split_norm(activated, gain_four, ffn_width * units, units)
        fourth.append((plain, std))
        fourth_low.append(normed.astype(BF16))

    grad_low = [out_grad[s] for s in each]
    pre_low, base_terms = [], []
    gain_four_grad = 0.0
    for s in each:
        grad_wide = dot(grad_low[s], down_full, 1, 1)
        grad_act, gain_part = split_norm_back(
            grad_wide, *fourth[s], gain_four, ffn_width * units, units
        )
        gain_four_grad += gain_part
        pre_low.append(gelu_backs[s](grad_act)[0].astype(BF16))
        base_terms.append(rounded(dot(pre_low[s], in_full, 1, 1)))
    grad_third = [unit_sum(base_terms[s], units) for s in each]

    in_parts = weight_grad(spot, third_low, pre_low, devices, groups)
    grad_in_w = scatter_sum(in_parts, groups)
    down_parts = weight_grad(spot, grad_low, fourth_low, devices, groups)
    grad_down_w = scatter_sum(down_parts, groups).T

    for s in each:
        branch = rounded(jnp.dot(fourth_low[s], down_full, preferred_element_type=F32))
        results.append((hidden[s] + unit_sum(branch, units)).astype(BF16))

    gain_three_grad, gain_two_grad = 0.0, 0.0
    grad_hidden, hidden_low, returned = [], [], []
    for s in each:
        gain_three_grad += jnp.sum(grad_third[s] * third[s][0], axis=0)
        grad_hidden.append(
            grad_low[s].astype(F32) + full_norm_back(grad_third[s], *third[s], gain_three)
        )
        hidden_low.append(grad_hidden[s].astype(BF16))
        grad_inner = dot(hidden_low[s], out_full, 1, 1)
        grad_attended, gain_part = split_norm_back(grad_inner, *second[s], gain_two, model, units)
        gain_two_grad += gain_part
        grads = pass_round(split_up(grad_attended.astype(BF16), place, groups), groups)
        made = attend_back(metas[s], messages[s], grads, mixed[s], logs[s], tables)
        back = pass_round(made, groups)
        returned.append(gathered(back, place, groups))
    out_parts = weight_grad(spot, hidden_low, second_low, devices, groups)
    grad_out_w = scatter_sum(out_parts, groups).T

    flat_returned = [returned[s].reshape(span, 3 * local_width) for s in each]
    gain_one_grad = 0.0
    first_terms = []
    for s in each:
        terms = jnp.einsum("tje,jde->td", returned[s], qkv_full, preferred_element_type=F32)
        gain_one_grad += jnp.sum(terms * first[s][1], axis=0)
        first_terms.append(rounded(terms))
    qkv_parts = weight_grad(spot, first_low, flat_returned, devices, groups)
    grad_qkv_w = scatter_sum(qkv_parts, groups).reshape(-1, 3, local_width).transpose(1, 0, 2)
    grad_inputs = []
    for s in each:
        grad_first = full_norm_back(
            unit_sum(first_terms[s], units), first[s][1], first[s][2], gain_one
        )
        grad_inputs.append((grad_hidden[s] + grad_first).astype(BF16))

    gain_rows = jnp.concatenate(
        [
            gain_one_grad.reshape(shards, -1),
            gain_three_grad.reshape(shards, -1),
            gain_two_grad.reshape(heads_here, shards, -1).transpose(1, 0, 2).reshape(shards, -1),
            gain_four_grad.reshape(ffn_width // HEAD_DIM, shards, -1)
            .transpose(1, 0, 2)
            .reshape(shards, -1),
        ],
        axis=1,
    )
    gain_sums = lax.psum_scatter(gain_rows, data, scatter_dimension=0, tiled=True).reshape(-1)
    one, three, two, four = [gain_sums[cuts[n] : cuts[n + 1]] for n in range(4)]
    return (
        jnp.stack(results),
        jnp.stack(grad_inputs),
        grad_qkv_w,
        grad_out_w,
        grad_in_w,
        grad_down_w,
        lax.psum(one, "mp"),
        two.reshape(gain_attn.shape),
        three,
        four.reshape(gain_ffn.shape),
    )


def solution(mesh):
    sizes = mesh.shape
    data = ("dp", "seq")
    in_specs = (
        P("dp", "seq", None),
        P("dp"),
        P(None, data, "mp"),
        P("mp", data),
        P(data, "mp"),
        P("mp", data),
        P(data),
        P("mp", data),
        P(data),
        P("mp", data),
        P("dp", "seq", None),
    )
    out_specs = (
        P("dp", "seq", None),
        P("dp", "seq", None),
        P(None, data, "mp"),
        P("mp", data),
        P(data, "mp"),
        P("mp", data),
        P(data),
        P("mp", data),
        P(data),
        P("mp", data),
    )
    run = partial(body, sizes["dp"], sizes["seq"], sizes["mp"])
    return jax.shard_map(run, mesh=mesh, in_specs=in_specs, out_specs=out_specs, check_vma=False)
```

```python
from functools import partial

import jax
import jax.numpy as jnp
from jax import lax
from jax.experimental import pallas as pl
from jax.experimental.pallas import tpu as pltpu
from jax.sharding import PartitionSpec as P

HEAD_DIM = 64
HALF = HEAD_DIM // 2
XPOS_BASE = 512
EPSILON = 1e-05
NEGATIVE = -1e30
LOG2_E = 1.4426950408889634
SCORE_SCALE = 0.125
VMEM = 56 * 2**20
Z_FIRST = True
BF16 = jnp.bfloat16
KERNEL_RATE = 0.25e9
BACK_WEIGHT = 25


def lasting(us):
    return pl.CostEstimate(flops=int(us * KERNEL_RATE), bytes_accessed=0, transcendentals=0)


F32 = jnp.float32


def params(limit=VMEM):
    return pltpu.CompilerParams(vmem_limit_bytes=limit)


def dot(left, right, left_dim, right_dim):
    return lax.dot_general(
        left, right, (((left_dim,), (right_dim,)), ((), ())), preferred_element_type=F32
    )


def swap_halves(block):
    width = block.shape[1]
    if width % 128:
        pieces = []
        for start in range(0, width, HEAD_DIM):
            pieces += [block[:, start + HALF : start + HEAD_DIM], block[:, start : start + HALF]]
        return jnp.concatenate(pieces, axis=1)
    lane = lax.broadcasted_iota(jnp.int32, (block.shape[0], 128), 1) % HEAD_DIM
    pieces = []
    for start in range(0, width, 128):
        part = block[:, start : start + 128]
        pieces.append(
            jnp.where(lane < HALF, pltpu.roll(part, 128 - HALF, 1), pltpu.roll(part, HALF, 1))
        )
    return pieces[0] if len(pieces) == 1 else jnp.concatenate(pieces, axis=1)


def turned(block, cosine, sine, sign):
    lanes = cosine.shape[1]
    pieces = []
    for start in range(0, block.shape[1], lanes):
        part = block[:, start : start + lanes]
        pieces.append(part * cosine + sign * (swap_halves(part) * sine))
    return pieces[0] if len(pieces) == 1 else jnp.concatenate(pieces, axis=1)


def project_kernel(place, rows, weight, cos_q, sin_q, cos_k, sin_k, *outs, extra):
    outs = outs[extra:]
    step = pl.program_id(0)
    block = rows[...]
    made = [dot(block, weight[j], 1, 0) for j in range(3)]
    made[0] = turned(made[0], cos_q[...], sin_q[...], 1)
    made[1] = turned(made[1], cos_k[...], sin_k[...], 1)
    for offset, out in enumerate(outs):

        @pl.when(step == offset)
        def _(out=out):
            for j in range(3):
                out[j] = made[j].astype(BF16)


def project(place, rows, qkv_full, tables, groups, after=()):
    span, width = rows.shape
    local = qkv_full.shape[2]
    share = local // groups
    if share % 128:
        weight = qkv_full.reshape(3, width, groups, share).transpose(2, 0, 1, 3)
        weight_spec = pl.BlockSpec(
            (None, 3, width, share), lambda o, p: (jnp.bitwise_xor(o, p[0]), 0, 0, 0)
        )
    else:
        weight = qkv_full
        weight_spec = pl.BlockSpec(
            (3, width, share), lambda o, p: (0, 0, jnp.bitwise_xor(o, p[0]))
        )
    table_spec = pl.BlockSpec(tables[0].shape, lambda o, p: (0, 0))
    return pl.pallas_call(
        partial(project_kernel, extra=len(after)),
        grid_spec=pltpu.PrefetchScalarGridSpec(
            num_scalar_prefetch=1,
            grid=(groups,),
            in_specs=[pl.BlockSpec((span, width), lambda o, p: (0, 0)), weight_spec]
            + [table_spec] * 4
            + [pl.BlockSpec(memory_space=pl.ANY)] * len(after),
            out_specs=[pl.BlockSpec((3, span, share), lambda o, p: (0, 0, 0))] * groups,
        ),
        out_shape=[jax.ShapeDtypeStruct((3, span, share), BF16)] * groups,
        compiler_params=params(),
        cost_estimate=lasting(1.2e-8 * span * width * local),
        name="project",
    )(place, rows, weight, *tables, *after)


def attend_kernel(meta, *refs, groups, heads, block, extra):
    messages, rest = refs[:groups], refs[groups + extra :]
    outs, log_ref = rest[:groups], rest[groups]
    q_all, k_all, vt_all, o_all = rest[groups + 1 :]
    step = pl.program_id(0)
    length, place = meta[0], meta[1]
    span = messages[0].shape[1]

    @pl.when(step == 0)
    def _():
        for offset, message in enumerate(messages):
            at = pl.multiple_of(jnp.bitwise_xor(place, offset) * span, span)
            q_all[pl.ds(at, span), :] = message[0]
            k_all[pl.ds(at, span), :] = message[1]
            for h in range(heads):
                lanes = slice(h * HEAD_DIM, (h + 1) * HEAD_DIM)
                vt_all[h, :, pl.ds(at, span)] = message[2, :, lanes].T

    start = pl.multiple_of(step * block, block)
    queries = [
        q_all[pl.ds(start, block), h * HEAD_DIM : (h + 1) * HEAD_DIM] for h in range(heads)
    ]
    scale = SCORE_SCALE * LOG2_E

    def keys_block(index, carry, masked):
        at = pl.multiple_of(index * block, block)
        if masked:
            key_pos = at + lax.broadcasted_iota(jnp.int32, (block, block), 0)
            query_pos = start + lax.broadcasted_iota(jnp.int32, (block, block), 1)
            allowed = (key_pos <= query_pos) & (key_pos < length)
        new = []
        for h in range(heads):
            top, total, mixed = carry[h]
            keys = k_all[pl.ds(at, block), h * HEAD_DIM : (h + 1) * HEAD_DIM]
            scores = dot(keys, queries[h], 1, 1)
            if masked:
                scores = jnp.where(allowed, scores, NEGATIVE)
            higher = jnp.maximum(top, jnp.max(scores, axis=0, keepdims=True))
            fade = jnp.exp2((top - higher) * scale)
            weights = jnp.exp2((scores - higher) * scale)
            total = total * fade + jnp.sum(weights, axis=0, keepdims=True)
            added = dot(vt_all[h, :, pl.ds(at, block)], weights.astype(BF16), 1, 0)
            new.append((higher, total, mixed * fade + added))
        return tuple(new)

    carry = tuple(
        (
            jnp.full((1, block), NEGATIVE, F32),
            jnp.zeros((1, block), F32),
            jnp.zeros((HEAD_DIM, block), F32),
        )
        for _ in range(heads)
    )
    whole = jnp.minimum(step, length // block)
    end = jnp.minimum(step + 1, (length + block - 1) // block)
    carry = lax.fori_loop(0, whole, lambda n, c: keys_block(n, c, False), carry)
    carry = lax.fori_loop(whole, end, lambda n, c: keys_block(n, c, True), carry)
    pieces = []
    for h in range(heads):
        top, total, mixed = carry[h]
        pieces.append((mixed / total).T)
        log_ref[h : h + 1, :] = top * scale + jnp.log2(total)
    o_all[pl.ds(start, block), :] = jnp.concatenate(pieces, axis=1).astype(BF16)

    @pl.when(step == pl.num_programs(0) - 1)
    def _():
        for offset, out in enumerate(outs):
            at = pl.multiple_of(jnp.bitwise_xor(place, offset) * span, span)
            out[...] = o_all[pl.ds(at, span), :]


def attend(meta, messages, after=()):
    groups = len(messages)
    _, span, share = messages[0].shape
    heads = share // HEAD_DIM
    count = groups * span
    block = min(512, span)
    message_spec = pl.BlockSpec((3, span, share), lambda n, m: (0, 0, 0))
    out_spec = pl.BlockSpec((span, share), lambda n, m: (0, 0))
    results = pl.pallas_call(
        partial(attend_kernel, groups=groups, heads=heads, block=block, extra=len(after)),
        grid_spec=pltpu.PrefetchScalarGridSpec(
            num_scalar_prefetch=1,
            grid=(count // block,),
            in_specs=[message_spec] * groups
            + [pl.BlockSpec(memory_space=pl.ANY)] * len(after),
            out_specs=[out_spec] * groups + [pl.BlockSpec((heads, block), lambda n, m: (0, n))],
            scratch_shapes=[
                pltpu.VMEM((count, share), BF16),
                pltpu.VMEM((count, share), BF16),
                pltpu.VMEM((heads, HEAD_DIM, count), BF16),
                pltpu.VMEM((count, share), BF16),
            ],
        ),
        out_shape=[jax.ShapeDtypeStruct((span, share), BF16)] * groups
        + [jax.ShapeDtypeStruct((heads, count), F32)],
        compiler_params=params(),
        cost_estimate=lasting(2.9e-8 * count * count * share),
        name="attend",
    )(meta, *messages, *after)
    return results[:groups], results[groups]


def attend_back_kernel(meta, *refs, groups, heads, block, extra):
    messages, grads, mixed = refs[:groups], refs[groups : 2 * groups], refs[2 * groups : 3 * groups]
    log_ref, cos_q, sin_q, cos_k, sin_k = refs[3 * groups : 3 * groups + 5]
    refs = refs[3 * groups + 5 + extra :]
    outs, scratch = refs[:groups], refs[groups:]
    q_all, k_all, v_all, g_all, kt_all, dot_all, dqt_all, dk_sum, dv_sum, out_all = scratch
    length, place = meta[0], meta[1]
    span = messages[0].shape[1]
    count = groups * span
    scale = SCORE_SCALE * LOG2_E

    def lanes(h):
        return slice(h * HEAD_DIM, (h + 1) * HEAD_DIM)

    for offset in range(groups):
        at = pl.multiple_of(jnp.bitwise_xor(place, offset) * span, span)
        message = messages[offset]
        q_all[pl.ds(at, span), :] = message[0]
        k_all[pl.ds(at, span), :] = message[1]
        v_all[pl.ds(at, span), :] = message[2]
        g_all[pl.ds(at, span), :] = grads[offset][...]
        both = grads[offset][...].astype(F32) * mixed[offset][...].astype(F32)
        for h in range(heads):
            kt_all[h, :, pl.ds(at, span)] = message[1, :, lanes(h)].T
            dot_all[h : h + 1, pl.ds(at, span)] = jnp.sum(
                both[:, lanes(h)].T, axis=0, keepdims=True
            )
    dqt_all[...] = jnp.zeros_like(dqt_all)
    query_blocks = count // block

    def keys_block(index, _):
        key_at = pl.multiple_of(index * block, block)
        keys = [k_all[pl.ds(key_at, block), lanes(h)] for h in range(heads)]
        values = [v_all[pl.ds(key_at, block), lanes(h)] for h in range(heads)]
        dk_sum[...] = jnp.zeros_like(dk_sum)
        dv_sum[...] = jnp.zeros_like(dv_sum)

        def query_block(index, _, masked):
            at = pl.multiple_of(index * block, block)
            if masked:
                key_pos = key_at + lax.broadcasted_iota(jnp.int32, (block, block), 0)
                query_pos = at + lax.broadcasted_iota(jnp.int32, (block, block), 1)
                allowed = (key_pos <= query_pos) & (key_pos < length)
            for h in range(heads):
                query = q_all[pl.ds(at, block), lanes(h)]
                grad = g_all[pl.ds(at, block), lanes(h)]
                scores = dot(keys[h], query, 1, 1)
                weights = jnp.exp2(scores * scale - log_ref[h : h + 1, pl.ds(at, block)])
                if masked:
                    weights = jnp.where(allowed, weights, 0.0)
                grad_weights = dot(values[h], grad, 1, 1)
                grad_scores = weights * (grad_weights - dot_all[h : h + 1, pl.ds(at, block)])
                grad_scores = grad_scores.astype(BF16)
                dv_sum[h] += dot(weights.astype(BF16), grad, 1, 0)
                dk_sum[h] += dot(grad_scores, query, 1, 0)
                dqt_all[h, :, pl.ds(at, block)] += dot(
                    kt_all[h, :, pl.ds(key_at, block)], grad_scores, 1, 0
                )
            return 0

        crosses = key_at + block > length
        whole = jnp.where(crosses, query_blocks, index + 1)
        lax.fori_loop(index, whole, partial(query_block, masked=True), 0)
        lax.fori_loop(whole, query_blocks, partial(query_block, masked=False), 0)
        dk = jnp.concatenate([dk_sum[h] for h in range(heads)], axis=1) * SCORE_SCALE
        dv = jnp.concatenate([dv_sum[h] for h in range(heads)], axis=1)
        turn = (cos_k[pl.ds(key_at, block), :], sin_k[pl.ds(key_at, block), :])
        out_all[1, pl.ds(key_at, block), :] = turned(dk, *turn, -1).astype(BF16)
        out_all[2, pl.ds(key_at, block), :] = dv.astype(BF16)
        return 0

    used = (length + block - 1) // block
    lax.fori_loop(0, used, keys_block, 0)

    def no_keys(index, _):
        at = pl.multiple_of(index * block, block)
        for j in (1, 2):
            out_all[j, pl.ds(at, block), :] = jnp.zeros((block, heads * HEAD_DIM), BF16)
        return 0

    lax.fori_loop(used, query_blocks, no_keys, 0)
    for index in range(query_blocks):
        at = slice(index * block, (index + 1) * block)
        dq = jnp.concatenate([dqt_all[h, :, at].T for h in range(heads)], axis=1) * SCORE_SCALE
        out_all[0, at, :] = turned(dq, cos_q[at, :], sin_q[at, :], -1).astype(BF16)
    for offset, out in enumerate(outs):
        at = pl.multiple_of(jnp.bitwise_xor(place, offset) * span, span)
        out[...] = out_all[:, pl.ds(at, span), :]


def attend_back(meta, messages, grads, mixed, logs, tables, after=(), weight=1):
    groups = len(messages)
    _, span, share = messages[0].shape
    heads = share // HEAD_DIM
    count = groups * span
    block = min(512, span)
    message_spec = pl.BlockSpec((3, span, share), lambda n, m: (0, 0, 0))
    row_spec = pl.BlockSpec((span, share), lambda n, m: (0, 0))
    table_spec = pl.BlockSpec(tables[0].shape, lambda n, m: (0, 0))
    return pl.pallas_call(
        partial(
            attend_back_kernel, groups=groups, heads=heads, block=block, extra=len(after)
        ),
        grid_spec=pltpu.PrefetchScalarGridSpec(
            num_scalar_prefetch=1,
            grid=(1,),
            in_specs=[message_spec] * groups
            + [row_spec] * (2 * groups)
            + [pl.BlockSpec(logs.shape, lambda n, m: (0, 0))]
            + [table_spec] * 4
            + [pl.BlockSpec(memory_space=pl.ANY)] * len(after),
            out_specs=[message_spec] * groups,
            scratch_shapes=[pltpu.VMEM((count, share), BF16)] * 4
            + [
                pltpu.VMEM((heads, HEAD_DIM, count), BF16),
                pltpu.VMEM((heads, count), F32),
                pltpu.VMEM((heads, HEAD_DIM, count), F32),
                pltpu.VMEM((heads, block, HEAD_DIM), F32),
                pltpu.VMEM((heads, block, HEAD_DIM), F32),
                pltpu.VMEM((3, count, share), BF16),
            ],
        ),
        out_shape=[jax.ShapeDtypeStruct((3, span, share), BF16)] * groups,
        compiler_params=params(),
        cost_estimate=lasting(4.2e-8 * count * count * share * weight),
        name="attend_back",
    )(meta, *messages, *grads, *mixed, logs, *tables, *after)


def normed_rows(block, column_mean, column_std, gain):
    return (block.astype(F32) - column_mean) * column_std * gain


def moments(own, other, width):
    total = own + other
    mean = total[0:1] / width
    return mean, lax.rsqrt(total[1:2] / width - mean * mean + EPSILON)


def as_column(row):
    return jnp.broadcast_to(row, (128, row.shape[1])).T[:, 0:1]


def as_row(block):
    width = block.shape[1]
    part = block[:, 0:128]
    for start in range(128, width, 128):
        part = part + block[:, start : start + 128]
    return jnp.sum(part.T, axis=0, keepdims=True)


def weight_grad_kernel(place, *refs, sequences, devices, groups, chunk, offsets, normed, extra):
    lefts, refs = refs[:sequences], refs[sequences:]
    rights, refs = refs[:sequences], refs[sequences:]
    if normed:
        own_sums, other_sums, gain = refs[:sequences], refs[sequences : 2 * sequences], refs[2 * sequences]
        refs = refs[2 * sequences + 1 :]
    away, kept, turned_left = refs[extra : extra + 3]
    columns_ref = refs[extra + 3] if normed else None
    span = lefts[0].shape[0]

    @pl.when(pl.program_id(0) == 0)
    def _():
        row = 0
        for device, offset in offsets:
            target = jnp.bitwise_xor(place[0], offset)
            at = pl.multiple_of((device * groups + target) * chunk, chunk)
            for s in range(sequences):
                turned_left[row : row + chunk, s * span : (s + 1) * span] = lefts[s][
                    :, pl.ds(at, chunk)
                ].T
            row += chunk
        if normed:
            for s in range(sequences):
                mean, std = moments(own_sums[s][...], other_sums[s][...], normed)
                columns_ref[2 * s] = jnp.broadcast_to(as_column(mean), (span, 128))
                columns_ref[2 * s + 1] = jnp.broadcast_to(as_column(std), (span, 128))

    values = []
    for s in range(sequences):
        block = rights[s][...]
        if normed:
            block = normed_rows(
                block, columns_ref[2 * s, :, 0:1], columns_ref[2 * s + 1, :, 0:1], gain[...]
            ).astype(BF16)
        values.append(block)
    block = turned_left.shape[0] // 4
    parts = [away.at[:block], away.at[block:], kept.at[:block], kept.at[block:]]
    for n, part in enumerate(parts):
        rows = slice(n * block, (n + 1) * block)
        total = dot(turned_left[rows, :span], values[0], 1, 0)
        for s in range(1, sequences):
            total += dot(turned_left[rows, s * span : (s + 1) * span], values[s], 1, 0)
        part[...] = total.astype(BF16)


def weight_grad(place, lefts, rights, devices, groups, norm=None, z_first=False, after=()):
    sequences = len(lefts)
    span, width = lefts[0].shape
    layers = rights[0].ndim == 3
    columns = rights[0].shape[0] * rights[0].shape[2] if layers else rights[0].shape[1]
    chunk = width // (devices * groups)
    tile = 512 if rights[0].shape[-1] % 512 == 0 else rights[0].shape[-1]
    half = width // 2
    if z_first:
        offsets = [(d, o) for core in (1, 0) for d in range(devices) for o in (2 + core, core)]
    else:
        offsets = [(d, o) for o in (3, 1, 2, 0) for d in range(devices)]
    if layers:
        tiles = rights[0].shape[2] // tile
        right_spec = pl.BlockSpec((None, span, tile), lambda n, p: (n // tiles, 0, n % tiles))
    else:
        right_spec = pl.BlockSpec((span, tile), lambda n, p: (0, n))
    in_specs = [pl.BlockSpec((span, width), lambda n, p: (0, 0))] * sequences
    in_specs += [right_spec] * sequences
    operands = [*lefts, *rights]
    scratch = [pltpu.VMEM((width, sequences * span), BF16)]
    full = 0
    if norm:
        own_sums, other_sums, gain, full = norm
        in_specs += [pl.BlockSpec((2, span), lambda n, p: (0, 0))] * (2 * sequences)
        in_specs += [pl.BlockSpec((1, tile), lambda n, p: (0, n))]
        operands += [*own_sums, *other_sums, gain]
        scratch += [pltpu.VMEM((2 * sequences, span, 128), F32)]
    in_specs += [pl.BlockSpec(memory_space=pl.ANY)] * len(after)
    return pl.pallas_call(
        partial(
            weight_grad_kernel,
            sequences=sequences,
            devices=devices,
            groups=groups,
            chunk=chunk,
            offsets=offsets,
            normed=full,
            extra=len(after),
        ),
        grid_spec=pltpu.PrefetchScalarGridSpec(
            num_scalar_prefetch=1,
            grid=(columns // tile,),
            in_specs=in_specs,
            out_specs=[pl.BlockSpec((half, tile), lambda n, p: (0, n))] * 2,
            scratch_shapes=scratch,
        ),
        out_shape=[jax.ShapeDtypeStruct((half, columns), BF16)] * 2,
        compiler_params=params(),
        cost_estimate=lasting(2.9e-9 * sequences * span * width * columns),
        name="weight_grad",
    )(place, *operands, *after)


def call(kernel, name, grid, ins, outs, scratch, us, after=(), scalars=None):
    extra = len(after)
    first = 0 if scalars is None else 1
    count = first + len(ins)

    def run(*refs):
        kernel(*refs[:count], *refs[count + extra :])

    def spec(block, index):
        if index is None:
            return pl.BlockSpec(block, lambda *_: (0,) * len(block))
        return pl.BlockSpec(block, index)

    return pl.pallas_call(
        run,
        grid_spec=pltpu.PrefetchScalarGridSpec(
            num_scalar_prefetch=first,
            grid=grid,
            in_specs=[spec(block, index) for _, block, index in ins]
            + [pl.BlockSpec(memory_space=pl.ANY)] * extra,
            out_specs=[spec(block, index) for _, _, block, index in outs],
            scratch_shapes=scratch,
        ),
        out_shape=[jax.ShapeDtypeStruct(shape, dtype) for shape, dtype, _, _ in outs],
        compiler_params=params(),
        cost_estimate=lasting(us),
        name=name,
    )(*(() if scalars is None else (scalars,)), *[array for array, _, _ in ins], *after)


def collect_kernel(place, *refs, groups):
    pieces, (whole, sums) = refs[:groups], refs[groups:]
    share = pieces[0].shape[1]
    total, squares = 0.0, 0.0
    for offset, piece in enumerate(pieces):
        at = pl.multiple_of(jnp.bitwise_xor(place[0], offset) * share, share)
        block = piece[...]
        whole[:, pl.ds(at, share)] = block
        wide = block.astype(F32)
        total += as_row(wide)
        squares += as_row(wide * wide)
    sums[...] = jnp.concatenate([total, squares], axis=0)


def collect(place, pieces, after=()):
    groups = len(pieces)
    span, share = pieces[0].shape
    if share % 128:
        stacked = jnp.stack(pieces)
        whole = jnp.concatenate(
            [
                lax.dynamic_index_in_dim(stacked, jnp.bitwise_xor(place[0], n), 0, False)
                for n in range(groups)
            ],
            axis=1,
        )
        wide = whole.astype(F32)
        return whole, jnp.stack([jnp.sum(wide, axis=1), jnp.sum(wide * wide, axis=1)])
    width = groups * share
    return call(
        partial(collect_kernel, groups=groups),
        "collect",
        (1,),
        [(piece, (span, share), None) for piece in pieces],
        [((span, width), BF16, (span, width), None), ((2, span), F32, (2, span), None)],
        [],
        5e-6 * span * width,
        after,
        place,
    )


def out_kernel(mixed, own, other, gain, weight, inner, branch, *, full):
    mean, std = moments(own[...], other[...], full)
    low = normed_rows(mixed[...], as_column(mean), as_column(std), gain[...]).astype(BF16)
    inner[...] = low
    branch[...] = dot(low, weight[...], 1, 1).astype(BF16)


def out_branch(mixed, own, other, gain, near_full, full, after=()):
    span, width = mixed.shape
    model = near_full.shape[0]
    place = near_full.shape[1] // width - 1
    rows = min(256, span)
    return call(
        partial(out_kernel, full=full),
        "out_branch",
        (span // rows,),
        [
            (mixed, (rows, width), lambda n: (n, 0)),
            (own, (2, rows), lambda n: (0, n)),
            (other, (2, rows), lambda n: (0, n)),
            (gain, (1, width), None),
            (near_full, (model, width), lambda n: (0, place)),
        ],
        [
            ((span, width), BF16, (rows, width), lambda n: (n, 0)),
            ((span, model), BF16, (rows, model), lambda n: (n, 0)),
        ],
        [],
        6e-9 * span * width * model,
        after,
    )


def row_norm(block):
    mean = jnp.mean(block, axis=-1, keepdims=True)
    centered = block - mean
    std = lax.rsqrt(jnp.mean(centered * centered, axis=-1, keepdims=True) + EPSILON)
    return centered * std, std


def widen_kernel(tokens, own, other, gain, weight, hidden, low, active, slope, sums, total, squares):
    step = pl.program_id(0)

    @pl.when(step == 0)
    def _():
        block = tokens[...].astype(F32) + (own[...].astype(F32) + other[...].astype(F32))
        hidden[...] = block
        normal, _ = row_norm(block)
        low[...] = (normal * gain[...]).astype(BF16)
        total[...] = jnp.zeros_like(total)
        squares[...] = jnp.zeros_like(squares)

    pre = dot(low[...], weight[...], 1, 0)
    below = 0.5 + 0.5 * lax.erf(pre * 0.7071067811865476)
    value = pre * below
    active[...] = value.astype(BF16)
    slope[...] = (below + pre * (0.3989422804014327 * jnp.exp2(pre * pre * (-0.5 * LOG2_E)))).astype(
        BF16
    )
    part, square = total[...], squares[...]
    for start in range(0, value.shape[1], 128):
        piece = value[:, start : start + 128]
        part += piece
        square += piece * piece
    total[...] = part
    squares[...] = square

    @pl.when(step == pl.num_programs(0) - 1)
    def _():
        sums[...] = jnp.concatenate([as_row(total[...]), as_row(squares[...])], axis=0)


def widen(tokens, own, other, gain, weight, units, after=()):
    span, model = tokens.shape
    tile = 512
    rows = (span, model)
    across = (span, tile)
    return call(
        widen_kernel,
        "widen",
        (units // tile,),
        [
            (tokens, rows, None),
            (own, rows, None),
            (other, rows, None),
            (gain, (1, model), None),
            (weight, (model, tile), lambda n: (0, n)),
        ],
        [
            (rows, F32, rows, None),
            (rows, BF16, rows, None),
            ((span, units), BF16, across, lambda n: (0, n)),
            ((span, units), BF16, across, lambda n: (0, n)),
            ((2, span), F32, (2, span), None),
        ],
        [pltpu.VMEM((span, 128), F32)] * 2,
        5.4e-9 * span * model * units,
        after,
    )


def narrow_kernel(active, own, other, gain, weight, branch, total, columns, *, full):
    step = pl.program_id(0)

    @pl.when(step == 0)
    def _():
        mean, std = moments(own[...], other[...], full)
        columns[0] = jnp.broadcast_to(as_column(mean), columns.shape[1:])
        columns[1] = jnp.broadcast_to(as_column(std), columns.shape[1:])
        total[...] = jnp.zeros_like(total)

    low = normed_rows(active[...], columns[0, :, 0:1], columns[1, :, 0:1], gain[...]).astype(BF16)
    total[...] += dot(low, weight[...], 1, 0)

    @pl.when(step == pl.num_programs(0) - 1)
    def _():
        branch[...] = total[...].astype(BF16)


def narrow(active, own, other, gain, weight, full, after=()):
    span, units = active.shape
    model = weight.shape[1]
    tile = 512
    sums = (2, span)
    return call(
        partial(narrow_kernel, full=full),
        "narrow",
        (units // tile,),
        [
            (active, (span, tile), lambda n: (0, n)),
            (own, sums, None),
            (other, sums, None),
            (gain, (1, tile), lambda n: (0, n)),
            (weight, (tile, model), lambda n: (n, 0)),
        ],
        [((span, model), BF16, (span, model), None)],
        [pltpu.VMEM((span, model), F32), pltpu.VMEM((2, span, 128), F32)],
        3.7e-9 * span * model * units,
        after,
    )[0]


def wide_back_kernel(
    grads, weight, active, own, other, gain, scaled, sums, gain_grad, columns, total, weighted, *, full
):
    step = pl.program_id(0)

    @pl.when(step == 0)
    def _():
        mean, std = moments(own[...], other[...], full)
        columns[0] = jnp.broadcast_to(as_column(mean), columns.shape[1:])
        columns[1] = jnp.broadcast_to(as_column(std), columns.shape[1:])
        total[...] = jnp.zeros_like(total)
        weighted[...] = jnp.zeros_like(weighted)

    grad = dot(grads[...], weight[...], 1, 1)
    normal = (active[...].astype(F32) - columns[0, :, 0:1]) * columns[1, :, 0:1]
    product = grad * normal
    gain_grad[...] = jnp.sum(product, axis=0, keepdims=True)
    scaled[...] = (grad * gain[...]).astype(BF16)
    product = product * gain[...]
    part, other_part = total[...], weighted[...]
    for start in range(0, grad.shape[1], 128):
        at = slice(start, start + 128)
        part += grad[:, at] * gain[:, at]
        other_part += product[:, at]
    total[...] = part
    weighted[...] = other_part

    @pl.when(step == pl.num_programs(0) - 1)
    def _():
        sums[...] = jnp.concatenate([as_row(total[...]), as_row(weighted[...])], axis=0)


def wide_back(grads, weight, active, own, other, gain, full, after=()):
    span, units = active.shape
    model = weight.shape[1]
    tile = 512
    sums = (2, span)
    across = (span, tile)
    return call(
        partial(wide_back_kernel, full=full),
        "wide_back",
        (units // tile,),
        [
            (grads, (span, model), None),
            (weight, (tile, model), lambda n: (n, 0)),
            (active, across, lambda n: (0, n)),
            (own, sums, None),
            (other, sums, None),
            (gain, (1, tile), lambda n: (0, n)),
        ],
        [
            ((span, units), BF16, across, lambda n: (0, n)),
            (sums, F32, sums, None),
            ((1, units), F32, (1, tile), lambda n: (0, n)),
        ],
        [pltpu.VMEM((2, span, 128), F32)] + [pltpu.VMEM((span, 128), F32)] * 2,
        4.2e-9 * span * model * units,
        after,
    )


def pre_back_kernel(
    scaled, active, slope, own, other, own_back, other_back, weight, grads, branch, total, columns, *, full
):
    step = pl.program_id(0)

    @pl.when(step == 0)
    def _():
        mean, std = moments(own[...], other[...], full)
        back = (own_back[...] + other_back[...]) / full
        for n, row in enumerate((mean, std, back[0:1], back[1:2])):
            columns[n] = jnp.broadcast_to(as_column(row), columns.shape[1:])
        total[...] = jnp.zeros_like(total)

    std = columns[1, :, 0:1]
    normal = (active[...].astype(F32) - columns[0, :, 0:1]) * std
    grad = std * (scaled[...].astype(F32) - columns[2, :, 0:1] - normal * columns[3, :, 0:1])
    low = (grad * slope[...].astype(F32)).astype(BF16)
    grads[...] = low
    total[...] += dot(low, weight[...], 1, 1)

    @pl.when(step == pl.num_programs(0) - 1)
    def _():
        branch[...] = total[...].astype(BF16)


def pre_back(scaled, active, slope, own, other, own_back, other_back, weight, full, after=()):
    span, units = active.shape
    model = weight.shape[0]
    tile = 512
    sums = (2, span)
    across = (span, tile)
    tiled = lambda n: (0, n)
    return call(
        partial(pre_back_kernel, full=full),
        "pre_back",
        (units // tile,),
        [
            (scaled, across, tiled),
            (active, across, tiled),
            (slope, across, tiled),
            (own, sums, None),
            (other, sums, None),
            (own_back, sums, None),
            (other_back, sums, None),
            (weight, (model, tile), tiled),
        ],
        [((span, units), BF16, across, tiled), ((span, model), BF16, (span, model), None)],
        [pltpu.VMEM((span, model), F32), pltpu.VMEM((4, span, 128), F32)],
        4.6e-9 * span * model * units,
        after,
    )


def middle_kernel(
    grads, own, other, hidden, gain, weight, mixed, own_sums, other_sums, gain_attn,
    grad_hidden, low, scaled, sums, gain_grad, gain_attn_grad, *, full
):
    step = pl.program_id(0)

    @pl.when(step == 0)
    def _():
        gain_grad[...] = jnp.zeros_like(gain_grad)
        gain_attn_grad[...] = jnp.zeros_like(gain_attn_grad)

    normal, std = row_norm(hidden[...])
    grad = own[...].astype(F32) + other[...].astype(F32)
    gain_grad[...] += jnp.sum(grad * normal, axis=0, keepdims=True)
    part = grad * gain[...]
    back = std * (
        part
        - jnp.mean(part, axis=-1, keepdims=True)
        - normal * jnp.mean(part * normal, axis=-1, keepdims=True)
    )
    total = grads[...].astype(F32) + back
    grad_hidden[...] = total
    rows = total.astype(BF16)
    low[...] = rows
    inner = dot(rows, weight[...], 1, 0)
    mean, deviation = moments(own_sums[...], other_sums[...], full)
    normal = (mixed[...].astype(F32) - as_column(mean)) * as_column(deviation)
    gain_attn_grad[...] += jnp.sum(inner * normal, axis=0, keepdims=True)
    inner = inner * gain_attn[...]
    scaled[...] = inner
    sums[...] = jnp.concatenate([as_row(inner), as_row(inner * normal)], axis=0)


def middle(
    grads, own, other, hidden, gain, near_full, mixed, own_sums, other_sums, gain_attn, full, after=()
):
    span, model = grads.shape
    width = mixed.shape[1]
    place = near_full.shape[1] // width - 1
    rows = min(256, span)
    by_row = lambda n: (n, 0)
    by_column = lambda n: (0, n)
    return call(
        partial(middle_kernel, full=full),
        "middle",
        (span // rows,),
        [
            (grads, (rows, model), by_row),
            (own, (rows, model), by_row),
            (other, (rows, model), by_row),
            (hidden, (rows, model), by_row),
            (gain, (1, model), None),
            (near_full, (model, width), lambda n: (0, place)),
            (mixed, (rows, width), by_row),
            (own_sums, (2, rows), by_column),
            (other_sums, (2, rows), by_column),
            (gain_attn, (1, width), None),
        ],
        [
            ((span, model), F32, (rows, model), by_row),
            ((span, model), BF16, (rows, model), by_row),
            ((span, width), F32, (rows, width), by_row),
            ((2, span), F32, (2, rows), by_column),
            ((1, model), F32, (1, model), None),
            ((1, width), F32, (1, width), None),
        ],
        [],
        1.2e-8 * span * width * model,
        after,
    )


def share_out_kernel(place, scaled, mixed, own, other, own_back, other_back, *outs, full):
    mean, std = moments(own[...], other[...], full)
    back = (own_back[...] + other_back[...]) / full
    mean, std, first, second = [as_column(row) for row in (mean, std, back[0:1], back[1:2])]
    share = outs[0].shape[1]
    for offset, out in enumerate(outs):
        at = pl.multiple_of(jnp.bitwise_xor(place[0], offset) * share, share)
        normal = (mixed[:, pl.ds(at, share)].astype(F32) - mean) * std
        out[...] = (std * (scaled[:, pl.ds(at, share)] - first - normal * second)).astype(BF16)


def share_out(place, scaled, mixed, own, other, own_back, other_back, full, groups, after=()):
    span, width = scaled.shape
    share = width // groups
    if share % 128:
        mean, std = moments(own, other, full)
        back = (own_back + other_back) / full
        mean, std, first, second = [row.reshape(-1, 1) for row in (mean, std, back[0], back[1])]
        normal = (mixed.astype(F32) - mean) * std
        grads = (std * (scaled - first - normal * second)).astype(BF16)
        return [
            lax.dynamic_slice_in_dim(grads, jnp.bitwise_xor(place[0], n) * share, share, 1)
            for n in range(groups)
        ]
    sums = (2, span)
    return call(
        partial(share_out_kernel, full=full),
        "share_out",
        (1,),
        [
            (scaled, (span, width), None),
            (mixed, (span, width), None),
            (own, sums, None),
            (other, sums, None),
            (own_back, sums, None),
            (other_back, sums, None),
        ],
        [((span, share), BF16, (span, share), None)] * groups,
        [],
        7.6e-6 * span * width,
        after,
        place,
    )


def first_back_kernel(place, *refs, groups):
    pieces, (weight, tokens, whole, branch, gain_grad, total) = refs[:groups], refs[groups:]
    step = pl.program_id(0)
    for offset, piece in enumerate(pieces):

        @pl.when(step == offset)
        def _(piece=piece, offset=offset):
            whole[...] = piece[...]
            made = dot(piece[0], weight[0], 1, 1)
            for j in (1, 2):
                made += dot(piece[j], weight[j], 1, 1)
            if offset:
                total[...] += made
            else:
                total[...] = made

    @pl.when(step == groups - 1)
    def _():
        normal, _ = row_norm(tokens[...].astype(F32))
        grad = total[...]
        gain_grad[...] = jnp.sum(grad * normal, axis=0, keepdims=True)
        branch[...] = grad.astype(BF16)


def first_back(place, pieces, qkv_full, tokens, after=()):
    groups = len(pieces)
    _, span, share = pieces[0].shape
    model, local = qkv_full.shape[1:]
    if share % 128:
        stacked = jnp.stack(pieces)
        whole = jnp.concatenate(
            [
                lax.dynamic_index_in_dim(stacked, jnp.bitwise_xor(place[0], n), 0, False)
                for n in range(groups)
            ],
            axis=2,
        )
        grad = jnp.einsum("jte,jde->td", whole, qkv_full, preferred_element_type=F32)
        normal, _ = row_norm(tokens.astype(F32))
        return whole, grad.astype(BF16), jnp.sum(grad * normal, axis=0, keepdims=True)
    across = lambda o, p: (0, 0, jnp.bitwise_xor(o, p[0]))
    return call(
        partial(first_back_kernel, groups=groups),
        "first_back",
        (groups,),
        [(piece, (3, span, share), None) for piece in pieces]
        + [(qkv_full, (3, model, share), across), (tokens, (span, model), None)],
        [
            ((3, span, local), BF16, (3, span, share), across),
            ((span, model), BF16, (span, model), None),
            ((1, model), F32, (1, model), None),
        ],
        [pltpu.VMEM((span, model), F32)],
        1.34e-8 * span * model * local,
        after,
        place,
    )


def exchange(array, axis, size, offset):
    return lax.ppermute(array, axis, [(n, n ^ offset) for n in range(size)])


def add_kernel(*refs):
    total = refs[0][...].astype(F32)
    for ref in refs[1:-1]:
        total += ref[...].astype(F32)
    refs[-1][...] = total.astype(BF16)


def add(arrays, rows, after=()):
    width = arrays[0][0].shape[1]
    tile = 128

    def from_row(first):
        return lambda n: (n + first // tile, 0)

    return call(
        add_kernel,
        "add",
        (rows // tile,),
        [(array, (tile, width), from_row(first)) for array, first in arrays],
        [((rows, width), BF16, (tile, width), lambda n: (n, 0))],
        [],
        1.5e-6 * rows * width,
        after,
    )[0]


class ScatterSum:
    def __init__(self, parts, groups, z_first=False):
        away, self.kept = parts
        self.groups, self.z_first = groups, z_first
        self.got = exchange(away, "seq", groups, 1)

    def mates(self, after=()):
        rows = self.kept.shape[0]
        pair = [(self.kept, 0), (self.got, 0)]
        if self.z_first:
            near = add(pair, rows, after)
            self.rows = lax.psum_scatter(near, "dp", scatter_dimension=0, tiled=True)
        else:
            near = add(pair, rows // 2, after)
            self.far = exchange(near, "seq", self.groups, 2)
        return near

    def chips(self, after=()):
        if self.z_first:
            half = self.rows.shape[0] // 2
            far = exchange(self.rows[:half], "seq", self.groups, 2)
            self.out = self.rows[half:].astype(F32) + far.astype(F32)
            return self.out
        half = self.kept.shape[0] // 2
        own = add([(self.kept, half), (self.got, half), (self.far, 0)], half, after)
        self.out = lax.psum_scatter(own, "dp", scatter_dimension=0, tiled=True).astype(F32)
        return own


def mp_sum(low, units):
    if units != 2:
        return lax.psum(low, "mp"), jnp.zeros_like(low)
    return low, exchange(low, "mp", 2, 1)


def mp_rows(sums, units):
    if units != 2:
        return lax.psum(sums, "mp"), jnp.zeros_like(sums)
    return sums, exchange(sums, "mp", 2, 1)


def data_sum(array, devices, groups):
    for axis, size in (("seq", groups), ("dp", devices)):
        offset = 1
        while offset < size:
            array = array + exchange(array, axis, size, offset)
            offset *= 2
    return array


def pass_round(pieces, groups):
    return [pieces[0]] + [exchange(pieces[n], "seq", groups, n) for n in range(1, groups)]


def xpos_tables(count, lanes):
    positions = jnp.arange(count, dtype=F32)
    pair_index = jnp.arange(HALF, dtype=F32)
    frequency = 1.0 / 10000.0 ** (2.0 * pair_index / HEAD_DIM)
    angles = positions[:, None] * frequency[None, :]
    base_ratio = (2.0 * pair_index + 0.4 * HEAD_DIM) / (1.4 * HEAD_DIM)
    growth = base_ratio[None, :] ** ((positions[:, None] - count // 2) / XPOS_BASE)
    cosine, sine = jnp.cos(angles), jnp.sin(angles)
    tables = []
    for factor in (growth, 1.0 / growth):
        tables.append(jnp.tile(cosine * factor, (1, lanes // HALF)))
        tables.append(
            jnp.tile(jnp.concatenate([-sine * factor, sine * factor], axis=1), (1, lanes // HEAD_DIM))
        )
    return tables


def body(
    devices,
    groups,
    units,
    tokens,
    lengths,
    qkv_weight,
    out_weight,
    in_weight,
    down_weight,
    gain_in,
    gain_attn,
    gain_mid,
    gain_ffn,
    out_grad,
):
    sequences, span, model = tokens.shape
    each = range(sequences)
    data = ("dp", "seq")
    shards = devices * groups
    place = lax.axis_index("seq").astype(jnp.int32)
    local_width = qkv_weight.shape[2]
    heads_here = local_width // HEAD_DIM
    ffn_width = in_weight.shape[1]
    share = local_width // groups

    number = lax.axis_index("dp") * groups + place
    sizes = [gain_in.size, gain_mid.size, gain_attn.size, gain_ffn.size]
    cuts = [sum(sizes[:n]) for n in range(5)]
    flat = jnp.concatenate(
        [gain_in, gain_mid, gain_attn.reshape(-1), gain_ffn.reshape(-1)]
    ).reshape(1, -1)
    row = lax.broadcasted_iota(jnp.int32, (shards, 1), 0)
    all_gains = data_sum(jnp.where(row == number, flat, 0).astype(F32), devices, groups)
    pieces = [all_gains[:, cuts[n] : cuts[n + 1]] for n in range(4)]
    gain_one, gain_three = pieces[0].reshape(1, -1), pieces[1].reshape(1, -1)
    gain_two = pieces[2].reshape(shards, heads_here, -1).transpose(1, 0, 2).reshape(1, -1)
    gain_four = (
        pieces[3].reshape(shards, ffn_width // HEAD_DIM, -1).transpose(1, 0, 2).reshape(1, -1)
    )

    qkv_full = lax.all_gather(qkv_weight, data, axis=1, tiled=True)
    near_full = lax.all_gather(
        jnp.concatenate([in_weight, out_weight.T], axis=1), data, axis=0, tiled=True
    )
    down_full = lax.all_gather(down_weight, data, axis=1, tiled=True)

    count = span * groups
    tables = xpos_tables(count, min(128, share))
    tables_here = [lax.dynamic_slice_in_dim(t, place * span, span, 0) for t in tables]
    spot = place.reshape(1)
    metas = [jnp.stack([lengths[s], place]) for s in each]
    full_units = ffn_width * units

    first_low = []
    for s in each:
        normal, _ = row_norm(tokens[s].astype(F32))
        first_low.append((normal * gain_one).astype(BF16))
    messages, mixed, logs, attended, att_sums, inner, branch = [], [], [], [], [], [], []
    last = ()
    for s in each:
        made = project(spot, first_low[s], qkv_full, tables_here, groups, last)
        messages.append(pass_round(made, groups))
        last = [made[0]]
    for s in each:
        outs, log = attend(metas[s], messages[s], last)
        mixed.append(outs)
        logs.append(log)
        last = [log]
    for s in each:
        whole, sums = collect(spot, pass_round(mixed[s], groups), last)
        attended.append(whole)
        att_sums.append(mp_rows(sums, units))
        low, terms = out_branch(whole, *att_sums[s], gain_two, near_full, model)
        inner.append(low)
        branch.append(mp_sum(terms, units))
        last = [terms]

    hidden, third_low, active, slope, act_sums = [], [], [], [], []
    for s in each:
        made = widen(tokens[s], *branch[s], gain_three, near_full, ffn_width, last)
        hidden.append(made[0])
        third_low.append(made[1])
        active.append(made[2])
        slope.append(made[3])
        act_sums.append(mp_rows(made[4], units))
        last = [made[4]]

    grad_low = [out_grad[s] for s in each]
    norm = ([a for a, _ in act_sums], [b for _, b in act_sums], gain_four, full_units)
    down_parts = weight_grad(spot, grad_low, active, devices, groups, norm, False, last)
    down_sum = ScatterSum(down_parts, groups)
    last = [down_parts[0]]
    pre_low, third_terms, scaled, back_sums = [], [], [], []
    gain_four_grad = 0.0
    for s in each:
        part, sums, gain_part = wide_back(
            grad_low[s], down_full, active[s], *act_sums[s], gain_four, full_units, last
        )
        scaled.append(part)
        gain_four_grad += gain_part
        back_sums.append(mp_rows(sums, units))
        last = [sums]
    last = [down_sum.mates(last)] + [other for _, other in back_sums]
    for s in each:
        low, terms = pre_back(
            scaled[s], active[s], slope[s], *act_sums[s], *back_sums[s], near_full, full_units,
            last,
        )
        pre_low.append(low)
        third_terms.append(mp_sum(terms, units))
        last = [terms]

    def finish(s, after):
        terms = narrow(active[s], *act_sums[s], gain_four, down_full, full_units, after)
        return mp_sum(terms, units)

    def result(s, after):
        own, other = wide_terms[s]
        return add([(own, 0), (other, 0), (hidden[s], 0)], span, after)

    gain_three_grad, gain_two_grad = 0.0, 0.0
    grad_hidden, hidden_low, grads, returned = [], [], [], []
    wide_terms = [finish(0, last)]
    last = [wide_terms[0][0]]
    for s in each:
        made = middle(
            grad_low[s], *third_terms[s], hidden[s], gain_three, near_full, attended[s],
            *att_sums[s], gain_two, model, last
        )
        grad_hidden.append(made[0])
        hidden_low.append(made[1])
        gain_three_grad += made[4]
        gain_two_grad += made[5]
        if s == 0:
            in_parts = weight_grad(
                spot, third_low, pre_low, devices, groups, None, Z_FIRST, [made[3]]
            )
            in_sum = ScatterSum(in_parts, groups, Z_FIRST)
            last = [down_sum.chips([in_parts[0], third_terms[1][1]])]
        else:
            wide_terms.append(finish(s, [made[3]]))
            last = [in_sum.mates([wide_terms[s][0]])]
        parts = share_out(
            spot, made[2], attended[s], *att_sums[s], *mp_rows(made[3], units), model, groups,
            last,
        )
        last = [parts[0]]
        grads.append(pass_round(parts, groups))
    for s in each:
        made = attend_back(
            metas[s], messages[s], grads[s], mixed[s], logs[s], tables, last,
            BACK_WEIGHT if s == 0 else 1,
        )
        returned.append(pass_round(made, groups))
        last = [made[0]]
        if s == 0:
            out_parts = weight_grad(spot, hidden_low, inner, devices, groups, None, False, last)
            out_sum = ScatterSum(out_parts, groups)
            last = [out_parts[0], down_sum.out]

    early = jnp.concatenate(
        [
            gain_three_grad.reshape(shards, -1),
            gain_two_grad.reshape(heads_here, shards, -1).transpose(1, 0, 2).reshape(shards, -1),
            gain_four_grad.reshape(ffn_width // HEAD_DIM, shards, -1)
            .transpose(1, 0, 2)
            .reshape(shards, -1),
        ],
        axis=1,
    )
    early = lax.dynamic_index_in_dim(data_sum(early, devices, groups), number, 0, False)
    cuts = [cut - cuts[1] for cut in cuts]
    three, two, four = [early[cuts[n] : cuts[n + 1]] for n in (1, 2, 3)]

    gain_one_grad = 0.0
    stacked, first_terms = [], []
    results = [result(0, last)]
    last = [out_sum.mates([results[0]])]
    for s in each:
        whole, terms, gain_part = first_back(spot, returned[s], qkv_full, tokens[s], last)
        stacked.append(whole)
        gain_one_grad += gain_part
        first_terms.append(mp_sum(terms, units))
        last = [terms]
    results.append(result(1, last))
    last = [out_sum.chips([results[1]])]
    qkv_parts = weight_grad(spot, first_low, stacked, devices, groups, None, False, last)
    qkv_sum = ScatterSum(qkv_parts, groups)
    grad_inputs = []
    for s in each:
        normal, std = row_norm(tokens[s].astype(F32))
        own, other = first_terms[s]
        part = (own.astype(F32) + other.astype(F32)) * gain_one
        grad_first = std * (
            part
            - jnp.mean(part, axis=-1, keepdims=True)
            - normal * jnp.mean(part * normal, axis=-1, keepdims=True)
        )
        grad_inputs.append((grad_hidden[s] + grad_first).astype(BF16))
    qkv_sum.mates([in_sum.chips()])
    qkv_sum.chips([grad_inputs[0]])
    grad_qkv_w = qkv_sum.out.reshape(-1, 3, local_width).transpose(1, 0, 2)
    own, other = mp_rows(gain_one_grad.reshape(shards, -1), units)
    one = lax.dynamic_index_in_dim(data_sum(own + other, devices, groups), number, 0, False)
    return (
        jnp.stack(results),
        jnp.stack(grad_inputs),
        grad_qkv_w,
        out_sum.out.T,
        in_sum.out,
        down_sum.out.T,
        one,
        two.reshape(gain_attn.shape),
        three,
        four.reshape(gain_ffn.shape),
    )


def solution(mesh):
    sizes = mesh.shape
    data = ("dp", "seq")
    in_specs = (
        P("dp", "seq", None),
        P("dp"),
        P(None, data, "mp"),
        P("mp", data),
        P(data, "mp"),
        P("mp", data),
        P(data),
        P("mp", data),
        P(data),
        P("mp", data),
        P("dp", "seq", None),
    )
    out_specs = (
        P("dp", "seq", None),
        P("dp", "seq", None),
        P(None, data, "mp"),
        P("mp", data),
        P(data, "mp"),
        P("mp", data),
        P(data),
        P("mp", data),
        P(data),
        P("mp", data),
    )
    run = partial(body, sizes["dp"], sizes["seq"], sizes["mp"])
    return jax.shard_map(run, mesh=mesh, in_specs=in_specs, out_specs=out_specs, check_vma=False)
```

```python
from functools import partial

import jax
import jax.numpy as jnp
from jax import lax
from jax.experimental import pallas as pl
from jax.experimental.pallas import tpu as pltpu
from jax.sharding import PartitionSpec as P

HEAD_DIM = 64
HALF = HEAD_DIM // 2
XPOS_BASE = 512
EPSILON = 1e-05
NEGATIVE = -1e30
LOG2_E = 1.4426950408889634
SCORE_SCALE = 0.125
VMEM = 56 * 2**20
Z_FIRST = True
BF16 = jnp.bfloat16
KERNEL_RATE = 0.25e9
BACK_WEIGHT = 25


def lasting(us):
    return pl.CostEstimate(flops=int(us * KERNEL_RATE), bytes_accessed=0, transcendentals=0)


F32 = jnp.float32


def params(limit=VMEM):
    return pltpu.CompilerParams(vmem_limit_bytes=limit)


def dot(left, right, left_dim, right_dim):
    return lax.dot_general(
        left, right, (((left_dim,), (right_dim,)), ((), ())), preferred_element_type=F32
    )


def swap_halves(block):
    width = block.shape[1]
    if width % 128:
        pieces = []
        for start in range(0, width, HEAD_DIM):
            pieces += [block[:, start + HALF : start + HEAD_DIM], block[:, start : start + HALF]]
        return jnp.concatenate(pieces, axis=1)
    lane = lax.broadcasted_iota(jnp.int32, (block.shape[0], 128), 1) % HEAD_DIM
    pieces = []
    for start in range(0, width, 128):
        part = block[:, start : start + 128]
        pieces.append(
            jnp.where(lane < HALF, pltpu.roll(part, 128 - HALF, 1), pltpu.roll(part, HALF, 1))
        )
    return pieces[0] if len(pieces) == 1 else jnp.concatenate(pieces, axis=1)


def turned(block, cosine, sine, sign):
    lanes = cosine.shape[1]
    pieces = []
    for start in range(0, block.shape[1], lanes):
        part = block[:, start : start + lanes]
        pieces.append(part * cosine + sign * (swap_halves(part) * sine))
    return pieces[0] if len(pieces) == 1 else jnp.concatenate(pieces, axis=1)


def project_kernel(place, *refs, groups, share):
    blocks, refs = refs[:groups], refs[groups:]
    gain, weight, cos_q, sin_q, cos_k, sin_k, low, made, held = refs
    for offset, block in enumerate(blocks):

        @pl.when(pl.program_id(0) == offset)
        def _(block=block):
            held[...] = block[...]

    normal, _ = row_norm(held[...].astype(F32))
    rows = (normal * gain[...]).astype(BF16)
    low[...] = rows
    out = dot(rows, weight[...], 1, 0)
    queries = turned(out[:, :share], cos_q[...], sin_q[...], 1)
    keys = turned(out[:, share : 2 * share], cos_k[...], sin_k[...], 1)
    made[...] = jnp.concatenate([queries, keys, out[:, 2 * share :]], axis=1).astype(BF16)


def project(place, blocks, gain, weight, tables, after=()):
    groups = len(blocks)
    span, model = blocks[0].shape
    width = weight.shape[1]
    lanes = tables[0].shape[1]

    def here(n, p):
        return (jnp.bitwise_xor(n, p[0]), 0)

    return call(
        partial(project_kernel, groups=groups, share=width // 3),
        "project",
        (groups,),
        [(block, (span, model), None) for block in blocks]
        + [(gain, (1, model), None), (weight, (model, width), None)]
        + [(table, (span, lanes), here) for table in tables],
        [
            ((groups * span, model), BF16, (span, model), here),
            ((groups * span, width), BF16, (span, width), here),
        ],
        [pltpu.VMEM((span, model), BF16)],
        5e-9 * groups * span * model * width,
        after,
        place,
    )


def attend_kernel(meta, projected, *refs, groups, heads, block):
    outs, log_ref, vt_all, o_all = refs[:groups], refs[groups], refs[groups + 1], refs[groups + 2]
    step = pl.program_id(0)
    length, place = meta[0], meta[1]
    share = heads * HEAD_DIM
    span = outs[0].shape[0]

    def lanes(part, h):
        return slice(part * share + h * HEAD_DIM, part * share + (h + 1) * HEAD_DIM)

    @pl.when(step == 0)
    def _():
        for h in range(heads):
            vt_all[h] = projected[:, lanes(2, h)].T

    start = pl.multiple_of(step * block, block)
    queries = [projected[pl.ds(start, block), lanes(0, h)] for h in range(heads)]
    scale = SCORE_SCALE * LOG2_E

    def keys_block(index, carry, masked):
        at = pl.multiple_of(index * block, block)
        if masked:
            key_pos = at + lax.broadcasted_iota(jnp.int32, (block, block), 0)
            query_pos = start + lax.broadcasted_iota(jnp.int32, (block, block), 1)
            allowed = (key_pos <= query_pos) & (key_pos < length)
        new = []
        for h in range(heads):
            top, total, mixed = carry[h]
            scores = dot(projected[pl.ds(at, block), lanes(1, h)], queries[h], 1, 1)
            if masked:
                scores = jnp.where(allowed, scores, NEGATIVE)
            higher = jnp.maximum(top, jnp.max(scores, axis=0, keepdims=True))
            fade = jnp.exp2((top - higher) * scale)
            weights = jnp.exp2((scores - higher) * scale)
            total = total * fade + jnp.sum(weights, axis=0, keepdims=True)
            added = dot(vt_all[h, :, pl.ds(at, block)], weights.astype(BF16), 1, 0)
            new.append((higher, total, mixed * fade + added))
        return tuple(new)

    carry = tuple(
        (
            jnp.full((1, block), NEGATIVE, F32),
            jnp.zeros((1, block), F32),
            jnp.zeros((HEAD_DIM, block), F32),
        )
        for _ in range(heads)
    )
    whole = jnp.minimum(step, length // block)
    end = jnp.minimum(step + 1, (length + block - 1) // block)
    carry = lax.fori_loop(0, whole, lambda n, c: keys_block(n, c, False), carry)
    carry = lax.fori_loop(whole, end, lambda n, c: keys_block(n, c, True), carry)
    pieces = []
    for h in range(heads):
        top, total, mixed = carry[h]
        pieces.append((mixed / total).T)
        log_ref[h : h + 1, :] = top * scale + jnp.log2(total)
    o_all[pl.ds(start, block), :] = jnp.concatenate(pieces, axis=1).astype(BF16)

    @pl.when(step == pl.num_programs(0) - 1)
    def _():
        for offset, out in enumerate(outs):
            at = pl.multiple_of(jnp.bitwise_xor(place, offset) * span, span)
            out[...] = o_all[pl.ds(at, span), :]


def attend(meta, projected, groups, after=()):
    count, width = projected.shape
    share = width // 3
    span = count // groups
    heads = share // HEAD_DIM
    block = min(512, span)
    results = call(
        partial(attend_kernel, groups=groups, heads=heads, block=block),
        "attend",
        (count // block,),
        [(projected, (count, width), None)],
        [((span, share), BF16, (span, share), None)] * groups
        + [((heads, count), F32, (heads, block), lambda n, m: (0, n))],
        [pltpu.VMEM((heads, HEAD_DIM, count), BF16), pltpu.VMEM((count, share), BF16)],
        2.9e-8 * count * count * share,
        after,
        meta,
    )
    return results[:groups], results[groups]


def attend_back_kernel(meta, projected, *refs, groups, heads, block):
    grads, mixed = refs[:groups], refs[groups : 2 * groups]
    log_ref, cos_q, sin_q, cos_k, sin_k, out = refs[2 * groups : 2 * groups + 6]
    g_all, kt_all, dot_all, dqt_all, dk_sum, dv_sum = refs[2 * groups + 6 :]
    length, place = meta[0], meta[1]
    span = grads[0].shape[0]
    count = groups * span
    share = heads * HEAD_DIM
    scale = SCORE_SCALE * LOG2_E

    def lanes(part, h):
        return slice(part * share + h * HEAD_DIM, part * share + (h + 1) * HEAD_DIM)

    for h in range(heads):
        kt_all[h] = projected[:, lanes(1, h)].T
    for offset in range(groups):
        at = pl.multiple_of(jnp.bitwise_xor(place, offset) * span, span)
        g_all[pl.ds(at, span), :] = grads[offset][...]
        both = grads[offset][...].astype(F32) * mixed[offset][...].astype(F32)
        for h in range(heads):
            dot_all[h : h + 1, pl.ds(at, span)] = jnp.sum(
                both[:, lanes(0, h)].T, axis=0, keepdims=True
            )
    dqt_all[...] = jnp.zeros_like(dqt_all)
    query_blocks = count // block

    def keys_block(index, _):
        key_at = pl.multiple_of(index * block, block)
        keys = [projected[pl.ds(key_at, block), lanes(1, h)] for h in range(heads)]
        values = [projected[pl.ds(key_at, block), lanes(2, h)] for h in range(heads)]
        dk_sum[...] = jnp.zeros_like(dk_sum)
        dv_sum[...] = jnp.zeros_like(dv_sum)

        def query_block(index, _, masked):
            at = pl.multiple_of(index * block, block)
            if masked:
                key_pos = key_at + lax.broadcasted_iota(jnp.int32, (block, block), 0)
                query_pos = at + lax.broadcasted_iota(jnp.int32, (block, block), 1)
                allowed = (key_pos <= query_pos) & (key_pos < length)
            for h in range(heads):
                query = projected[pl.ds(at, block), lanes(0, h)]
                grad = g_all[pl.ds(at, block), lanes(0, h)]
                scores = dot(keys[h], query, 1, 1)
                weights = jnp.exp2(scores * scale - log_ref[h : h + 1, pl.ds(at, block)])
                if masked:
                    weights = jnp.where(allowed, weights, 0.0)
                grad_weights = dot(values[h], grad, 1, 1)
                grad_scores = weights * (grad_weights - dot_all[h : h + 1, pl.ds(at, block)])
                grad_scores = grad_scores.astype(BF16)
                dv_sum[h] += dot(weights.astype(BF16), grad, 1, 0)
                dk_sum[h] += dot(grad_scores, query, 1, 0)
                dqt_all[h, :, pl.ds(at, block)] += dot(
                    kt_all[h, :, pl.ds(key_at, block)], grad_scores, 1, 0
                )
            return 0

        crosses = key_at + block > length
        whole = jnp.where(crosses, query_blocks, index + 1)
        lax.fori_loop(index, whole, partial(query_block, masked=True), 0)
        lax.fori_loop(whole, query_blocks, partial(query_block, masked=False), 0)
        dk = jnp.concatenate([dk_sum[h] for h in range(heads)], axis=1) * SCORE_SCALE
        dv = jnp.concatenate([dv_sum[h] for h in range(heads)], axis=1)
        turn = (cos_k[pl.ds(key_at, block), :], sin_k[pl.ds(key_at, block), :])
        out[pl.ds(key_at, block), share : 2 * share] = turned(dk, *turn, -1).astype(BF16)
        out[pl.ds(key_at, block), 2 * share :] = dv.astype(BF16)
        return 0

    used = (length + block - 1) // block
    lax.fori_loop(0, used, keys_block, 0)

    def no_keys(index, _):
        at = pl.multiple_of(index * block, block)
        out[pl.ds(at, block), share:] = jnp.zeros((block, 2 * share), BF16)
        return 0

    lax.fori_loop(used, query_blocks, no_keys, 0)
    for index in range(query_blocks):
        at = slice(index * block, (index + 1) * block)
        dq = jnp.concatenate([dqt_all[h, :, at].T for h in range(heads)], axis=1) * SCORE_SCALE
        out[at, :share] = turned(dq, cos_q[at, :], sin_q[at, :], -1).astype(BF16)


def attend_back(meta, projected, grads, mixed, logs, tables, after=(), weight=1):
    groups = len(grads)
    count, width = projected.shape
    share = width // 3
    span = count // groups
    heads = share // HEAD_DIM
    block = min(512, span)
    return call(
        partial(attend_back_kernel, groups=groups, heads=heads, block=block),
        "attend_back",
        (1,),
        [(projected, (count, width), None)]
        + [(piece, (span, share), None) for piece in (*grads, *mixed)]
        + [(logs, logs.shape, None)]
        + [(table, table.shape, None) for table in tables],
        [((count, width), BF16, (count, width), None)],
        [
            pltpu.VMEM((count, share), BF16),
            pltpu.VMEM((heads, HEAD_DIM, count), BF16),
            pltpu.VMEM((heads, count), F32),
            pltpu.VMEM((heads, HEAD_DIM, count), F32),
            pltpu.VMEM((heads, block, HEAD_DIM), F32),
            pltpu.VMEM((heads, block, HEAD_DIM), F32),
        ],
        4.2e-8 * count * count * share * weight,
        after,
        meta,
    )[0]


def heads_grad_kernel(*refs, sequences):
    grads, lows, out, turned_grads = (
        refs[:sequences],
        refs[sequences : 2 * sequences],
        refs[2 * sequences],
        refs[2 * sequences + 1],
    )
    count = grads[0].shape[0]

    @pl.when(pl.program_id(0) == 0)
    def _():
        for s in range(sequences):
            turned_grads[:, s * count : (s + 1) * count] = grads[s][...].T

    total = dot(turned_grads[:, :count], lows[0][...], 1, 0)
    for s in range(1, sequences):
        total += dot(turned_grads[:, s * count : (s + 1) * count], lows[s][...], 1, 0)
    out[...] = total.T.astype(BF16)


def heads_grad(lows, grads, after=()):
    sequences = len(lows)
    count, model = lows[0].shape
    width = grads[0].shape[1]
    tile = 512
    return call(
        partial(heads_grad_kernel, sequences=sequences),
        "heads_grad",
        (model // tile,),
        [(grad, (count, width), None) for grad in grads]
        + [(low, (count, tile), lambda n: (0, n)) for low in lows],
        [((model, width), BF16, (tile, width), lambda n: (n, 0))],
        [pltpu.VMEM((width, sequences * count), BF16)],
        3e-9 * sequences * count * model * width,
        after,
    )[0]


def normed_rows(block, column_mean, column_std, gain):
    return (block.astype(F32) - column_mean) * column_std * gain


def moments(own, other, width):
    total = own + other
    mean = total[0:1] / width
    return mean, lax.rsqrt(total[1:2] / width - mean * mean + EPSILON)


def as_column(row):
    return jnp.broadcast_to(row, (128, row.shape[1])).T[:, 0:1]


def as_row(block):
    width = block.shape[1]
    part = block[:, 0:128]
    for start in range(128, width, 128):
        part = part + block[:, start : start + 128]
    return jnp.sum(part.T, axis=0, keepdims=True)


def weight_grad_kernel(place, *refs, sequences, devices, groups, chunk, offsets, normed, extra):
    lefts, refs = refs[:sequences], refs[sequences:]
    rights, refs = refs[:sequences], refs[sequences:]
    if normed:
        own_sums, other_sums, gain = refs[:sequences], refs[sequences : 2 * sequences], refs[2 * sequences]
        refs = refs[2 * sequences + 1 :]
    away, kept, turned_left = refs[extra : extra + 3]
    columns_ref = refs[extra + 3] if normed else None
    span = lefts[0].shape[0]

    @pl.when(pl.program_id(0) == 0)
    def _():
        row = 0
        for device, offset in offsets:
            target = jnp.bitwise_xor(place[0], offset)
            at = pl.multiple_of((device * groups + target) * chunk, chunk)
            for s in range(sequences):
                turned_left[row : row + chunk, s * span : (s + 1) * span] = lefts[s][
                    :, pl.ds(at, chunk)
                ].T
            row += chunk
        if normed:
            for s in range(sequences):
                mean, std = moments(own_sums[s][...], other_sums[s][...], normed)
                columns_ref[2 * s] = jnp.broadcast_to(as_column(mean), (span, 128))
                columns_ref[2 * s + 1] = jnp.broadcast_to(as_column(std), (span, 128))

    values = []
    for s in range(sequences):
        block = rights[s][...]
        if normed:
            block = normed_rows(
                block, columns_ref[2 * s, :, 0:1], columns_ref[2 * s + 1, :, 0:1], gain[...]
            ).astype(BF16)
        values.append(block)
    block = turned_left.shape[0] // 4
    parts = [away.at[:block], away.at[block:], kept.at[:block], kept.at[block:]]
    for n, part in enumerate(parts):
        rows = slice(n * block, (n + 1) * block)
        total = dot(turned_left[rows, :span], values[0], 1, 0)
        for s in range(1, sequences):
            total += dot(turned_left[rows, s * span : (s + 1) * span], values[s], 1, 0)
        part[...] = total.astype(BF16)


def weight_grad(place, lefts, rights, devices, groups, norm=None, z_first=False, after=()):
    sequences = len(lefts)
    span, width = lefts[0].shape
    layers = rights[0].ndim == 3
    columns = rights[0].shape[0] * rights[0].shape[2] if layers else rights[0].shape[1]
    chunk = width // (devices * groups)
    tile = 512 if rights[0].shape[-1] % 512 == 0 else rights[0].shape[-1]
    half = width // 2
    if z_first:
        offsets = [(d, o) for core in (1, 0) for d in range(devices) for o in (2 + core, core)]
    else:
        offsets = [(d, o) for o in (3, 1, 2, 0) for d in range(devices)]
    if layers:
        tiles = rights[0].shape[2] // tile
        right_spec = pl.BlockSpec((None, span, tile), lambda n, p: (n // tiles, 0, n % tiles))
    else:
        right_spec = pl.BlockSpec((span, tile), lambda n, p: (0, n))
    in_specs = [pl.BlockSpec((span, width), lambda n, p: (0, 0))] * sequences
    in_specs += [right_spec] * sequences
    operands = [*lefts, *rights]
    scratch = [pltpu.VMEM((width, sequences * span), BF16)]
    full = 0
    if norm:
        own_sums, other_sums, gain, full = norm
        in_specs += [pl.BlockSpec((2, span), lambda n, p: (0, 0))] * (2 * sequences)
        in_specs += [pl.BlockSpec((1, tile), lambda n, p: (0, n))]
        operands += [*own_sums, *other_sums, gain]
        scratch += [pltpu.VMEM((2 * sequences, span, 128), F32)]
    in_specs += [pl.BlockSpec(memory_space=pl.ANY)] * len(after)
    return pl.pallas_call(
        partial(
            weight_grad_kernel,
            sequences=sequences,
            devices=devices,
            groups=groups,
            chunk=chunk,
            offsets=offsets,
            normed=full,
            extra=len(after),
        ),
        grid_spec=pltpu.PrefetchScalarGridSpec(
            num_scalar_prefetch=1,
            grid=(columns // tile,),
            in_specs=in_specs,
            out_specs=[pl.BlockSpec((half, tile), lambda n, p: (0, n))] * 2,
            scratch_shapes=scratch,
        ),
        out_shape=[jax.ShapeDtypeStruct((half, columns), BF16)] * 2,
        compiler_params=params(),
        cost_estimate=lasting(2.9e-9 * sequences * span * width * columns),
        name="weight_grad",
    )(place, *operands, *after)


def call(kernel, name, grid, ins, outs, scratch, us, after=(), scalars=None, into=None):
    if into is not None:
        after = [into, *after]
    extra = len(after)
    first = 0 if scalars is None else 1
    count = first + len(ins)

    def run(*refs):
        kernel(*refs[:count], *refs[count + extra :])

    def spec(block, index):
        if index is None:
            return pl.BlockSpec(block, lambda *_: (0,) * len(block))
        return pl.BlockSpec(block, index)

    return pl.pallas_call(
        run,
        grid_spec=pltpu.PrefetchScalarGridSpec(
            num_scalar_prefetch=first,
            grid=grid,
            in_specs=[spec(block, index) for _, block, index in ins]
            + [pl.BlockSpec(memory_space=pl.ANY)] * extra,
            out_specs=[spec(block, index) for _, _, block, index in outs],
            scratch_shapes=scratch,
        ),
        out_shape=[jax.ShapeDtypeStruct(shape, dtype) for shape, dtype, _, _ in outs],
        input_output_aliases={} if into is None else {count: 0},
        compiler_params=params(),
        cost_estimate=lasting(us),
        name=name,
    )(*(() if scalars is None else (scalars,)), *[array for array, _, _ in ins], *after)


def pack_kernel(columns, rows, out):
    width = columns.shape[1]
    out[:, :width] = columns[...]
    out[:, width:] = rows[...].T


def pack(columns, rows, after=()):
    height, width = columns.shape
    total = width + rows.shape[0]
    return call(
        pack_kernel,
        "pack",
        (1,),
        [(columns, columns.shape, None), (rows, rows.shape, None)],
        [((height, total), BF16, (height, total), None)],
        [],
        1,
        after,
    )[0]


def collect_kernel(place, *refs, groups):
    pieces, (whole, sums) = refs[:groups], refs[groups:]
    share = pieces[0].shape[1]
    total, squares = 0.0, 0.0
    for offset, piece in enumerate(pieces):
        at = pl.multiple_of(jnp.bitwise_xor(place[0], offset) * share, share)
        block = piece[...]
        whole[:, pl.ds(at, share)] = block
        wide = block.astype(F32)
        total += as_row(wide)
        squares += as_row(wide * wide)
    sums[...] = jnp.concatenate([total, squares], axis=0)


def collect(place, pieces, after=()):
    groups = len(pieces)
    span, share = pieces[0].shape
    if share % 128:
        stacked = jnp.stack(pieces)
        whole = jnp.concatenate(
            [
                lax.dynamic_index_in_dim(stacked, jnp.bitwise_xor(place[0], n), 0, False)
                for n in range(groups)
            ],
            axis=1,
        )
        wide = whole.astype(F32)
        return whole, jnp.stack([jnp.sum(wide, axis=1), jnp.sum(wide * wide, axis=1)])
    width = groups * share
    return call(
        partial(collect_kernel, groups=groups),
        "collect",
        (1,),
        [(piece, (span, share), None) for piece in pieces],
        [((span, width), BF16, (span, width), None), ((2, span), F32, (2, span), None)],
        [],
        5e-6 * span * width,
        after,
        place,
    )


def out_kernel(mixed, own, other, gain, weight, inner, branch, *, full):
    mean, std = moments(own[...], other[...], full)
    low = normed_rows(mixed[...], as_column(mean), as_column(std), gain[...]).astype(BF16)
    inner[...] = low
    branch[...] = dot(low, weight[...], 1, 1).astype(BF16)


def out_branch(mixed, own, other, gain, near_full, full, after=()):
    span, width = mixed.shape
    model = near_full.shape[0]
    place = near_full.shape[1] // width - 1
    rows = min(256, span)
    return call(
        partial(out_kernel, full=full),
        "out_branch",
        (span // rows,),
        [
            (mixed, (rows, width), lambda n: (n, 0)),
            (own, (2, rows), lambda n: (0, n)),
            (other, (2, rows), lambda n: (0, n)),
            (gain, (1, width), None),
            (near_full, (model, width), lambda n: (0, place)),
        ],
        [
            ((span, width), BF16, (rows, width), lambda n: (n, 0)),
            ((span, model), BF16, (rows, model), lambda n: (n, 0)),
        ],
        [],
        6e-9 * span * width * model,
        after,
    )


def row_norm(block):
    mean = jnp.mean(block, axis=-1, keepdims=True)
    centered = block - mean
    std = lax.rsqrt(jnp.mean(centered * centered, axis=-1, keepdims=True) + EPSILON)
    return centered * std, std


def widen_kernel(tokens, own, other, gain, weight, hidden, low, active, slope, sums, total, squares):
    step = pl.program_id(0)

    @pl.when(step == 0)
    def _():
        block = tokens[...].astype(F32) + (own[...].astype(F32) + other[...].astype(F32))
        hidden[...] = block
        normal, _ = row_norm(block)
        low[...] = (normal * gain[...]).astype(BF16)
        total[...] = jnp.zeros_like(total)
        squares[...] = jnp.zeros_like(squares)

    pre = dot(low[...], weight[...], 1, 0)
    below = 0.5 + 0.5 * lax.erf(pre * 0.7071067811865476)
    value = pre * below
    active[...] = value.astype(BF16)
    slope[...] = (below + pre * (0.3989422804014327 * jnp.exp2(pre * pre * (-0.5 * LOG2_E)))).astype(
        BF16
    )
    part, square = total[...], squares[...]
    for start in range(0, value.shape[1], 128):
        piece = value[:, start : start + 128]
        part += piece
        square += piece * piece
    total[...] = part
    squares[...] = square

    @pl.when(step == pl.num_programs(0) - 1)
    def _():
        sums[...] = jnp.concatenate([as_row(total[...]), as_row(squares[...])], axis=0)


def widen(tokens, own, other, gain, weight, units, after=()):
    span, model = tokens.shape
    tile = 512
    rows = (span, model)
    across = (span, tile)
    return call(
        widen_kernel,
        "widen",
        (units // tile,),
        [
            (tokens, rows, None),
            (own, rows, None),
            (other, rows, None),
            (gain, (1, model), None),
            (weight, (model, tile), lambda n: (0, n)),
        ],
        [
            (rows, F32, rows, None),
            (rows, BF16, rows, None),
            ((span, units), BF16, across, lambda n: (0, n)),
            ((span, units), BF16, across, lambda n: (0, n)),
            ((2, span), F32, (2, span), None),
        ],
        [pltpu.VMEM((span, 128), F32)] * 2,
        5.4e-9 * span * model * units,
        after,
    )


def narrow_kernel(active, own, other, gain, weight, branch, total, columns, *, full):
    step = pl.program_id(0)

    @pl.when(step == 0)
    def _():
        mean, std = moments(own[...], other[...], full)
        columns[0] = jnp.broadcast_to(as_column(mean), columns.shape[1:])
        columns[1] = jnp.broadcast_to(as_column(std), columns.shape[1:])
        total[...] = jnp.zeros_like(total)

    low = normed_rows(active[...], columns[0, :, 0:1], columns[1, :, 0:1], gain[...]).astype(BF16)
    total[...] += dot(low, weight[...], 1, 0)

    @pl.when(step == pl.num_programs(0) - 1)
    def _():
        branch[...] = total[...].astype(BF16)


def narrow(active, own, other, gain, weight, full, after=()):
    span, units = active.shape
    model = weight.shape[1]
    tile = 512
    sums = (2, span)
    return call(
        partial(narrow_kernel, full=full),
        "narrow",
        (units // tile,),
        [
            (active, (span, tile), lambda n: (0, n)),
            (own, sums, None),
            (other, sums, None),
            (gain, (1, tile), lambda n: (0, n)),
            (weight, (tile, model), lambda n: (n, 0)),
        ],
        [((span, model), BF16, (span, model), None)],
        [pltpu.VMEM((span, model), F32), pltpu.VMEM((2, span, 128), F32)],
        3.7e-9 * span * model * units,
        after,
    )[0]


def wide_back_kernel(
    grads, weight, active, own, other, gain, scaled, sums, gain_grad, columns, total, weighted, *, full
):
    step = pl.program_id(0)

    @pl.when(step == 0)
    def _():
        mean, std = moments(own[...], other[...], full)
        columns[0] = jnp.broadcast_to(as_column(mean), columns.shape[1:])
        columns[1] = jnp.broadcast_to(as_column(std), columns.shape[1:])
        total[...] = jnp.zeros_like(total)
        weighted[...] = jnp.zeros_like(weighted)

    grad = dot(grads[...], weight[...], 1, 1)
    normal = (active[...].astype(F32) - columns[0, :, 0:1]) * columns[1, :, 0:1]
    product = grad * normal
    gain_grad[...] = jnp.sum(product, axis=0, keepdims=True)
    scaled[...] = (grad * gain[...]).astype(BF16)
    product = product * gain[...]
    part, other_part = total[...], weighted[...]
    for start in range(0, grad.shape[1], 128):
        at = slice(start, start + 128)
        part += grad[:, at] * gain[:, at]
        other_part += product[:, at]
    total[...] = part
    weighted[...] = other_part

    @pl.when(step == pl.num_programs(0) - 1)
    def _():
        sums[...] = jnp.concatenate([as_row(total[...]), as_row(weighted[...])], axis=0)


def wide_back(grads, weight, active, own, other, gain, full, after=()):
    span, units = active.shape
    model = weight.shape[1]
    tile = 512
    sums = (2, span)
    across = (span, tile)
    return call(
        partial(wide_back_kernel, full=full),
        "wide_back",
        (units // tile,),
        [
            (grads, (span, model), None),
            (weight, (tile, model), lambda n: (n, 0)),
            (active, across, lambda n: (0, n)),
            (own, sums, None),
            (other, sums, None),
            (gain, (1, tile), lambda n: (0, n)),
        ],
        [
            ((span, units), BF16, across, lambda n: (0, n)),
            (sums, F32, sums, None),
            ((1, units), F32, (1, tile), lambda n: (0, n)),
        ],
        [pltpu.VMEM((2, span, 128), F32)] + [pltpu.VMEM((span, 128), F32)] * 2,
        4.2e-9 * span * model * units,
        after,
    )


def pre_back_kernel(
    scaled, active, slope, own, other, own_back, other_back, weight, grads, branch, total, columns, *, full
):
    step = pl.program_id(0)

    @pl.when(step == 0)
    def _():
        mean, std = moments(own[...], other[...], full)
        back = (own_back[...] + other_back[...]) / full
        for n, row in enumerate((mean, std, back[0:1], back[1:2])):
            columns[n] = jnp.broadcast_to(as_column(row), columns.shape[1:])
        total[...] = jnp.zeros_like(total)

    std = columns[1, :, 0:1]
    normal = (active[...].astype(F32) - columns[0, :, 0:1]) * std
    grad = std * (scaled[...].astype(F32) - columns[2, :, 0:1] - normal * columns[3, :, 0:1])
    low = (grad * slope[...].astype(F32)).astype(BF16)
    grads[...] = low
    total[...] += dot(low, weight[...], 1, 1)

    @pl.when(step == pl.num_programs(0) - 1)
    def _():
        branch[...] = total[...].astype(BF16)


def pre_back(scaled, active, slope, own, other, own_back, other_back, weight, full, after=()):
    span, units = active.shape
    model = weight.shape[0]
    tile = 512
    sums = (2, span)
    across = (span, tile)
    tiled = lambda n: (0, n)
    return call(
        partial(pre_back_kernel, full=full),
        "pre_back",
        (units // tile,),
        [
            (scaled, across, tiled),
            (active, across, tiled),
            (slope, across, tiled),
            (own, sums, None),
            (other, sums, None),
            (own_back, sums, None),
            (other_back, sums, None),
            (weight, (model, tile), tiled),
        ],
        [((span, units), BF16, across, tiled), ((span, model), BF16, (span, model), None)],
        [pltpu.VMEM((span, model), F32), pltpu.VMEM((4, span, 128), F32)],
        4.6e-9 * span * model * units,
        after,
    )


def middle_kernel(
    grads, own, other, hidden, gain, weight, mixed, own_sums, other_sums, gain_attn,
    grad_hidden, low, scaled, sums, gain_grad, gain_attn_grad, *, full
):
    step = pl.program_id(0)

    @pl.when(step == 0)
    def _():
        gain_grad[...] = jnp.zeros_like(gain_grad)
        gain_attn_grad[...] = jnp.zeros_like(gain_attn_grad)

    normal, std = row_norm(hidden[...])
    grad = own[...].astype(F32) + other[...].astype(F32)
    gain_grad[...] += jnp.sum(grad * normal, axis=0, keepdims=True)
    part = grad * gain[...]
    back = std * (
        part
        - jnp.mean(part, axis=-1, keepdims=True)
        - normal * jnp.mean(part * normal, axis=-1, keepdims=True)
    )
    total = grads[...].astype(F32) + back
    grad_hidden[...] = total
    rows = total.astype(BF16)
    low[...] = rows
    inner = dot(rows, weight[...], 1, 0)
    mean, deviation = moments(own_sums[...], other_sums[...], full)
    normal = (mixed[...].astype(F32) - as_column(mean)) * as_column(deviation)
    gain_attn_grad[...] += jnp.sum(inner * normal, axis=0, keepdims=True)
    inner = inner * gain_attn[...]
    scaled[...] = inner
    sums[...] = jnp.concatenate([as_row(inner), as_row(inner * normal)], axis=0)


def middle(
    grads, own, other, hidden, gain, near_full, mixed, own_sums, other_sums, gain_attn, full, after=()
):
    span, model = grads.shape
    width = mixed.shape[1]
    place = near_full.shape[1] // width - 1
    rows = min(256, span)
    by_row = lambda n: (n, 0)
    by_column = lambda n: (0, n)
    return call(
        partial(middle_kernel, full=full),
        "middle",
        (span // rows,),
        [
            (grads, (rows, model), by_row),
            (own, (rows, model), by_row),
            (other, (rows, model), by_row),
            (hidden, (rows, model), by_row),
            (gain, (1, model), None),
            (near_full, (model, width), lambda n: (0, place)),
            (mixed, (rows, width), by_row),
            (own_sums, (2, rows), by_column),
            (other_sums, (2, rows), by_column),
            (gain_attn, (1, width), None),
        ],
        [
            ((span, model), F32, (rows, model), by_row),
            ((span, model), BF16, (rows, model), by_row),
            ((span, width), F32, (rows, width), by_row),
            ((2, span), F32, (2, rows), by_column),
            ((1, model), F32, (1, model), None),
            ((1, width), F32, (1, width), None),
        ],
        [],
        1.2e-8 * span * width * model,
        after,
    )


def share_out_kernel(place, scaled, mixed, own, other, own_back, other_back, *outs, full):
    mean, std = moments(own[...], other[...], full)
    back = (own_back[...] + other_back[...]) / full
    mean, std, first, second = [as_column(row) for row in (mean, std, back[0:1], back[1:2])]
    share = outs[0].shape[1]
    for offset, out in enumerate(outs):
        at = pl.multiple_of(jnp.bitwise_xor(place[0], offset) * share, share)
        normal = (mixed[:, pl.ds(at, share)].astype(F32) - mean) * std
        out[...] = (std * (scaled[:, pl.ds(at, share)] - first - normal * second)).astype(BF16)


def share_out(place, scaled, mixed, own, other, own_back, other_back, full, groups, after=()):
    span, width = scaled.shape
    share = width // groups
    if share % 128:
        mean, std = moments(own, other, full)
        back = (own_back + other_back) / full
        mean, std, first, second = [row.reshape(-1, 1) for row in (mean, std, back[0], back[1])]
        normal = (mixed.astype(F32) - mean) * std
        grads = (std * (scaled - first - normal * second)).astype(BF16)
        return [
            lax.dynamic_slice_in_dim(grads, jnp.bitwise_xor(place[0], n) * share, share, 1)
            for n in range(groups)
        ]
    sums = (2, span)
    return call(
        partial(share_out_kernel, full=full),
        "share_out",
        (1,),
        [
            (scaled, (span, width), None),
            (mixed, (span, width), None),
            (own, sums, None),
            (other, sums, None),
            (own_back, sums, None),
            (other_back, sums, None),
        ],
        [((span, share), BF16, (span, share), None)] * groups,
        [],
        7.6e-6 * span * width,
        after,
        place,
    )


def first_back_kernel(order, grads, low, weight, gain, away, kept, gain_grad, total):
    step = pl.program_id(0)
    grad = dot(grads[...], weight[...], 1, 1)
    made = grad.astype(BF16)

    @pl.when(step < 2)
    def _():
        away[...] = made

    @pl.when(step >= 2)
    def _():
        kept[...] = made

    @pl.when(step == 0)
    def _():
        total[...] = jnp.zeros_like(total)

    total[...] += jnp.sum(grad * low[...].astype(F32), axis=0, keepdims=True)

    @pl.when(step == pl.num_programs(0) - 1)
    def _():
        gain_grad[...] = total[...] / gain[...]


def first_back(order, grads, low, weight, gain, groups, after=()):
    count, width = grads.shape
    model = weight.shape[0]
    span = count // groups
    rows = (span, model)
    return call(
        first_back_kernel,
        "first_back",
        (groups,),
        [
            (grads, (span, width), lambda n, p: (p[n], 0)),
            (low, rows, lambda n, p: (p[n], 0)),
            (weight, (model, width), None),
            (gain, (1, model), None),
        ],
        [
            ((2 * span, model), BF16, rows, lambda n, p: (jnp.minimum(n, 1), 0)),
            ((2 * span, model), BF16, rows, lambda n, p: (jnp.maximum(n - 2, 0), 0)),
            ((1, model), F32, (1, model), None),
        ],
        [pltpu.VMEM((1, model), F32)],
        4.5e-9 * count * model * width,
        after,
        order,
    )


def relay_kernel(array, out):
    out[...] = array[...]


def relay(array, after):
    rows = min(128, array.shape[0])
    block = (rows, array.shape[1])
    return call(
        relay_kernel,
        "relay",
        (array.shape[0] // rows,),
        [(array, block, lambda n: (n, 0))],
        [(array.shape, array.dtype, block, lambda n: (n, 0))],
        [],
        1,
        after,
    )[0]


def exchange(array, axis, size, offset):
    return lax.ppermute(array, axis, [(n, n ^ offset) for n in range(size)])


def add_kernel(*refs):
    total = refs[0][...].astype(F32)
    for ref in refs[1:-1]:
        total += ref[...].astype(F32)
    refs[-1][...] = total.astype(BF16)


def add(arrays, rows, after=()):
    width = arrays[0][0].shape[1]
    tile = 128

    def from_row(first):
        return lambda n: (n + first // tile, 0)

    return call(
        add_kernel,
        "add",
        (rows // tile,),
        [(array, (tile, width), from_row(first)) for array, first in arrays],
        [((rows, width), BF16, (tile, width), lambda n: (n, 0))],
        [],
        1.5e-6 * rows * width,
        after,
    )[0]


def result_kernel(own, other, hidden, out):
    out[...] = (hidden[...] + (own[...].astype(F32) + other[...].astype(F32))).astype(BF16)


def result_rows(number, count, own, other, hidden, into, after=()):
    span, model = hidden.shape
    tile = min(128, span)
    block = (tile, model)
    return call(
        result_kernel,
        "result",
        (span // tile,),
        [(array, block, lambda n: (n, 0)) for array in (own, other, hidden)],
        [((count, span, model), BF16, (None, *block), lambda n: (number, n, 0))],
        [],
        1.5e-6 * span * model,
        after,
        None,
        into,
    )[0]


def input_kernel(tokens, own, other, gain, grads, out):
    normal, std = row_norm(tokens[...].astype(F32))
    part = (own[...].astype(F32) + other[...].astype(F32)) * gain[...]
    first = std * (
        part
        - jnp.mean(part, axis=-1, keepdims=True)
        - normal * jnp.mean(part * normal, axis=-1, keepdims=True)
    )
    out[...] = (grads[...] + first).astype(BF16)


def input_rows(number, count, tokens, own, other, gain, grads, into, after=()):
    span, model = tokens.shape
    tile = min(128, span)
    block = (tile, model)
    by_row = lambda n: (n, 0)
    return call(
        input_kernel,
        "input_grad",
        (span // tile,),
        [
            (tokens, block, by_row),
            (own, block, by_row),
            (other, block, by_row),
            (gain, (1, model), None),
            (grads, block, by_row),
        ],
        [((count, span, model), BF16, (None, *block), lambda n: (number, n, 0))],
        [],
        2e-6 * span * model,
        after,
        None,
        into,
    )[0]


class ScatterSum:
    def __init__(self, parts, groups, z_first=False):
        away, self.kept = parts
        self.groups, self.z_first = groups, z_first
        self.got = exchange(away, "seq", groups, 1)

    def mates(self, after=()):
        rows = self.kept.shape[0]
        pair = [(self.kept, 0), (self.got, 0)]
        if self.z_first:
            near = add(pair, rows, after)
            self.rows = lax.psum_scatter(near, "dp", scatter_dimension=0, tiled=True)
        else:
            near = add(pair, rows // 2, after)
            self.far = exchange(near, "seq", self.groups, 2)
        return near

    def own(self, after=()):
        half = self.kept.shape[0] // 2
        return add([(self.kept, half), (self.got, half), (self.far, 0)], half, after)

    def chips(self, after=()):
        if self.z_first:
            half = self.rows.shape[0] // 2
            far = exchange(self.rows[:half], "seq", self.groups, 2)
            self.out = self.rows[half:].astype(F32) + far.astype(F32)
            return self.out
        own = self.own(after)
        self.out = lax.psum_scatter(own, "dp", scatter_dimension=0, tiled=True).astype(F32)
        return own


def mp_sum(low, units):
    if units != 2:
        return lax.psum(low, "mp"), jnp.zeros_like(low)
    return low, exchange(low, "mp", 2, 1)


def mp_rows(sums, units):
    if units != 2:
        return lax.psum(sums, "mp"), jnp.zeros_like(sums)
    return sums, exchange(sums, "mp", 2, 1)


def axis_sum(array, axis, size):
    offset = 1
    while offset < size:
        array = array + exchange(array, axis, size, offset)
        offset *= 2
    return array


def data_sum(array, devices, groups):
    array = axis_sum(array + exchange(array, "seq", groups, 1), "dp", devices)
    return array + exchange(array, "seq", groups, 2)


def in_order(pieces, place):
    stacked = jnp.stack(pieces)
    return [
        lax.dynamic_index_in_dim(stacked, jnp.bitwise_xor(place, n), 0, False)
        for n in range(len(pieces))
    ]


def pass_round(pieces, groups):
    return [pieces[0]] + [exchange(pieces[n], "seq", groups, n) for n in range(1, groups)]


def xpos_tables(count, lanes):
    positions = jnp.arange(count, dtype=F32)
    pair_index = jnp.arange(HALF, dtype=F32)
    frequency = 1.0 / 10000.0 ** (2.0 * pair_index / HEAD_DIM)
    angles = positions[:, None] * frequency[None, :]
    base_ratio = (2.0 * pair_index + 0.4 * HEAD_DIM) / (1.4 * HEAD_DIM)
    growth = base_ratio[None, :] ** ((positions[:, None] - count // 2) / XPOS_BASE)
    cosine, sine = jnp.cos(angles), jnp.sin(angles)
    tables = []
    for factor in (growth, 1.0 / growth):
        tables.append(jnp.tile(cosine * factor, (1, lanes // HALF)))
        tables.append(
            jnp.tile(jnp.concatenate([-sine * factor, sine * factor], axis=1), (1, lanes // HEAD_DIM))
        )
    return tables


def body(
    devices,
    groups,
    units,
    tokens,
    lengths,
    qkv_weight,
    out_weight,
    in_weight,
    down_weight,
    gain_in,
    gain_attn,
    gain_mid,
    gain_ffn,
    out_grad,
):
    sequences, span, model = tokens.shape
    each = range(sequences)
    data = ("dp", "seq")
    shards = devices * groups
    place = lax.axis_index("seq").astype(jnp.int32)
    local_width = qkv_weight.shape[2]
    heads_here = local_width // HEAD_DIM
    ffn_width = in_weight.shape[1]
    share = local_width // groups

    blocks = []
    for s in each:
        far = exchange(tokens[s], "seq", groups, 2)
        blocks.append([tokens[s], exchange(tokens[s], "seq", groups, 1), far])
    blocks[0].append(exchange(blocks[0][2], "seq", groups, 1))

    number = lax.axis_index("dp") * groups + place
    sizes = [gain_in.size, gain_mid.size, gain_attn.size, gain_ffn.size]
    cuts = [sum(sizes[:n]) for n in range(5)]
    chunk = qkv_weight.shape[1]
    by_device = qkv_weight.reshape(3, chunk, groups, share).transpose(2, 1, 0, 3)
    by_device = by_device.reshape(groups, chunk, 3 * share)
    flat = jnp.concatenate([gain_in, gain_mid, gain_attn.reshape(-1), gain_ffn.reshape(-1)])
    flat = jnp.pad(flat, (0, 16 * 3 * share - cuts[4])).reshape(16, 3 * share)
    pieces = [
        jnp.concatenate(
            [
                lax.dynamic_index_in_dim(by_device, jnp.bitwise_xor(place, n), 0, False),
                flat,
            ]
        )
        for n in range(groups)
    ]
    pieces = in_order(pass_round(pieces, groups), place)
    rows = jnp.concatenate([piece[:chunk] for piece in pieces], axis=0)
    heads_weight = lax.all_gather(rows, "dp", axis=0, tiled=True)

    flat = jnp.stack([piece[chunk:].reshape(-1)[: cuts[4]] for piece in pieces]).reshape(1, -1)
    row = lax.broadcasted_iota(jnp.int32, (devices, 1), 0)
    all_gains = jnp.where(row == lax.axis_index("dp"), flat, 0).astype(F32)
    all_gains = axis_sum(all_gains, "dp", devices).reshape(shards, cuts[4])
    pieces = [all_gains[:, cuts[n] : cuts[n + 1]] for n in range(4)]
    gain_one, gain_three = pieces[0].reshape(1, -1), pieces[1].reshape(1, -1)
    gain_two = pieces[2].reshape(shards, heads_here, -1).transpose(1, 0, 2).reshape(1, -1)
    gain_four = (
        pieces[3].reshape(shards, ffn_width // HEAD_DIM, -1).transpose(1, 0, 2).reshape(1, -1)
    )

    near_full = lax.all_gather(
        pack(in_weight, out_weight, [all_gains, blocks[0][2]]), data, axis=0, tiled=True
    )
    down_full = lax.all_gather(down_weight, data, axis=1, tiled=True)

    count = span * groups
    tables = xpos_tables(count, min(128, share))
    spot = place.reshape(1)
    metas = [jnp.stack([lengths[s], place]) for s in each]
    full_units = ffn_width * units

    first_low, projected = [], []
    mixed, logs, attended, att_sums, inner, branch = [], [], [], [], [], []
    last = ()
    for s in each:
        low, made = project(spot, blocks[s], gain_one, heads_weight, tables, last)
        first_low.append(low)
        projected.append(made)
        outs, log = attend(metas[s], made, groups)
        mixed.append(outs)
        logs.append(log)
        last = [log]
        if s == 0:
            far = relay(blocks[1][2], last)
            blocks[1].append(exchange(far, "seq", groups, 1))
            last = [far]
    passed = [pass_round(mixed[s], groups) for s in each]
    last = [*last, *passed[-1][1:]]
    for s in each:
        whole, sums = collect(spot, passed[s], last)
        attended.append(whole)
        att_sums.append(mp_rows(sums, units))
        last = [sums]
    last = [other for _, other in att_sums]
    for s in each:
        low, terms = out_branch(attended[s], *att_sums[s], gain_two, near_full, model, last)
        inner.append(low)
        branch.append(mp_sum(terms, units))
        last = [terms]

    hidden, third_low, active, slope, act_sums = [], [], [], [], []
    for s in each:
        made = widen(tokens[s], *branch[s], gain_three, near_full, ffn_width, last)
        hidden.append(made[0])
        third_low.append(made[1])
        active.append(made[2])
        slope.append(made[3])
        act_sums.append(mp_rows(made[4], units))
        last = [made[4]]

    grad_low = [out_grad[s] for s in each]
    norm = ([a for a, _ in act_sums], [b for _, b in act_sums], gain_four, full_units)
    down_parts = weight_grad(spot, grad_low, active, devices, groups, norm, False, last)
    down_sum = ScatterSum(down_parts, groups)
    last = [down_parts[0]]
    pre_low, third_terms, scaled, back_sums = [], [], [], []
    gain_four_grad = 0.0
    for s in each:
        part, sums, gain_part = wide_back(
            grad_low[s], down_full, active[s], *act_sums[s], gain_four, full_units, last
        )
        scaled.append(part)
        gain_four_grad += gain_part
        back_sums.append(mp_rows(sums, units))
        last = [sums]
    last = [down_sum.mates(last)] + [other for _, other in back_sums]
    for s in each:
        low, terms = pre_back(
            scaled[s], active[s], slope[s], *act_sums[s], *back_sums[s], near_full, full_units,
            last,
        )
        pre_low.append(low)
        third_terms.append(mp_sum(terms, units))
        last = [terms]

    def finish(s, after):
        terms = narrow(active[s], *act_sums[s], gain_four, down_full, full_units, after)
        return mp_sum(terms, units)

    def result(s, into, after):
        return result_rows(s, sequences, *wide_terms[s], hidden[s], into, after)

    gain_three_grad, gain_two_grad, gain_one_grad = 0.0, 0.0, 0.0
    order = jnp.bitwise_xor(place, jnp.array([3, 1, 2, 0], jnp.int32))
    first_sums = []
    grad_hidden, hidden_low, grads, projected_grads = [], [], [], []
    wide_terms = [finish(0, last)]
    last = [wide_terms[0][0]]
    for s in each:
        made = middle(
            grad_low[s], *third_terms[s], hidden[s], gain_three, near_full, attended[s],
            *att_sums[s], gain_two, model, last
        )
        grad_hidden.append(made[0])
        hidden_low.append(made[1])
        gain_three_grad += made[4]
        gain_two_grad += made[5]
        if s == 0:
            in_parts = weight_grad(
                spot, third_low, pre_low, devices, groups, None, Z_FIRST, [made[3]]
            )
            in_sum = ScatterSum(in_parts, groups, Z_FIRST)
            last = [down_sum.chips([in_parts[0], third_terms[1][1]])]
        else:
            wide_terms.append(finish(s, [made[3]]))
            last = [in_sum.mates([wide_terms[s][0]])]
        parts = share_out(
            spot, made[2], attended[s], *att_sums[s], *mp_rows(made[3], units), model, groups,
            last,
        )
        last = [parts[0]]
        grads.append(pass_round(parts, groups))
    for s in each:
        made = attend_back(
            metas[s], projected[s], grads[s], mixed[s], logs[s], tables, last,
            BACK_WEIGHT if s == 0 else 1,
        )
        projected_grads.append(made)
        last = [made]
        if s == 0:
            out_parts = weight_grad(
                spot, hidden_low, inner, devices, groups, None, False, last + grads[1][1:]
            )
            out_sum = ScatterSum(out_parts, groups)
            results = result(0, None, [out_parts[0], down_sum.out])
            last = [results]
        else:
            first_terms = [mp_sum(first_sums[0].own(last), units)]
            results = result(1, results, [first_terms[0][0]])
            last = [out_sum.chips([results])]
        away, kept, gain_part = first_back(
            order, made, first_low[s], heads_weight, gain_one, groups, last
        )
        gain_one_grad += gain_part
        first_sums.append(ScatterSum((away, kept), groups))
        if s == 0:
            last = [first_sums[0].mates([away])]
            last = [out_sum.mates(last)]
        else:
            last = [away, in_sum.rows]

    heads_part = heads_grad(first_low, projected_grads, last)
    heads_rows = lax.psum_scatter(heads_part, "dp", scatter_dimension=0, tiled=True)
    last = [first_sums[1].mates([heads_part])]
    gain_one_sums = mp_rows(gain_one_grad, units)

    def input_grad(s, into, after):
        return input_rows(
            s, sequences, tokens[s], *first_terms[s], gain_one, grad_hidden[s], into, after
        )

    gain_rows = jnp.concatenate(
        [
            (gain_one_sums[0] + gain_one_sums[1]).reshape(shards, -1),
            gain_three_grad.reshape(shards, -1),
            gain_two_grad.reshape(heads_here, shards, -1).transpose(1, 0, 2).reshape(shards, -1),
            gain_four_grad.reshape(ffn_width // HEAD_DIM, shards, -1)
            .transpose(1, 0, 2)
            .reshape(shards, -1),
        ],
        axis=1,
    )
    gain_rows = data_sum(gain_rows, devices, groups)

    grad_input = input_grad(0, None, last)
    first_terms.append(mp_sum(first_sums[1].own([grad_input, gain_rows]), units))
    in_sum.chips()
    pieces = [
        lax.dynamic_slice_in_dim(heads_rows, jnp.bitwise_xor(place, n) * chunk, chunk, 0)
        for n in range(groups)
    ]
    pieces = pass_round(pieces, groups)
    grad_input = input_grad(1, grad_input, [*last, *pieces[1:]])
    rows = jnp.stack(in_order(pieces, place)).astype(F32)
    grad_qkv_w = rows.reshape(groups, chunk, 3, share).transpose(2, 1, 0, 3)
    grad_qkv_w = grad_qkv_w.reshape(3, chunk, local_width)
    gain_sums = lax.dynamic_index_in_dim(gain_rows, number, 0, False)
    one, three, two, four = [gain_sums[cuts[n] : cuts[n + 1]] for n in range(4)]
    return (
        results,
        grad_input,
        grad_qkv_w,
        out_sum.out.T,
        in_sum.out,
        down_sum.out.T,
        one,
        two.reshape(gain_attn.shape),
        three,
        four.reshape(gain_ffn.shape),
    )


def solution(mesh):
    sizes = mesh.shape
    data = ("dp", "seq")
    in_specs = (
        P("dp", "seq", None),
        P("dp"),
        P(None, data, "mp"),
        P("mp", data),
        P(data, "mp"),
        P("mp", data),
        P(data),
        P("mp", data),
        P(data),
        P("mp", data),
        P("dp", "seq", None),
    )
    out_specs = (
        P("dp", "seq", None),
        P("dp", "seq", None),
        P(None, data, "mp"),
        P("mp", data),
        P(data, "mp"),
        P("mp", data),
        P(data),
        P("mp", data),
        P(data),
        P("mp", data),
    )
    run = partial(body, sizes["dp"], sizes["seq"], sizes["mp"])
    return jax.shard_map(run, mesh=mesh, in_specs=in_specs, out_specs=out_specs, check_vma=False)
```

```python
from functools import partial

import jax
import jax.numpy as jnp
from jax import lax
from jax.experimental import pallas as pl
from jax.experimental.pallas import tpu as pltpu
from jax.sharding import PartitionSpec as P

HEAD_DIM = 64
HALF = HEAD_DIM // 2
XPOS_BASE = 512
EPSILON = 1e-05
NEGATIVE = -1e30
LOG2_E = 1.4426950408889634
SCORE_SCALE = 0.125
VMEM = 56 * 2**20
Z_FIRST = True
BF16 = jnp.bfloat16
KERNEL_RATE = 0.25e9
BACK_WEIGHT = 25
PAUSE = 300
LONG_PAUSE = 200


def lasting(us):
    return pl.CostEstimate(flops=int(us * KERNEL_RATE), bytes_accessed=0, transcendentals=0)


F32 = jnp.float32


def params(limit=VMEM):
    return pltpu.CompilerParams(vmem_limit_bytes=limit)


def dot(left, right, left_dim, right_dim):
    return lax.dot_general(
        left, right, (((left_dim,), (right_dim,)), ((), ())), preferred_element_type=F32
    )


def swap_halves(block):
    width = block.shape[1]
    if width % 128:
        pieces = []
        for start in range(0, width, HEAD_DIM):
            pieces += [block[:, start + HALF : start + HEAD_DIM], block[:, start : start + HALF]]
        return jnp.concatenate(pieces, axis=1)
    lane = lax.broadcasted_iota(jnp.int32, (block.shape[0], 128), 1) % HEAD_DIM
    pieces = []
    for start in range(0, width, 128):
        part = block[:, start : start + 128]
        pieces.append(
            jnp.where(lane < HALF, pltpu.roll(part, 128 - HALF, 1), pltpu.roll(part, HALF, 1))
        )
    return pieces[0] if len(pieces) == 1 else jnp.concatenate(pieces, axis=1)


def turned(block, cosine, sine, sign):
    lanes = cosine.shape[1]
    pieces = []
    for start in range(0, block.shape[1], lanes):
        part = block[:, start : start + lanes]
        pieces.append(part * cosine + sign * (swap_halves(part) * sine))
    return pieces[0] if len(pieces) == 1 else jnp.concatenate(pieces, axis=1)


def project_kernel(place, *refs, groups, share):
    blocks, refs = refs[:groups], refs[groups:]
    gain, weight, cos_q, sin_q, cos_k, sin_k, low, made, held = refs
    for offset, block in enumerate(blocks):

        @pl.when(pl.program_id(0) == offset)
        def _(block=block):
            held[...] = block[...]

    normal, _ = row_norm(held[...].astype(F32))
    rows = (normal * gain[...]).astype(BF16)
    low[...] = rows
    out = dot(rows, weight[...], 1, 0)
    queries = turned(out[:, :share], cos_q[...], sin_q[...], 1)
    keys = turned(out[:, share : 2 * share], cos_k[...], sin_k[...], 1)
    made[...] = jnp.concatenate([queries, keys, out[:, 2 * share :]], axis=1).astype(BF16)


def project(place, blocks, gain, weight, tables, after=()):
    groups = len(blocks)
    span, model = blocks[0].shape
    width = weight.shape[1]
    lanes = tables[0].shape[1]

    def here(n, p):
        return (jnp.bitwise_xor(n, p[0]), 0)

    return call(
        partial(project_kernel, groups=groups, share=width // 3),
        "project",
        (groups,),
        [(block, (span, model), None) for block in blocks]
        + [(gain, (1, model), None), (weight, (model, width), None)]
        + [(table, (span, lanes), here) for table in tables],
        [
            ((groups * span, model), BF16, (span, model), here),
            ((groups * span, width), BF16, (span, width), here),
        ],
        [pltpu.VMEM((span, model), BF16)],
        5e-9 * groups * span * model * width,
        after,
        place,
    )


def attend_kernel(meta, projected, *refs, groups, heads, block):
    outs, log_ref, vt_all, o_all = refs[:groups], refs[groups], refs[groups + 1], refs[groups + 2]
    step = pl.program_id(0)
    length, place = meta[0], meta[1]
    share = heads * HEAD_DIM
    span = outs[0].shape[0]

    def lanes(part, h):
        return slice(part * share + h * HEAD_DIM, part * share + (h + 1) * HEAD_DIM)

    @pl.when(step == 0)
    def _():
        for h in range(heads):
            vt_all[h] = projected[:, lanes(2, h)].T

    start = pl.multiple_of(step * block, block)
    queries = [projected[pl.ds(start, block), lanes(0, h)] for h in range(heads)]
    scale = SCORE_SCALE * LOG2_E

    def keys_block(index, carry, masked):
        at = pl.multiple_of(index * block, block)
        if masked:
            key_pos = at + lax.broadcasted_iota(jnp.int32, (block, block), 0)
            query_pos = start + lax.broadcasted_iota(jnp.int32, (block, block), 1)
            allowed = (key_pos <= query_pos) & (key_pos < length)
        new = []
        for h in range(heads):
            top, total, mixed = carry[h]
            scores = dot(projected[pl.ds(at, block), lanes(1, h)], queries[h], 1, 1)
            if masked:
                scores = jnp.where(allowed, scores, NEGATIVE)
            higher = jnp.maximum(top, jnp.max(scores, axis=0, keepdims=True))
            fade = jnp.exp2((top - higher) * scale)
            weights = jnp.exp2((scores - higher) * scale)
            total = total * fade + jnp.sum(weights, axis=0, keepdims=True)
            added = dot(vt_all[h, :, pl.ds(at, block)], weights.astype(BF16), 1, 0)
            new.append((higher, total, mixed * fade + added))
        return tuple(new)

    carry = tuple(
        (
            jnp.full((1, block), NEGATIVE, F32),
            jnp.zeros((1, block), F32),
            jnp.zeros((HEAD_DIM, block), F32),
        )
        for _ in range(heads)
    )
    whole = jnp.minimum(step, length // block)
    end = jnp.minimum(step + 1, (length + block - 1) // block)
    carry = lax.fori_loop(0, whole, lambda n, c: keys_block(n, c, False), carry)
    carry = lax.fori_loop(whole, end, lambda n, c: keys_block(n, c, True), carry)
    pieces = []
    for h in range(heads):
        top, total, mixed = carry[h]
        pieces.append((mixed / total).T)
        log_ref[h : h + 1, :] = top * scale + jnp.log2(total)
    o_all[pl.ds(start, block), :] = jnp.concatenate(pieces, axis=1).astype(BF16)

    @pl.when(step == pl.num_programs(0) - 1)
    def _():
        for offset, out in enumerate(outs):
            at = pl.multiple_of(jnp.bitwise_xor(place, offset) * span, span)
            out[...] = o_all[pl.ds(at, span), :]


def attend(meta, projected, groups, after=()):
    count, width = projected.shape
    share = width // 3
    span = count // groups
    heads = share // HEAD_DIM
    block = min(512, span)
    results = call(
        partial(attend_kernel, groups=groups, heads=heads, block=block),
        "attend",
        (count // block,),
        [(projected, (count, width), None)],
        [((span, share), BF16, (span, share), None)] * groups
        + [((heads, count), F32, (heads, block), lambda n, m: (0, n))],
        [pltpu.VMEM((heads, HEAD_DIM, count), BF16), pltpu.VMEM((count, share), BF16)],
        2.9e-8 * count * count * share,
        after,
        meta,
    )
    return results[:groups], results[groups]


def attend_back_kernel(meta, projected, *refs, groups, heads, block):
    grads, mixed = refs[:groups], refs[groups : 2 * groups]
    log_ref, cos_q, sin_q, cos_k, sin_k, out = refs[2 * groups : 2 * groups + 6]
    g_all, kt_all, dot_all, dqt_all, dk_sum, dv_sum = refs[2 * groups + 6 :]
    length, place = meta[0], meta[1]
    span = grads[0].shape[0]
    count = groups * span
    share = heads * HEAD_DIM
    scale = SCORE_SCALE * LOG2_E

    def lanes(part, h):
        return slice(part * share + h * HEAD_DIM, part * share + (h + 1) * HEAD_DIM)

    for h in range(heads):
        kt_all[h] = projected[:, lanes(1, h)].T
    for offset in range(groups):
        at = pl.multiple_of(jnp.bitwise_xor(place, offset) * span, span)
        g_all[pl.ds(at, span), :] = grads[offset][...]
        both = grads[offset][...].astype(F32) * mixed[offset][...].astype(F32)
        for h in range(heads):
            dot_all[h : h + 1, pl.ds(at, span)] = jnp.sum(
                both[:, lanes(0, h)].T, axis=0, keepdims=True
            )
    dqt_all[...] = jnp.zeros_like(dqt_all)
    query_blocks = count // block

    def keys_block(index, _):
        key_at = pl.multiple_of(index * block, block)
        keys = [projected[pl.ds(key_at, block), lanes(1, h)] for h in range(heads)]
        values = [projected[pl.ds(key_at, block), lanes(2, h)] for h in range(heads)]
        dk_sum[...] = jnp.zeros_like(dk_sum)
        dv_sum[...] = jnp.zeros_like(dv_sum)

        def query_block(index, _, masked):
            at = pl.multiple_of(index * block, block)
            if masked:
                key_pos = key_at + lax.broadcasted_iota(jnp.int32, (block, block), 0)
                query_pos = at + lax.broadcasted_iota(jnp.int32, (block, block), 1)
                allowed = (key_pos <= query_pos) & (key_pos < length)
            for h in range(heads):
                query = projected[pl.ds(at, block), lanes(0, h)]
                grad = g_all[pl.ds(at, block), lanes(0, h)]
                scores = dot(keys[h], query, 1, 1)
                weights = jnp.exp2(scores * scale - log_ref[h : h + 1, pl.ds(at, block)])
                if masked:
                    weights = jnp.where(allowed, weights, 0.0)
                grad_weights = dot(values[h], grad, 1, 1)
                grad_scores = weights * (grad_weights - dot_all[h : h + 1, pl.ds(at, block)])
                grad_scores = grad_scores.astype(BF16)
                dv_sum[h] += dot(weights.astype(BF16), grad, 1, 0)
                dk_sum[h] += dot(grad_scores, query, 1, 0)
                dqt_all[h, :, pl.ds(at, block)] += dot(
                    kt_all[h, :, pl.ds(key_at, block)], grad_scores, 1, 0
                )
            return 0

        crosses = key_at + block > length
        whole = jnp.where(crosses, query_blocks, index + 1)
        lax.fori_loop(index, whole, partial(query_block, masked=True), 0)
        lax.fori_loop(whole, query_blocks, partial(query_block, masked=False), 0)
        dk = jnp.concatenate([dk_sum[h] for h in range(heads)], axis=1) * SCORE_SCALE
        dv = jnp.concatenate([dv_sum[h] for h in range(heads)], axis=1)
        turn = (cos_k[pl.ds(key_at, block), :], sin_k[pl.ds(key_at, block), :])
        out[pl.ds(key_at, block), share : 2 * share] = turned(dk, *turn, -1).astype(BF16)
        out[pl.ds(key_at, block), 2 * share :] = dv.astype(BF16)
        return 0

    used = (length + block - 1) // block
    lax.fori_loop(0, used, keys_block, 0)

    def no_keys(index, _):
        at = pl.multiple_of(index * block, block)
        out[pl.ds(at, block), share:] = jnp.zeros((block, 2 * share), BF16)
        return 0

    lax.fori_loop(used, query_blocks, no_keys, 0)
    for index in range(query_blocks):
        at = slice(index * block, (index + 1) * block)
        dq = jnp.concatenate([dqt_all[h, :, at].T for h in range(heads)], axis=1) * SCORE_SCALE
        out[at, :share] = turned(dq, cos_q[at, :], sin_q[at, :], -1).astype(BF16)


def attend_back(meta, projected, grads, mixed, logs, tables, after=(), weight=1):
    groups = len(grads)
    count, width = projected.shape
    share = width // 3
    span = count // groups
    heads = share // HEAD_DIM
    block = min(512, span)
    return call(
        partial(attend_back_kernel, groups=groups, heads=heads, block=block),
        "attend_back",
        (1,),
        [(projected, (count, width), None)]
        + [(piece, (span, share), None) for piece in (*grads, *mixed)]
        + [(logs, logs.shape, None)]
        + [(table, table.shape, None) for table in tables],
        [((count, width), BF16, (count, width), None)],
        [
            pltpu.VMEM((count, share), BF16),
            pltpu.VMEM((heads, HEAD_DIM, count), BF16),
            pltpu.VMEM((heads, count), F32),
            pltpu.VMEM((heads, HEAD_DIM, count), F32),
            pltpu.VMEM((heads, block, HEAD_DIM), F32),
            pltpu.VMEM((heads, block, HEAD_DIM), F32),
        ],
        4.2e-8 * count * count * share * weight,
        after,
        meta,
    )[0]


def heads_grad_kernel(*refs, sequences):
    grads, lows, out, turned_grads = (
        refs[:sequences],
        refs[sequences : 2 * sequences],
        refs[2 * sequences],
        refs[2 * sequences + 1],
    )
    count = grads[0].shape[0]

    @pl.when(pl.program_id(0) == 0)
    def _():
        for s in range(sequences):
            turned_grads[:, s * count : (s + 1) * count] = grads[s][...].T

    total = dot(turned_grads[:, :count], lows[0][...], 1, 0)
    for s in range(1, sequences):
        total += dot(turned_grads[:, s * count : (s + 1) * count], lows[s][...], 1, 0)
    out[...] = total.T.astype(BF16)


def heads_grad(lows, grads, after=()):
    sequences = len(lows)
    count, model = lows[0].shape
    width = grads[0].shape[1]
    tile = 512
    return call(
        partial(heads_grad_kernel, sequences=sequences),
        "heads_grad",
        (model // tile,),
        [(grad, (count, width), None) for grad in grads]
        + [(low, (count, tile), lambda n: (0, n)) for low in lows],
        [((model, width), BF16, (tile, width), lambda n: (n, 0))],
        [pltpu.VMEM((width, sequences * count), BF16)],
        3e-9 * sequences * count * model * width,
        after,
    )[0]


def normed_rows(block, column_mean, column_std, gain):
    return (block.astype(F32) - column_mean) * column_std * gain


def moments(own, other, width):
    total = own + other
    mean = total[0:1] / width
    return mean, lax.rsqrt(total[1:2] / width - mean * mean + EPSILON)


def as_column(row):
    return jnp.broadcast_to(row, (128, row.shape[1])).T[:, 0:1]


def as_row(block):
    width = block.shape[1]
    part = block[:, 0:128]
    for start in range(128, width, 128):
        part = part + block[:, start : start + 128]
    return jnp.sum(part.T, axis=0, keepdims=True)


def weight_grad_kernel(place, *refs, sequences, devices, groups, chunk, offsets, normed, extra):
    lefts, refs = refs[:sequences], refs[sequences:]
    rights, refs = refs[:sequences], refs[sequences:]
    if normed:
        own_sums, other_sums, gain = refs[:sequences], refs[sequences : 2 * sequences], refs[2 * sequences]
        refs = refs[2 * sequences + 1 :]
    away, kept, turned_left = refs[extra : extra + 3]
    columns_ref = refs[extra + 3] if normed else None
    span = lefts[0].shape[0]

    @pl.when(pl.program_id(0) == 0)
    def _():
        row = 0
        for device, offset in offsets:
            target = jnp.bitwise_xor(place[0], offset)
            at = pl.multiple_of((device * groups + target) * chunk, chunk)
            for s in range(sequences):
                turned_left[row : row + chunk, s * span : (s + 1) * span] = lefts[s][
                    :, pl.ds(at, chunk)
                ].T
            row += chunk
        if normed:
            for s in range(sequences):
                mean, std = moments(own_sums[s][...], other_sums[s][...], normed)
                columns_ref[2 * s] = jnp.broadcast_to(as_column(mean), (span, 128))
                columns_ref[2 * s + 1] = jnp.broadcast_to(as_column(std), (span, 128))

    values = []
    for s in range(sequences):
        block = rights[s][...]
        if normed:
            block = normed_rows(
                block, columns_ref[2 * s, :, 0:1], columns_ref[2 * s + 1, :, 0:1], gain[...]
            ).astype(BF16)
        values.append(block)
    block = turned_left.shape[0] // 4
    parts = [away.at[:block], away.at[block:], kept.at[:block], kept.at[block:]]
    for n, part in enumerate(parts):
        rows = slice(n * block, (n + 1) * block)
        total = dot(turned_left[rows, :span], values[0], 1, 0)
        for s in range(1, sequences):
            total += dot(turned_left[rows, s * span : (s + 1) * span], values[s], 1, 0)
        part[...] = total.astype(BF16)


def weight_grad(place, lefts, rights, devices, groups, norm=None, z_first=False, after=()):
    sequences = len(rights)
    span = rights[0].shape[-2]
    width = lefts[0].shape[1]
    layers = rights[0].ndim == 3
    columns = rights[0].shape[0] * rights[0].shape[2] if layers else rights[0].shape[1]
    chunk = width // (devices * groups)
    tile = 512 if rights[0].shape[-1] % 512 == 0 else rights[0].shape[-1]
    half = width // 2
    if z_first:
        offsets = [(d, o) for core in (1, 0) for d in range(devices) for o in (2 + core, core)]
    else:
        offsets = [(d, o) for o in (3, 1, 2, 0) for d in range(devices)]
    if layers:
        tiles = rights[0].shape[2] // tile
        right_spec = pl.BlockSpec((None, span, tile), lambda n, p: (n // tiles, 0, n % tiles))
    else:
        right_spec = pl.BlockSpec((span, tile), lambda n, p: (0, n))
    if len(lefts) == sequences:
        in_specs = [pl.BlockSpec((span, width), lambda n, p: (0, 0))] * sequences
    else:
        lefts = lefts * sequences
        in_specs = [
            pl.BlockSpec((span, width), lambda n, p, s=s: (s, 0)) for s in range(sequences)
        ]
    in_specs += [right_spec] * sequences
    operands = [*lefts, *rights]
    scratch = [pltpu.VMEM((width, sequences * span), BF16)]
    full = 0
    if norm:
        own_sums, other_sums, gain, full = norm
        in_specs += [pl.BlockSpec((2, span), lambda n, p: (0, 0))] * (2 * sequences)
        in_specs += [pl.BlockSpec((1, tile), lambda n, p: (0, n))]
        operands += [*own_sums, *other_sums, gain]
        scratch += [pltpu.VMEM((2 * sequences, span, 128), F32)]
    in_specs += [pl.BlockSpec(memory_space=pl.ANY)] * len(after)
    return pl.pallas_call(
        partial(
            weight_grad_kernel,
            sequences=sequences,
            devices=devices,
            groups=groups,
            chunk=chunk,
            offsets=offsets,
            normed=full,
            extra=len(after),
        ),
        grid_spec=pltpu.PrefetchScalarGridSpec(
            num_scalar_prefetch=1,
            grid=(columns // tile,),
            in_specs=in_specs,
            out_specs=[pl.BlockSpec((half, tile), lambda n, p: (0, n))] * 2,
            scratch_shapes=scratch,
        ),
        out_shape=[jax.ShapeDtypeStruct((half, columns), BF16)] * 2,
        compiler_params=params(),
        cost_estimate=lasting(2.9e-9 * sequences * span * width * columns),
        name="weight_grad",
    )(place, *operands, *after)


def call(kernel, name, grid, ins, outs, scratch, us, after=(), scalars=None, into=None):
    if into is not None:
        after = [into, *after]
    extra = len(after)
    first = 0 if scalars is None else 1
    count = first + len(ins)

    def run(*refs):
        kernel(*refs[:count], *refs[count + extra :])

    def spec(block, index):
        if index is None:
            return pl.BlockSpec(block, lambda *_: (0,) * len(block))
        return pl.BlockSpec(block, index)

    return pl.pallas_call(
        run,
        grid_spec=pltpu.PrefetchScalarGridSpec(
            num_scalar_prefetch=first,
            grid=grid,
            in_specs=[spec(block, index) for _, block, index in ins]
            + [pl.BlockSpec(memory_space=pl.ANY)] * extra,
            out_specs=[spec(block, index) for _, _, block, index in outs],
            scratch_shapes=scratch,
        ),
        out_shape=[jax.ShapeDtypeStruct(shape, dtype) for shape, dtype, _, _ in outs],
        input_output_aliases={} if into is None else {count: 0},
        compiler_params=params(),
        cost_estimate=lasting(us),
        name=name,
    )(*(() if scalars is None else (scalars,)), *[array for array, _, _ in ins], *after)


def pack_kernel(columns, rows, out):
    width = columns.shape[1]
    out[:, :width] = columns[...]
    out[:, width:] = rows[...].T


def pack(columns, rows, after=()):
    height, width = columns.shape
    total = width + rows.shape[0]
    return call(
        pack_kernel,
        "pack",
        (1,),
        [(columns, columns.shape, None), (rows, rows.shape, None)],
        [((height, total), BF16, (height, total), None)],
        [],
        1,
        after,
    )[0]


def collect_kernel(place, *refs, groups):
    pieces, (whole, sums) = refs[:groups], refs[groups:]
    share = pieces[0].shape[1]
    total, squares = 0.0, 0.0
    for offset, piece in enumerate(pieces):
        at = pl.multiple_of(jnp.bitwise_xor(place[0], offset) * share, share)
        block = piece[...]
        whole[:, pl.ds(at, share)] = block
        wide = block.astype(F32)
        total += as_row(wide)
        squares += as_row(wide * wide)
    sums[...] = jnp.concatenate([total, squares], axis=0)


def collect(place, pieces, after=()):
    groups = len(pieces)
    span, share = pieces[0].shape
    if share % 128:
        stacked = jnp.stack(pieces)
        whole = jnp.concatenate(
            [
                lax.dynamic_index_in_dim(stacked, jnp.bitwise_xor(place[0], n), 0, False)
                for n in range(groups)
            ],
            axis=1,
        )
        wide = whole.astype(F32)
        return whole, jnp.stack([jnp.sum(wide, axis=1), jnp.sum(wide * wide, axis=1)])
    width = groups * share
    return call(
        partial(collect_kernel, groups=groups),
        "collect",
        (1,),
        [(piece, (span, share), None) for piece in pieces],
        [((span, width), BF16, (span, width), None), ((2, span), F32, (2, span), None)],
        [],
        5e-6 * span * width,
        after,
        place,
    )


def out_kernel(mixed, own, other, gain, weight, inner, branch, *, full):
    mean, std = moments(own[...], other[...], full)
    low = normed_rows(mixed[...], as_column(mean), as_column(std), gain[...]).astype(BF16)
    inner[...] = low
    branch[...] = dot(low, weight[...], 1, 1).astype(BF16)


def out_branch(mixed, own, other, gain, near_full, full, after=()):
    span, width = mixed.shape
    model = near_full.shape[0]
    place = near_full.shape[1] // width - 1
    rows = min(256, span)
    return call(
        partial(out_kernel, full=full),
        "out_branch",
        (span // rows,),
        [
            (mixed, (rows, width), lambda n: (n, 0)),
            (own, (2, rows), lambda n: (0, n)),
            (other, (2, rows), lambda n: (0, n)),
            (gain, (1, width), None),
            (near_full, (model, width), lambda n: (0, place)),
        ],
        [
            ((span, width), BF16, (rows, width), lambda n: (n, 0)),
            ((span, model), BF16, (rows, model), lambda n: (n, 0)),
        ],
        [],
        6e-9 * span * width * model,
        after,
    )


def row_norm(block):
    mean = jnp.mean(block, axis=-1, keepdims=True)
    centered = block - mean
    std = lax.rsqrt(jnp.mean(centered * centered, axis=-1, keepdims=True) + EPSILON)
    return centered * std, std


def widen_kernel(tokens, own, other, gain, weight, hidden, low, active, slope, sums, total, squares):
    step = pl.program_id(0)

    @pl.when(step == 0)
    def _():
        block = tokens[...].astype(F32) + (own[...].astype(F32) + other[...].astype(F32))
        hidden[...] = block
        normal, _ = row_norm(block)
        low[...] = (normal * gain[...]).astype(BF16)
        total[...] = jnp.zeros_like(total)
        squares[...] = jnp.zeros_like(squares)

    pre = dot(low[...], weight[...], 1, 0)
    below = 0.5 + 0.5 * lax.erf(pre * 0.7071067811865476)
    value = pre * below
    active[...] = value.astype(BF16)
    slope[...] = (below + pre * (0.3989422804014327 * jnp.exp2(pre * pre * (-0.5 * LOG2_E)))).astype(
        BF16
    )
    part, square = total[...], squares[...]
    for start in range(0, value.shape[1], 128):
        piece = value[:, start : start + 128]
        part += piece
        square += piece * piece
    total[...] = part
    squares[...] = square

    @pl.when(step == pl.num_programs(0) - 1)
    def _():
        sums[...] = jnp.concatenate([as_row(total[...]), as_row(squares[...])], axis=0)


def widen(number, tokens, own, other, gain, weight, units, after=()):
    span, model = own.shape
    tile = 512
    rows = (span, model)
    across = (span, tile)
    return call(
        widen_kernel,
        "widen",
        (units // tile,),
        [
            (tokens, rows, lambda n: (number, 0)),
            (own, rows, None),
            (other, rows, None),
            (gain, (1, model), None),
            (weight, (model, tile), lambda n: (0, n)),
        ],
        [
            (rows, F32, rows, None),
            (rows, BF16, rows, None),
            ((span, units), BF16, across, lambda n: (0, n)),
            ((span, units), BF16, across, lambda n: (0, n)),
            ((2, span), F32, (2, span), None),
        ],
        [pltpu.VMEM((span, 128), F32)] * 2,
        5.4e-9 * span * model * units,
        after,
    )


def narrow_kernel(active, own, other, gain, weight, branch, total, columns, *, full):
    step = pl.program_id(0)

    @pl.when(step == 0)
    def _():
        mean, std = moments(own[...], other[...], full)
        columns[0] = jnp.broadcast_to(as_column(mean), columns.shape[1:])
        columns[1] = jnp.broadcast_to(as_column(std), columns.shape[1:])
        total[...] = jnp.zeros_like(total)

    low = normed_rows(active[...], columns[0, :, 0:1], columns[1, :, 0:1], gain[...]).astype(BF16)
    total[...] += dot(low, weight[...], 1, 0)

    @pl.when(step == pl.num_programs(0) - 1)
    def _():
        branch[...] = total[...].astype(BF16)


def narrow(active, own, other, gain, weight, full, after=()):
    span, units = active.shape
    model = weight.shape[1]
    tile = 512
    sums = (2, span)
    return call(
        partial(narrow_kernel, full=full),
        "narrow",
        (units // tile,),
        [
            (active, (span, tile), lambda n: (0, n)),
            (own, sums, None),
            (other, sums, None),
            (gain, (1, tile), lambda n: (0, n)),
            (weight, (tile, model), lambda n: (n, 0)),
        ],
        [((span, model), BF16, (span, model), None)],
        [pltpu.VMEM((span, model), F32), pltpu.VMEM((2, span, 128), F32)],
        3.7e-9 * span * model * units,
        after,
    )[0]


def wide_back_kernel(grads, weight, gain, *refs, sequences, full):
    active, refs = refs[:sequences], refs[sequences:]
    own, refs = refs[:sequences], refs[sequences:]
    other, refs = refs[:sequences], refs[sequences:]
    scaled, refs = refs[:sequences], refs[sequences:]
    sums, refs = refs[:sequences], refs[sequences:]
    gain_grad, columns, totals = refs
    step = pl.program_id(0)
    span = active[0].shape[0]

    @pl.when(step == 0)
    def _():
        for s in range(sequences):
            mean, std = moments(own[s][...], other[s][...], full)
            columns[2 * s] = jnp.broadcast_to(as_column(mean), columns.shape[1:])
            columns[2 * s + 1] = jnp.broadcast_to(as_column(std), columns.shape[1:])
        totals[...] = jnp.zeros_like(totals)

    every = dot(grads[...], weight[...], 1, 1)
    gain_part = 0.0
    for s in range(sequences):
        grad = every[s * span : (s + 1) * span]
        normal = (active[s][...].astype(F32) - columns[2 * s, :, 0:1]) * columns[2 * s + 1, :, 0:1]
        product = grad * normal
        gain_part += jnp.sum(product, axis=0, keepdims=True)
        grad = grad * gain[...]
        scaled[s][...] = grad.astype(BF16)
        product = product * gain[...]
        part, other_part = totals[2 * s], totals[2 * s + 1]
        for start in range(0, grad.shape[1], 128):
            part += grad[:, start : start + 128]
            other_part += product[:, start : start + 128]
        totals[2 * s] = part
        totals[2 * s + 1] = other_part
    gain_grad[...] = gain_part

    @pl.when(step == pl.num_programs(0) - 1)
    def _():
        for s in range(sequences):
            sums[s][...] = jnp.concatenate(
                [as_row(totals[2 * s]), as_row(totals[2 * s + 1])], axis=0
            )


def wide_back(grads, weight, active, own, other, gain, full, after=()):
    sequences = len(active)
    span, units = active[0].shape
    model = weight.shape[1]
    tile = 512
    sums = (2, span)
    across = (span, tile)
    tiled = lambda n: (0, n)
    made = call(
        partial(wide_back_kernel, sequences=sequences, full=full),
        "wide_back",
        (units // tile,),
        [
            (grads, (sequences * span, model), None),
            (weight, (tile, model), lambda n: (n, 0)),
            (gain, (1, tile), tiled),
        ]
        + [(array, across, tiled) for array in active]
        + [(array, sums, None) for array in (*own, *other)],
        [((span, units), BF16, across, tiled)] * sequences
        + [(sums, F32, sums, None)] * sequences
        + [((1, units), F32, (1, tile), tiled)],
        [pltpu.VMEM((2 * sequences, span, 128), F32)] * 2,
        3.5e-9 * sequences * span * model * units,
        after,
    )
    return made[:sequences], made[sequences : 2 * sequences], made[2 * sequences]


def pre_back_kernel(
    scaled, active, slope, own, other, own_back, other_back, weight, grads, branch, total, columns, *, full
):
    step = pl.program_id(0)

    @pl.when(step == 0)
    def _():
        mean, std = moments(own[...], other[...], full)
        back = (own_back[...] + other_back[...]) / full
        for n, row in enumerate((mean, std, back[0:1], back[1:2])):
            columns[n] = jnp.broadcast_to(as_column(row), columns.shape[1:])
        total[...] = jnp.zeros_like(total)

    std = columns[1, :, 0:1]
    normal = (active[...].astype(F32) - columns[0, :, 0:1]) * std
    grad = std * (scaled[...].astype(F32) - columns[2, :, 0:1] - normal * columns[3, :, 0:1])
    low = (grad * slope[...].astype(F32)).astype(BF16)
    grads[...] = low
    total[...] += dot(low, weight[...], 1, 1)

    @pl.when(step == pl.num_programs(0) - 1)
    def _():
        branch[...] = total[...].astype(BF16)


def pre_back(scaled, active, slope, own, other, own_back, other_back, weight, full, after=()):
    span, units = active.shape
    model = weight.shape[0]
    tile = 512
    sums = (2, span)
    across = (span, tile)
    tiled = lambda n: (0, n)
    return call(
        partial(pre_back_kernel, full=full),
        "pre_back",
        (units // tile,),
        [
            (scaled, across, tiled),
            (active, across, tiled),
            (slope, across, tiled),
            (own, sums, None),
            (other, sums, None),
            (own_back, sums, None),
            (other_back, sums, None),
            (weight, (model, tile), tiled),
        ],
        [((span, units), BF16, across, tiled), ((span, model), BF16, (span, model), None)],
        [pltpu.VMEM((span, model), F32), pltpu.VMEM((4, span, 128), F32)],
        4.6e-9 * span * model * units,
        after,
    )


def middle_kernel(
    grads, own, other, hidden, gain, weight, mixed, own_sums, other_sums, gain_attn,
    grad_hidden, low, scaled, sums, gain_grad, gain_attn_grad, *, full
):
    step = pl.program_id(0)

    @pl.when(step == 0)
    def _():
        gain_grad[...] = jnp.zeros_like(gain_grad)
        gain_attn_grad[...] = jnp.zeros_like(gain_attn_grad)

    normal, std = row_norm(hidden[...])
    grad = own[...].astype(F32) + other[...].astype(F32)
    gain_grad[...] += jnp.sum(grad * normal, axis=0, keepdims=True)
    part = grad * gain[...]
    back = std * (
        part
        - jnp.mean(part, axis=-1, keepdims=True)
        - normal * jnp.mean(part * normal, axis=-1, keepdims=True)
    )
    total = grads[...].astype(F32) + back
    grad_hidden[...] = total
    rows = total.astype(BF16)
    low[...] = rows
    inner = dot(rows, weight[...], 1, 0)
    mean, deviation = moments(own_sums[...], other_sums[...], full)
    normal = (mixed[...].astype(F32) - as_column(mean)) * as_column(deviation)
    gain_attn_grad[...] += jnp.sum(inner * normal, axis=0, keepdims=True)
    inner = inner * gain_attn[...]
    scaled[...] = inner
    sums[...] = jnp.concatenate([as_row(inner), as_row(inner * normal)], axis=0)


def middle(
    number, grads, own, other, hidden, gain, near_full, mixed, own_sums, other_sums, gain_attn, full, after=()
):
    span, model = hidden.shape
    width = mixed.shape[1]
    place = near_full.shape[1] // width - 1
    rows = min(256, span)
    below = number * (span // rows)
    by_row = lambda n: (n, 0)
    by_column = lambda n: (0, n)
    return call(
        partial(middle_kernel, full=full),
        "middle",
        (span // rows,),
        [
            (grads, (rows, model), lambda n: (n + below, 0)),
            (own, (rows, model), by_row),
            (other, (rows, model), by_row),
            (hidden, (rows, model), by_row),
            (gain, (1, model), None),
            (near_full, (model, width), lambda n: (0, place)),
            (mixed, (rows, width), by_row),
            (own_sums, (2, rows), by_column),
            (other_sums, (2, rows), by_column),
            (gain_attn, (1, width), None),
        ],
        [
            ((span, model), F32, (rows, model), by_row),
            ((span, model), BF16, (rows, model), by_row),
            ((span, width), F32, (rows, width), by_row),
            ((2, span), F32, (2, rows), by_column),
            ((1, model), F32, (1, model), None),
            ((1, width), F32, (1, width), None),
        ],
        [],
        1.2e-8 * span * width * model,
        after,
    )


def share_out_kernel(place, scaled, mixed, own, other, own_back, other_back, *outs, full):
    mean, std = moments(own[...], other[...], full)
    back = (own_back[...] + other_back[...]) / full
    mean, std, first, second = [as_column(row) for row in (mean, std, back[0:1], back[1:2])]
    share = outs[0].shape[1]
    for offset, out in enumerate(outs):
        at = pl.multiple_of(jnp.bitwise_xor(place[0], offset) * share, share)
        normal = (mixed[:, pl.ds(at, share)].astype(F32) - mean) * std
        out[...] = (std * (scaled[:, pl.ds(at, share)] - first - normal * second)).astype(BF16)


def share_out(place, scaled, mixed, own, other, own_back, other_back, full, groups, after=()):
    span, width = scaled.shape
    share = width // groups
    if share % 128:
        mean, std = moments(own, other, full)
        back = (own_back + other_back) / full
        mean, std, first, second = [row.reshape(-1, 1) for row in (mean, std, back[0], back[1])]
        normal = (mixed.astype(F32) - mean) * std
        grads = (std * (scaled - first - normal * second)).astype(BF16)
        return [
            lax.dynamic_slice_in_dim(grads, jnp.bitwise_xor(place[0], n) * share, share, 1)
            for n in range(groups)
        ]
    sums = (2, span)
    return call(
        partial(share_out_kernel, full=full),
        "share_out",
        (1,),
        [
            (scaled, (span, width), None),
            (mixed, (span, width), None),
            (own, sums, None),
            (other, sums, None),
            (own_back, sums, None),
            (other_back, sums, None),
        ],
        [((span, share), BF16, (span, share), None)] * groups,
        [],
        7.6e-6 * span * width,
        after,
        place,
    )


def first_back_kernel(order, grads, low, weight, gain, away, kept, gain_grad, total):
    step = pl.program_id(0)
    grad = dot(grads[...], weight[...], 1, 1)
    made = grad.astype(BF16)

    @pl.when(step < 2)
    def _():
        away[...] = made

    @pl.when(step >= 2)
    def _():
        kept[...] = made

    @pl.when(step == 0)
    def _():
        total[...] = jnp.zeros_like(total)

    total[...] += jnp.sum(grad * low[...].astype(F32), axis=0, keepdims=True)

    @pl.when(step == pl.num_programs(0) - 1)
    def _():
        gain_grad[...] = total[...] / gain[...]


def first_back(order, grads, low, weight, gain, groups, after=()):
    count, width = grads.shape
    model = weight.shape[0]
    span = count // groups
    rows = (span, model)
    return call(
        first_back_kernel,
        "first_back",
        (groups,),
        [
            (grads, (span, width), lambda n, p: (p[n], 0)),
            (low, rows, lambda n, p: (p[n], 0)),
            (weight, (model, width), None),
            (gain, (1, model), None),
        ],
        [
            ((2 * span, model), BF16, rows, lambda n, p: (jnp.minimum(n, 1), 0)),
            ((2 * span, model), BF16, rows, lambda n, p: (jnp.maximum(n - 2, 0), 0)),
            ((1, model), F32, (1, model), None),
        ],
        [pltpu.VMEM((1, model), F32)],
        4.5e-9 * count * model * width,
        after,
        order,
    )


def relay_kernel(array, out):
    out[...] = array[...]


def relay(array, after):
    rows = min(128, array.shape[0])
    block = (rows, array.shape[1])
    return call(
        relay_kernel,
        "relay",
        (array.shape[0] // rows,),
        [(array, block, lambda n: (n, 0))],
        [(array.shape, array.dtype, block, lambda n: (n, 0))],
        [],
        1,
        after,
    )[0]


def exchange(array, axis, size, offset):
    return lax.ppermute(array, axis, [(n, n ^ offset) for n in range(size)])


def add_kernel(*refs):
    total = refs[0][...].astype(F32)
    for ref in refs[1:-1]:
        total += ref[...].astype(F32)
    refs[-1][...] = total.astype(BF16)


def add(arrays, rows, after=(), width=None, us=None):
    width = width or arrays[0][0].shape[1]
    tile = 128

    def place(row, column):
        return lambda n: (n + row // tile, column // width)

    return call(
        add_kernel,
        "add",
        (rows // tile,),
        [(array, (tile, width), place(row, column)) for array, row, column in arrays],
        [((rows, width), BF16, (tile, width), lambda n: (n, 0))],
        [],
        us or 1.5e-6 * rows * width,
        after,
    )[0]


def add_halves_kernel(first, second, left, right):
    total = (first[...].astype(F32) + second[...].astype(F32)).astype(BF16)
    half = total.shape[1] // 2
    left[...] = total[:, :half]
    right[...] = total[:, half:]


def add_halves(first, second, rows, after=()):
    width = first.shape[1]
    tile = 128
    block = (tile, width)
    half = ((rows, width // 2), BF16, (tile, width // 2), lambda n: (n, 0))
    return call(
        add_halves_kernel,
        "add_halves",
        (rows // tile,),
        [(first, block, lambda n: (n, 0)), (second, block, lambda n: (n, 0))],
        [half, half],
        [],
        1.5e-6 * rows * width,
        after,
    )


def result_kernel(own, other, hidden, out):
    out[...] = (hidden[...] + (own[...].astype(F32) + other[...].astype(F32))).astype(BF16)


def result_rows(number, count, own, other, hidden, into, after=()):
    span, model = hidden.shape
    tile = min(128, span)
    block = (tile, model)
    return call(
        result_kernel,
        "result",
        (span // tile,),
        [(array, block, lambda n: (n, 0)) for array in (own, other, hidden)],
        [((count, span, model), BF16, (None, *block), lambda n: (number, n, 0))],
        [],
        1.5e-6 * span * model,
        after,
        None,
        into,
    )[0]


def input_kernel(tokens, gain, grads, *refs):
    out = refs[-1]
    pieces = [
        own[...].astype(F32) + other[...].astype(F32)
        for own, other in zip(refs[:-1:2], refs[1:-1:2])
    ]
    total = pieces[0] if len(pieces) == 1 else jnp.concatenate(pieces, axis=1)
    normal, std = row_norm(tokens[...].astype(F32))
    part = total * gain[...]
    first = std * (
        part
        - jnp.mean(part, axis=-1, keepdims=True)
        - normal * jnp.mean(part * normal, axis=-1, keepdims=True)
    )
    out[...] = (grads[...] + first).astype(BF16)


def input_rows(number, count, tokens, terms, gain, grads, into, after=()):
    span, model = grads.shape
    tile = min(128, span)
    block = (tile, model)
    by_row = lambda n: (n, 0)
    below = number * (span // tile)
    sums = [array for pair in terms for array in pair]
    return call(
        input_kernel,
        "input_grad",
        (span // tile,),
        [
            (tokens, block, lambda n: (n + below, 0)),
            (gain, (1, model), None),
            (grads, block, by_row),
        ]
        + [(array, (tile, array.shape[1]), by_row) for array in sums],
        [((count, span, model), BF16, (None, *block), lambda n: (number, n, 0))],
        [],
        2e-6 * span * model,
        after,
        None,
        into,
    )[0]


class ScatterSum:
    def __init__(self, parts, groups, z_first=False):
        away, self.kept = parts
        self.groups, self.z_first = groups, z_first
        self.got = exchange(away, "seq", groups, 1)

    def mates(self, after=()):
        rows = self.kept.shape[0]
        pair = [(self.kept, 0, 0), (self.got, 0, 0)]
        if self.z_first:
            near = add(pair, rows, after)
            self.rows = lax.psum_scatter(near, "dp", scatter_dimension=0, tiled=True)
        else:
            near = add(pair, rows // 2, after)
            self.far = exchange(near, "seq", self.groups, 2)
        return near

    def own(self, after=(), us=None):
        half = self.kept.shape[0] // 2
        pieces = [(self.kept, half, 0), (self.got, half, 0), (self.far, 0, 0)]
        return add(pieces, half, after, None, us)

    def chips(self, after=(), us=None):
        if self.z_first:
            half = self.rows.shape[0] // 2
            far = exchange(self.rows[:half], "seq", self.groups, 2)
            self.out = self.rows[half:].astype(F32) + far.astype(F32)
            return self.out
        own = self.own(after, us)
        self.out = lax.psum_scatter(own, "dp", scatter_dimension=0, tiled=True).astype(F32)
        return own


def mp_sum(low, units):
    if units != 2:
        return lax.psum(low, "mp"), jnp.zeros_like(low)
    return low, exchange(low, "mp", 2, 1)


def mp_rows(sums, units):
    if units != 2:
        return lax.psum(sums, "mp"), jnp.zeros_like(sums)
    return sums, exchange(sums, "mp", 2, 1)


def axis_sum(array, axis, size):
    offset = 1
    while offset < size:
        array = array + exchange(array, axis, size, offset)
        offset *= 2
    return array


def in_order(pieces, place):
    stacked = jnp.stack(pieces)
    return [
        lax.dynamic_index_in_dim(stacked, jnp.bitwise_xor(place, n), 0, False)
        for n in range(len(pieces))
    ]


def pass_round(pieces, groups):
    return [pieces[0]] + [exchange(pieces[n], "seq", groups, n) for n in range(1, groups)]


def xpos_tables(count, lanes):
    positions = jnp.arange(count, dtype=F32)
    pair_index = jnp.arange(HALF, dtype=F32)
    frequency = 1.0 / 10000.0 ** (2.0 * pair_index / HEAD_DIM)
    angles = positions[:, None] * frequency[None, :]
    base_ratio = (2.0 * pair_index + 0.4 * HEAD_DIM) / (1.4 * HEAD_DIM)
    growth = base_ratio[None, :] ** ((positions[:, None] - count // 2) / XPOS_BASE)
    cosine, sine = jnp.cos(angles), jnp.sin(angles)
    tables = []
    for factor in (growth, 1.0 / growth):
        tables.append(jnp.tile(cosine * factor, (1, lanes // HALF)))
        tables.append(
            jnp.tile(jnp.concatenate([-sine * factor, sine * factor], axis=1), (1, lanes // HEAD_DIM))
        )
    return tables


def body(
    devices,
    groups,
    units,
    tokens,
    lengths,
    qkv_weight,
    out_weight,
    in_weight,
    down_weight,
    gain_in,
    gain_attn,
    gain_mid,
    gain_ffn,
    out_grad,
):
    sequences, span, model = tokens.shape
    each = range(sequences)
    data = ("dp", "seq")
    shards = devices * groups
    place = lax.axis_index("seq").astype(jnp.int32)
    local_width = qkv_weight.shape[2]
    heads_here = local_width // HEAD_DIM
    ffn_width = in_weight.shape[1]
    share = local_width // groups

    blocks = []
    for s in each:
        far = exchange(tokens[s], "seq", groups, 2)
        blocks.append([tokens[s], exchange(tokens[s], "seq", groups, 1), far])
    blocks[0].append(exchange(blocks[0][2], "seq", groups, 1))

    number = lax.axis_index("dp") * groups + place
    sizes = [gain_in.size, gain_mid.size, gain_attn.size, gain_ffn.size]
    cuts = [sum(sizes[:n]) for n in range(5)]
    chunk = qkv_weight.shape[1]
    by_device = qkv_weight.reshape(3, chunk, groups, share).transpose(2, 1, 0, 3)
    by_device = by_device.reshape(groups, chunk, 3 * share)
    flat = jnp.concatenate([gain_in, gain_mid, gain_attn.reshape(-1), gain_ffn.reshape(-1)])
    flat = jnp.pad(flat, (0, 16 * 3 * share - cuts[4])).reshape(16, 3 * share)
    pieces = [
        jnp.concatenate(
            [
                lax.dynamic_index_in_dim(by_device, jnp.bitwise_xor(place, n), 0, False),
                flat,
            ]
        )
        for n in range(groups)
    ]
    pieces = in_order(pass_round(pieces, groups), place)
    rows = jnp.concatenate([piece[:chunk] for piece in pieces], axis=0)
    heads_weight = lax.all_gather(rows, "dp", axis=0, tiled=True)

    flat = jnp.stack([piece[chunk:].reshape(-1)[: cuts[4]] for piece in pieces]).reshape(1, -1)
    row = lax.broadcasted_iota(jnp.int32, (devices, 1), 0)
    all_gains = jnp.where(row == lax.axis_index("dp"), flat, 0).astype(F32)
    all_gains = axis_sum(all_gains, "dp", devices).reshape(shards, cuts[4])
    pieces = [all_gains[:, cuts[n] : cuts[n + 1]] for n in range(4)]
    gain_one, gain_three = pieces[0].reshape(1, -1), pieces[1].reshape(1, -1)
    gain_two = pieces[2].reshape(shards, heads_here, -1).transpose(1, 0, 2).reshape(1, -1)
    gain_four = (
        pieces[3].reshape(shards, ffn_width // HEAD_DIM, -1).transpose(1, 0, 2).reshape(1, -1)
    )

    near_full = lax.all_gather(
        pack(in_weight, out_weight, [all_gains, blocks[0][2]]), data, axis=0, tiled=True
    )
    down_full = lax.all_gather(down_weight, data, axis=1, tiled=True)

    count = span * groups
    tables = xpos_tables(count, min(128, share))
    spot = place.reshape(1)
    metas = [jnp.stack([lengths[s], place]) for s in each]
    full_units = ffn_width * units

    first_low, projected = [], []
    mixed, logs, attended, att_sums, inner, branch = [], [], [], [], [], []
    last = ()
    for s in each:
        low, made = project(spot, blocks[s], gain_one, heads_weight, tables, last)
        first_low.append(low)
        projected.append(made)
        outs, log = attend(metas[s], made, groups)
        mixed.append(outs)
        logs.append(log)
        last = [log]
        if s == 0:
            far = relay(blocks[1][2], last)
            blocks[1].append(exchange(far, "seq", groups, 1))
            last = [far]
    passed = [pass_round(mixed[s], groups) for s in each]
    last = [*last, *passed[-1][1:]]
    for s in each:
        whole, sums = collect(spot, passed[s], last)
        attended.append(whole)
        att_sums.append(mp_rows(sums, units))
        last = [sums]
    last = [other for _, other in att_sums]
    for s in each:
        low, terms = out_branch(attended[s], *att_sums[s], gain_two, near_full, model, last)
        inner.append(low)
        branch.append(mp_sum(terms, units))
        last = [terms]

    flat_tokens = tokens.reshape(sequences * span, model)
    flat_grads = out_grad.reshape(sequences * span, model)
    hidden, third_low, active, slope, act_sums = [], [], [], [], []
    for s in each:
        made = widen(s, flat_tokens, *branch[s], gain_three, near_full, ffn_width, last)
        hidden.append(made[0])
        third_low.append(made[1])
        active.append(made[2])
        slope.append(made[3])
        act_sums.append(mp_rows(made[4], units))
        last = [made[4]]

    own_sums, other_sums = [a for a, _ in act_sums], [b for _, b in act_sums]
    norm = (own_sums, other_sums, gain_four, full_units)
    down_parts = weight_grad(spot, [flat_grads], active, devices, groups, norm, False, last)
    down_sum = ScatterSum(down_parts, groups)
    last = [down_parts[0]]
    pre_low, third_terms = [], []
    scaled, back_sums, gain_four_grad = wide_back(
        flat_grads, down_full, active, own_sums, other_sums, gain_four, full_units, last
    )
    last = [back_sums[-1]]
    back_sums = [mp_rows(sums, units) for sums in back_sums]
    last = [down_sum.mates(last)] + [other for _, other in back_sums]
    for s in each:
        low, terms = pre_back(
            scaled[s], active[s], slope[s], *act_sums[s], *back_sums[s], near_full, full_units,
            last,
        )
        pre_low.append(low)
        third_terms.append(mp_sum(terms, units))
        last = [terms]

    def finish(s, after):
        terms = narrow(active[s], *act_sums[s], gain_four, down_full, full_units, after)
        return mp_sum(terms, units)

    def result(s, into, after):
        return result_rows(s, sequences, *wide_terms[s], hidden[s], into, after)

    gain_three_grad, gain_two_grad, gain_one_grad = 0.0, 0.0, 0.0
    order = jnp.bitwise_xor(place, jnp.array([3, 1, 2, 0], jnp.int32))
    first_sums = []
    grad_hidden, hidden_low, grads, projected_grads = [], [], [], []
    wide_terms = [finish(0, last)]
    last = [wide_terms[0][0]]
    for s in each:
        made = middle(
            s, flat_grads, *third_terms[s], hidden[s], gain_three, near_full, attended[s],
            *att_sums[s], gain_two, model, last
        )
        grad_hidden.append(made[0])
        hidden_low.append(made[1])
        gain_three_grad += made[4]
        gain_two_grad += made[5]
        if s == 0:
            in_parts = weight_grad(
                spot, third_low, pre_low, devices, groups, None, Z_FIRST, [made[3]]
            )
            in_sum = ScatterSum(in_parts, groups, Z_FIRST)
            last = [down_sum.chips([in_parts[0], third_terms[1][1]])]
        else:
            wide_terms.append(finish(s, [made[3]]))
            last = [in_sum.mates([wide_terms[s][0]])]
        parts = share_out(
            spot, made[2], attended[s], *att_sums[s], *mp_rows(made[3], units), model, groups,
            last,
        )
        last = [parts[0]]
        grads.append(pass_round(parts, groups))
    for s in each:
        made = attend_back(
            metas[s], projected[s], grads[s], mixed[s], logs[s], tables, last,
            BACK_WEIGHT if s == 0 else 1,
        )
        projected_grads.append(made)
        last = [made]
        if s == 0:
            out_parts = weight_grad(
                spot, hidden_low, inner, devices, groups, None, False, last + grads[1][1:]
            )
            out_sum = ScatterSum(out_parts, groups)
            results = result(0, None, [out_parts[0], down_sum.out])
            last = [results]
        else:
            first_terms = mp_sum(first_sums[0].own(last), units)
            last = [first_terms[0]]
        away, kept, gain_part = first_back(
            order, made, first_low[s], heads_weight, gain_one, groups, last
        )
        gain_one_grad += gain_part
        if s == 0:
            first_sums.append(ScatterSum((away, kept), groups))
            last = [first_sums[0].mates([away])]
            last = [out_sum.mates(last)]
        else:
            gain_one_sums = mp_rows(gain_one_grad, units)
            got = exchange(away, "seq", groups, 1)
            results = result(1, results, [away])
            last = [out_sum.chips([results], PAUSE)]
            near = add_halves(kept, got, span, last)
            last = [near[0], in_sum.rows]

    heads_part = heads_grad(first_low, projected_grads, last)
    heads_rows = lax.psum_scatter(heads_part, "dp", scatter_dimension=0, tiled=True)

    def input_grad(s, terms, into, after):
        return input_rows(
            s, sequences, flat_tokens, terms, gain_one, grad_hidden[s], into, after
        )

    gain_rows = jnp.concatenate(
        [
            (gain_one_sums[0] + gain_one_sums[1]).reshape(shards, -1),
            gain_three_grad.reshape(shards, -1),
            gain_two_grad.reshape(heads_here, shards, -1).transpose(1, 0, 2).reshape(shards, -1),
            gain_four_grad.reshape(ffn_width // HEAD_DIM, shards, -1)
            .transpose(1, 0, 2)
            .reshape(shards, -1),
        ],
        axis=1,
    )
    terms = []
    last = [heads_part, gain_one_sums[1]]
    for n, part in enumerate(near):
        far = exchange(part, "seq", groups, 2)
        column = n * (model // 2)
        own = add(
            [(kept, span, column), (got, span, column), (far, 0, 0)],
            span,
            last,
            model // 2,
            None if n == 0 else LONG_PAUSE,
        )
        terms.append(mp_sum(own, units))
        if n == 0:
            grad_input = input_grad(0, [first_terms], None, [own])
            gain_rows = relay(gain_rows, [grad_input])
            gain_rows = gain_rows + exchange(gain_rows, "seq", groups, 1)
            gain_rows = axis_sum(gain_rows, "dp", devices)
            last = [terms[0][1], gain_rows]
    gain_rows = gain_rows + exchange(gain_rows, "seq", groups, 2)
    in_sum.chips()
    pieces = [
        lax.dynamic_slice_in_dim(heads_rows, jnp.bitwise_xor(place, n) * chunk, chunk, 0)
        for n in range(groups)
    ]
    pieces = pass_round(pieces, groups)
    grad_input = input_grad(1, terms, grad_input, [gain_rows])
    rows = jnp.stack(in_order(pieces, place)).astype(F32)
    grad_qkv_w = rows.reshape(groups, chunk, 3, share).transpose(2, 1, 0, 3)
    grad_qkv_w = grad_qkv_w.reshape(3, chunk, local_width)
    gain_sums = lax.dynamic_index_in_dim(gain_rows, number, 0, False)
    one, three, two, four = [gain_sums[cuts[n] : cuts[n + 1]] for n in range(4)]
    return (
        results,
        grad_input,
        grad_qkv_w,
        out_sum.out.T,
        in_sum.out,
        down_sum.out.T,
        one,
        two.reshape(gain_attn.shape),
        three,
        four.reshape(gain_ffn.shape),
    )


def solution(mesh):
    sizes = mesh.shape
    data = ("dp", "seq")
    in_specs = (
        P("dp", "seq", None),
        P("dp"),
        P(None, data, "mp"),
        P("mp", data),
        P(data, "mp"),
        P("mp", data),
        P(data),
        P("mp", data),
        P(data),
        P("mp", data),
        P("dp", "seq", None),
    )
    out_specs = (
        P("dp", "seq", None),
        P("dp", "seq", None),
        P(None, data, "mp"),
        P("mp", data),
        P(data, "mp"),
        P("mp", data),
        P(data),
        P("mp", data),
        P(data),
        P("mp", data),
    )
    run = partial(body, sizes["dp"], sizes["seq"], sizes["mp"])
    return jax.shard_map(run, mesh=mesh, in_specs=in_specs, out_specs=out_specs, check_vma=False)
```

```python
from functools import partial

import jax
import jax.numpy as jnp
from jax import lax
from jax.experimental import pallas as pl
from jax.experimental.pallas import tpu as pltpu
from jax.sharding import PartitionSpec as P

HEAD_DIM = 64
HALF = HEAD_DIM // 2
XPOS_BASE = 512
EPSILON = 1e-05
NEGATIVE = -1e30
LOG2_E = 1.4426950408889634
SCORE_SCALE = 0.125
VMEM = 56 * 2**20
Z_FIRST = True
BF16 = jnp.bfloat16
KERNEL_RATE = 0.25e9
BACK_WEIGHT = 25
PAUSE = 300
LONG_PAUSE = 160


def lasting(us):
    return pl.CostEstimate(flops=int(us * KERNEL_RATE), bytes_accessed=0, transcendentals=0)


F32 = jnp.float32


def params(limit=VMEM):
    return pltpu.CompilerParams(vmem_limit_bytes=limit)


def dot(left, right, left_dim, right_dim):
    return lax.dot_general(
        left, right, (((left_dim,), (right_dim,)), ((), ())), preferred_element_type=F32
    )


def swap_halves(block):
    width = block.shape[1]
    if width % 128:
        pieces = []
        for start in range(0, width, HEAD_DIM):
            pieces += [block[:, start + HALF : start + HEAD_DIM], block[:, start : start + HALF]]
        return jnp.concatenate(pieces, axis=1)
    lane = lax.broadcasted_iota(jnp.int32, (block.shape[0], 128), 1) % HEAD_DIM
    pieces = []
    for start in range(0, width, 128):
        part = block[:, start : start + 128]
        pieces.append(
            jnp.where(lane < HALF, pltpu.roll(part, 128 - HALF, 1), pltpu.roll(part, HALF, 1))
        )
    return pieces[0] if len(pieces) == 1 else jnp.concatenate(pieces, axis=1)


def turned(block, cosine, sine, sign):
    lanes = cosine.shape[1]
    pieces = []
    for start in range(0, block.shape[1], lanes):
        part = block[:, start : start + lanes]
        pieces.append(part * cosine + sign * (swap_halves(part) * sine))
    return pieces[0] if len(pieces) == 1 else jnp.concatenate(pieces, axis=1)


def project_kernel(place, *refs, groups, share):
    blocks, refs = refs[:groups], refs[groups:]
    gain, weight, cos_q, sin_q, cos_k, sin_k, low, made, held = refs
    for offset, block in enumerate(blocks):

        @pl.when(pl.program_id(0) == offset)
        def _(block=block):
            held[...] = block[...]

    normal, _ = row_norm(held[...].astype(F32))
    rows = (normal * gain[...]).astype(BF16)
    low[...] = rows
    out = dot(rows, weight[...], 1, 0)
    queries = turned(out[:, :share], cos_q[...], sin_q[...], 1)
    keys = turned(out[:, share : 2 * share], cos_k[...], sin_k[...], 1)
    made[...] = jnp.concatenate([queries, keys, out[:, 2 * share :]], axis=1).astype(BF16)


def project(place, blocks, gain, weight, tables, after=()):
    groups = len(blocks)
    span, model = blocks[0].shape
    width = weight.shape[1]
    lanes = tables[0].shape[1]

    def here(n, p):
        return (jnp.bitwise_xor(n, p[0]), 0)

    return call(
        partial(project_kernel, groups=groups, share=width // 3),
        "project",
        (groups,),
        [(block, (span, model), None) for block in blocks]
        + [(gain, (1, model), None), (weight, (model, width), None)]
        + [(table, (span, lanes), here) for table in tables],
        [
            ((groups * span, model), BF16, (span, model), here),
            ((groups * span, width), BF16, (span, width), here),
        ],
        [pltpu.VMEM((span, model), BF16)],
        5e-9 * groups * span * model * width,
        after,
        place,
    )


def attend_kernel(meta, projected, *refs, groups, heads, block):
    outs, log_ref, vt_all, o_all = refs[:groups], refs[groups], refs[groups + 1], refs[groups + 2]
    step = pl.program_id(0)
    length, place = meta[0], meta[1]
    share = heads * HEAD_DIM
    span = outs[0].shape[0]

    def lanes(part, h):
        return slice(part * share + h * HEAD_DIM, part * share + (h + 1) * HEAD_DIM)

    @pl.when(step == 0)
    def _():
        for h in range(heads):
            vt_all[h] = projected[:, lanes(2, h)].T

    start = pl.multiple_of(step * block, block)
    queries = [projected[pl.ds(start, block), lanes(0, h)] for h in range(heads)]
    scale = SCORE_SCALE * LOG2_E

    def keys_block(index, carry, masked):
        at = pl.multiple_of(index * block, block)
        if masked:
            key_pos = at + lax.broadcasted_iota(jnp.int32, (block, block), 0)
            query_pos = start + lax.broadcasted_iota(jnp.int32, (block, block), 1)
            allowed = (key_pos <= query_pos) & (key_pos < length)
        new = []
        for h in range(heads):
            top, total, mixed = carry[h]
            scores = dot(projected[pl.ds(at, block), lanes(1, h)], queries[h], 1, 1)
            if masked:
                scores = jnp.where(allowed, scores, NEGATIVE)
            higher = jnp.maximum(top, jnp.max(scores, axis=0, keepdims=True))
            fade = jnp.exp2((top - higher) * scale)
            weights = jnp.exp2((scores - higher) * scale)
            total = total * fade + jnp.sum(weights, axis=0, keepdims=True)
            added = dot(vt_all[h, :, pl.ds(at, block)], weights.astype(BF16), 1, 0)
            new.append((higher, total, mixed * fade + added))
        return tuple(new)

    carry = tuple(
        (
            jnp.full((1, block), NEGATIVE, F32),
            jnp.zeros((1, block), F32),
            jnp.zeros((HEAD_DIM, block), F32),
        )
        for _ in range(heads)
    )
    whole = jnp.minimum(step, length // block)
    end = jnp.minimum(step + 1, (length + block - 1) // block)
    carry = lax.fori_loop(0, whole, lambda n, c: keys_block(n, c, False), carry)
    carry = lax.fori_loop(whole, end, lambda n, c: keys_block(n, c, True), carry)
    pieces = []
    for h in range(heads):
        top, total, mixed = carry[h]
        pieces.append((mixed / total).T)
        log_ref[h : h + 1, :] = top * scale + jnp.log2(total)
    o_all[pl.ds(start, block), :] = jnp.concatenate(pieces, axis=1).astype(BF16)

    @pl.when(step == pl.num_programs(0) - 1)
    def _():
        for offset, out in enumerate(outs):
            at = pl.multiple_of(jnp.bitwise_xor(place, offset) * span, span)
            out[...] = o_all[pl.ds(at, span), :]


def attend(meta, projected, groups, after=()):
    count, width = projected.shape
    share = width // 3
    span = count // groups
    heads = share // HEAD_DIM
    block = min(512, span)
    results = call(
        partial(attend_kernel, groups=groups, heads=heads, block=block),
        "attend",
        (count // block,),
        [(projected, (count, width), None)],
        [((span, share), BF16, (span, share), None)] * groups
        + [((heads, count), F32, (heads, block), lambda n, m: (0, n))],
        [pltpu.VMEM((heads, HEAD_DIM, count), BF16), pltpu.VMEM((count, share), BF16)],
        2.9e-8 * count * count * share,
        after,
        meta,
    )
    return results[:groups], results[groups]


def attend_back_kernel(meta, projected, *refs, groups, heads, block):
    grads, mixed = refs[:groups], refs[groups : 2 * groups]
    log_ref, cos_q, sin_q, cos_k, sin_k, out = refs[2 * groups : 2 * groups + 6]
    g_all, kt_all, dot_all, dqt_all, dk_sum, dv_sum = refs[2 * groups + 6 :]
    length, place = meta[0], meta[1]
    span = grads[0].shape[0]
    count = groups * span
    share = heads * HEAD_DIM
    scale = SCORE_SCALE * LOG2_E

    def lanes(part, h):
        return slice(part * share + h * HEAD_DIM, part * share + (h + 1) * HEAD_DIM)

    for h in range(heads):
        kt_all[h] = projected[:, lanes(1, h)].T
    for offset in range(groups):
        at = pl.multiple_of(jnp.bitwise_xor(place, offset) * span, span)
        g_all[pl.ds(at, span), :] = grads[offset][...]
        both = grads[offset][...].astype(F32) * mixed[offset][...].astype(F32)
        for h in range(heads):
            dot_all[h : h + 1, pl.ds(at, span)] = jnp.sum(
                both[:, lanes(0, h)].T, axis=0, keepdims=True
            )
    dqt_all[...] = jnp.zeros_like(dqt_all)
    query_blocks = count // block

    def keys_block(index, _):
        key_at = pl.multiple_of(index * block, block)
        keys = [projected[pl.ds(key_at, block), lanes(1, h)] for h in range(heads)]
        values = [projected[pl.ds(key_at, block), lanes(2, h)] for h in range(heads)]
        dk_sum[...] = jnp.zeros_like(dk_sum)
        dv_sum[...] = jnp.zeros_like(dv_sum)

        def query_block(index, _, masked):
            at = pl.multiple_of(index * block, block)
            if masked:
                key_pos = key_at + lax.broadcasted_iota(jnp.int32, (block, block), 0)
                query_pos = at + lax.broadcasted_iota(jnp.int32, (block, block), 1)
                allowed = (key_pos <= query_pos) & (key_pos < length)
            for h in range(heads):
                query = projected[pl.ds(at, block), lanes(0, h)]
                grad = g_all[pl.ds(at, block), lanes(0, h)]
                scores = dot(keys[h], query, 1, 1)
                weights = jnp.exp2(scores * scale - log_ref[h : h + 1, pl.ds(at, block)])
                if masked:
                    weights = jnp.where(allowed, weights, 0.0)
                grad_weights = dot(values[h], grad, 1, 1)
                grad_scores = weights * (grad_weights - dot_all[h : h + 1, pl.ds(at, block)])
                grad_scores = grad_scores.astype(BF16)
                dv_sum[h] += dot(weights.astype(BF16), grad, 1, 0)
                dk_sum[h] += dot(grad_scores, query, 1, 0)
                dqt_all[h, :, pl.ds(at, block)] += dot(
                    kt_all[h, :, pl.ds(key_at, block)], grad_scores, 1, 0
                )
            return 0

        crosses = key_at + block > length
        whole = jnp.where(crosses, query_blocks, index + 1)
        lax.fori_loop(index, whole, partial(query_block, masked=True), 0)
        lax.fori_loop(whole, query_blocks, partial(query_block, masked=False), 0)
        dk = jnp.concatenate([dk_sum[h] for h in range(heads)], axis=1) * SCORE_SCALE
        dv = jnp.concatenate([dv_sum[h] for h in range(heads)], axis=1)
        turn = (cos_k[pl.ds(key_at, block), :], sin_k[pl.ds(key_at, block), :])
        out[pl.ds(key_at, block), share : 2 * share] = turned(dk, *turn, -1).astype(BF16)
        out[pl.ds(key_at, block), 2 * share :] = dv.astype(BF16)
        return 0

    used = (length + block - 1) // block
    lax.fori_loop(0, used, keys_block, 0)

    def no_keys(index, _):
        at = pl.multiple_of(index * block, block)
        out[pl.ds(at, block), share:] = jnp.zeros((block, 2 * share), BF16)
        return 0

    lax.fori_loop(used, query_blocks, no_keys, 0)
    for index in range(query_blocks):
        at = slice(index * block, (index + 1) * block)
        dq = jnp.concatenate([dqt_all[h, :, at].T for h in range(heads)], axis=1) * SCORE_SCALE
        out[at, :share] = turned(dq, cos_q[at, :], sin_q[at, :], -1).astype(BF16)


def attend_back(meta, projected, grads, mixed, logs, tables, after=(), weight=1):
    groups = len(grads)
    count, width = projected.shape
    share = width // 3
    span = count // groups
    heads = share // HEAD_DIM
    block = min(512, span)
    return call(
        partial(attend_back_kernel, groups=groups, heads=heads, block=block),
        "attend_back",
        (1,),
        [(projected, (count, width), None)]
        + [(piece, (span, share), None) for piece in (*grads, *mixed)]
        + [(logs, logs.shape, None)]
        + [(table, table.shape, None) for table in tables],
        [((count, width), BF16, (count, width), None)],
        [
            pltpu.VMEM((count, share), BF16),
            pltpu.VMEM((heads, HEAD_DIM, count), BF16),
            pltpu.VMEM((heads, count), F32),
            pltpu.VMEM((heads, HEAD_DIM, count), F32),
            pltpu.VMEM((heads, block, HEAD_DIM), F32),
            pltpu.VMEM((heads, block, HEAD_DIM), F32),
        ],
        4.2e-8 * count * count * share * weight,
        after,
        meta,
    )[0]


def heads_grad_kernel(*refs, sequences):
    grads, lows, out = refs[:sequences], refs[sequences : 2 * sequences], refs[2 * sequences]
    total = dot(lows[0][...].T, grads[0][...], 1, 0)
    for s in range(1, sequences):
        total += dot(lows[s][...].T, grads[s][...], 1, 0)
    out[...] = total.astype(BF16)


def heads_grad(lows, grads, after=()):
    sequences = len(lows)
    count, model = lows[0].shape
    width = grads[0].shape[1]
    tile = 512
    return call(
        partial(heads_grad_kernel, sequences=sequences),
        "heads_grad",
        (model // tile,),
        [(grad, (count, width), None) for grad in grads]
        + [(low, (count, tile), lambda n: (0, n)) for low in lows],
        [((model, width), BF16, (tile, width), lambda n: (n, 0))],
        [],
        3e-9 * sequences * count * model * width,
        after,
    )[0]


def normed_rows(block, column_mean, column_std, gain):
    return (block.astype(F32) - column_mean) * column_std * gain


def moments(own, other, width):
    total = own + other
    mean = total[0:1] / width
    return mean, lax.rsqrt(total[1:2] / width - mean * mean + EPSILON)


def as_column(row):
    return jnp.broadcast_to(row, (128, row.shape[1])).T[:, 0:1]


def as_row(block):
    width = block.shape[1]
    part = block[:, 0:128]
    for start in range(128, width, 128):
        part = part + block[:, start : start + 128]
    return jnp.sum(part.T, axis=0, keepdims=True)


def weight_grad_kernel(place, *refs, sequences, devices, groups, chunk, offsets, normed, extra):
    lefts, refs = refs[:sequences], refs[sequences:]
    rights, refs = refs[:sequences], refs[sequences:]
    if normed:
        own_sums, other_sums, gain = refs[:sequences], refs[sequences : 2 * sequences], refs[2 * sequences]
        refs = refs[2 * sequences + 1 :]
    away, kept, turned_left = refs[extra : extra + 3]
    columns_ref = refs[extra + 3] if normed else None
    span = lefts[0].shape[0]

    @pl.when(pl.program_id(0) == 0)
    def _():
        row = 0
        for device, offset in offsets:
            target = jnp.bitwise_xor(place[0], offset)
            at = pl.multiple_of((device * groups + target) * chunk, chunk)
            for s in range(sequences):
                turned_left[row : row + chunk, s * span : (s + 1) * span] = lefts[s][
                    :, pl.ds(at, chunk)
                ].T
            row += chunk
        if normed:
            for s in range(sequences):
                mean, std = moments(own_sums[s][...], other_sums[s][...], normed)
                columns_ref[2 * s] = jnp.broadcast_to(as_column(mean), (span, 128))
                columns_ref[2 * s + 1] = jnp.broadcast_to(as_column(std), (span, 128))

    values = []
    for s in range(sequences):
        block = rights[s][...]
        if normed:
            block = normed_rows(
                block, columns_ref[2 * s, :, 0:1], columns_ref[2 * s + 1, :, 0:1], gain[...]
            ).astype(BF16)
        values.append(block)
    block = turned_left.shape[0] // 4
    parts = [away.at[:block], away.at[block:], kept.at[:block], kept.at[block:]]
    for n, part in enumerate(parts):
        rows = slice(n * block, (n + 1) * block)
        total = dot(turned_left[rows, :span], values[0], 1, 0)
        for s in range(1, sequences):
            total += dot(turned_left[rows, s * span : (s + 1) * span], values[s], 1, 0)
        part[...] = total.astype(BF16)


def weight_grad(place, lefts, rights, devices, groups, norm=None, z_first=False, after=()):
    sequences = len(rights)
    span = rights[0].shape[-2]
    width = lefts[0].shape[1]
    layers = rights[0].ndim == 3
    columns = rights[0].shape[0] * rights[0].shape[2] if layers else rights[0].shape[1]
    chunk = width // (devices * groups)
    tile = 512 if rights[0].shape[-1] % 512 == 0 else rights[0].shape[-1]
    half = width // 2
    if z_first:
        offsets = [(d, o) for core in (1, 0) for d in range(devices) for o in (2 + core, core)]
    else:
        offsets = [(d, o) for o in (3, 1, 2, 0) for d in range(devices)]
    if layers:
        tiles = rights[0].shape[2] // tile
        right_spec = pl.BlockSpec((None, span, tile), lambda n, p: (n // tiles, 0, n % tiles))
    else:
        right_spec = pl.BlockSpec((span, tile), lambda n, p: (0, n))
    if len(lefts) == sequences:
        in_specs = [pl.BlockSpec((span, width), lambda n, p: (0, 0))] * sequences
    else:
        lefts = lefts * sequences
        in_specs = [
            pl.BlockSpec((span, width), lambda n, p, s=s: (s, 0)) for s in range(sequences)
        ]
    in_specs += [right_spec] * sequences
    operands = [*lefts, *rights]
    scratch = [pltpu.VMEM((width, sequences * span), BF16)]
    full = 0
    if norm:
        own_sums, other_sums, gain, full = norm
        in_specs += [pl.BlockSpec((2, span), lambda n, p: (0, 0))] * (2 * sequences)
        in_specs += [pl.BlockSpec((1, tile), lambda n, p: (0, n))]
        operands += [*own_sums, *other_sums, gain]
        scratch += [pltpu.VMEM((2 * sequences, span, 128), F32)]
    in_specs += [pl.BlockSpec(memory_space=pl.ANY)] * len(after)
    return pl.pallas_call(
        partial(
            weight_grad_kernel,
            sequences=sequences,
            devices=devices,
            groups=groups,
            chunk=chunk,
            offsets=offsets,
            normed=full,
            extra=len(after),
        ),
        grid_spec=pltpu.PrefetchScalarGridSpec(
            num_scalar_prefetch=1,
            grid=(columns // tile,),
            in_specs=in_specs,
            out_specs=[pl.BlockSpec((half, tile), lambda n, p: (0, n))] * 2,
            scratch_shapes=scratch,
        ),
        out_shape=[jax.ShapeDtypeStruct((half, columns), BF16)] * 2,
        compiler_params=params(),
        cost_estimate=lasting(2.9e-9 * sequences * span * width * columns),
        name="weight_grad",
    )(place, *operands, *after)


def call(kernel, name, grid, ins, outs, scratch, us, after=(), scalars=None, into=None):
    into = into or []
    after = [*into, *after]
    extra = len(after)
    first = 0 if scalars is None else 1
    count = first + len(ins)

    def run(*refs):
        kernel(*refs[:count], *refs[count + extra :])

    def spec(block, index):
        if index is None:
            return pl.BlockSpec(block, lambda *_: (0,) * len(block))
        return pl.BlockSpec(block, index)

    return pl.pallas_call(
        run,
        grid_spec=pltpu.PrefetchScalarGridSpec(
            num_scalar_prefetch=first,
            grid=grid,
            in_specs=[spec(block, index) for _, block, index in ins]
            + [pl.BlockSpec(memory_space=pl.ANY)] * extra,
            out_specs=[spec(block, index) for _, _, block, index in outs],
            scratch_shapes=scratch,
        ),
        out_shape=[jax.ShapeDtypeStruct(shape, dtype) for shape, dtype, _, _ in outs],
        input_output_aliases={count + n: n for n in range(len(into))},
        compiler_params=params(),
        cost_estimate=lasting(us),
        name=name,
    )(*(() if scalars is None else (scalars,)), *[array for array, _, _ in ins], *after)


def pack_kernel(columns, rows, out):
    width = columns.shape[1]
    out[:, :width] = columns[...]
    out[:, width:] = rows[...].T


def pack(columns, rows, after=()):
    height, width = columns.shape
    total = width + rows.shape[0]
    return call(
        pack_kernel,
        "pack",
        (1,),
        [(columns, columns.shape, None), (rows, rows.shape, None)],
        [((height, total), BF16, (height, total), None)],
        [],
        1,
        after,
    )[0]


def collect_kernel(place, *refs, groups):
    pieces, (whole, sums) = refs[:groups], refs[groups:]
    share = pieces[0].shape[1]
    total, squares = 0.0, 0.0
    for offset, piece in enumerate(pieces):
        at = pl.multiple_of(jnp.bitwise_xor(place[0], offset) * share, share)
        block = piece[...]
        whole[:, pl.ds(at, share)] = block
        wide = block.astype(F32)
        total += as_row(wide)
        squares += as_row(wide * wide)
    sums[...] = jnp.concatenate([total, squares], axis=0)


def collect(place, pieces, after=()):
    groups = len(pieces)
    span, share = pieces[0].shape
    if share % 128:
        stacked = jnp.stack(pieces)
        whole = jnp.concatenate(
            [
                lax.dynamic_index_in_dim(stacked, jnp.bitwise_xor(place[0], n), 0, False)
                for n in range(groups)
            ],
            axis=1,
        )
        wide = whole.astype(F32)
        return whole, jnp.stack([jnp.sum(wide, axis=1), jnp.sum(wide * wide, axis=1)])
    width = groups * share
    return call(
        partial(collect_kernel, groups=groups),
        "collect",
        (1,),
        [(piece, (span, share), None) for piece in pieces],
        [((span, width), BF16, (span, width), None), ((2, span), F32, (2, span), None)],
        [],
        5e-6 * span * width,
        after,
        place,
    )


def out_kernel(mixed, own, other, gain, weight, inner, branch, *, full):
    mean, std = moments(own[...], other[...], full)
    low = normed_rows(mixed[...], as_column(mean), as_column(std), gain[...]).astype(BF16)
    inner[...] = low
    branch[...] = dot(low, weight[...], 1, 1).astype(BF16)


def out_branch(mixed, own, other, gain, near_full, full, parts=1, after=()):
    span, width = mixed.shape
    model = near_full.shape[0]
    place = near_full.shape[1] // width - 1
    rows = span // parts
    made = [None]
    branches = []
    for n in range(parts):
        made = call(
            partial(out_kernel, full=full),
            "out_branch",
            (1,),
            [
                (mixed, (rows, width), lambda _, n=n: (n, 0)),
                (own, (2, rows), lambda _, n=n: (0, n)),
                (other, (2, rows), lambda _, n=n: (0, n)),
                (gain, (1, width), None),
                (near_full, (model, width), lambda _: (0, place)),
            ],
            [
                ((span, width), BF16, (rows, width), lambda _, n=n: (n, 0)),
                ((rows, model), BF16, (rows, model), None),
            ],
            [],
            6e-9 * rows * width * model,
            after,
            None,
            made[:1] if n else None,
        )
        branches.append(made[1])
        after = [made[1]]
    return made[0], branches


def row_norm(block):
    mean = jnp.mean(block, axis=-1, keepdims=True)
    centered = block - mean
    std = lax.rsqrt(jnp.mean(centered * centered, axis=-1, keepdims=True) + EPSILON)
    return centered * std, std


def widen_kernel(tokens, own, other, gain, weight, hidden, low, active, slope, sums, total, squares):
    step = pl.program_id(0)

    @pl.when(step == 0)
    def _():
        block = tokens[...].astype(F32) + (own[...].astype(F32) + other[...].astype(F32))
        hidden[...] = block
        normal, _ = row_norm(block)
        low[...] = (normal * gain[...]).astype(BF16)
        total[...] = jnp.zeros_like(total)
        squares[...] = jnp.zeros_like(squares)

    pre = dot(low[...], weight[...], 1, 0)
    below = 0.5 + 0.5 * lax.erf(pre * 0.7071067811865476)
    value = pre * below
    active[...] = value.astype(BF16)
    slope[...] = (below + pre * (0.3989422804014327 * jnp.exp2(pre * pre * (-0.5 * LOG2_E)))).astype(
        BF16
    )
    part, square = total[...], squares[...]
    for start in range(0, value.shape[1], 128):
        piece = value[:, start : start + 128]
        part += piece
        square += piece * piece
    total[...] = part
    squares[...] = square

    @pl.when(step == pl.num_programs(0) - 1)
    def _():
        sums[...] = jnp.concatenate([as_row(total[...]), as_row(squares[...])], axis=0)


def widen(number, part, parts, tokens, own, other, gain, weight, units, into=None, after=()):
    rows, model = own.shape
    span = rows * parts
    tile = 512
    block = (rows, model)
    across = (rows, tile)
    here = lambda n: (part, 0)
    tiled = lambda n: (part, n)
    return call(
        widen_kernel,
        "widen",
        (units // tile,),
        [
            (tokens, block, lambda n: (number * parts + part, 0)),
            (own, block, None),
            (other, block, None),
            (gain, (1, model), None),
            (weight, (model, tile), lambda n: (0, n)),
        ],
        [
            ((span, model), F32, block, here),
            ((span, model), BF16, block, here),
            ((span, units), BF16, across, tiled),
            ((span, units), BF16, across, tiled),
            ((2, span), F32, (2, rows), lambda n: (0, part)),
        ],
        [pltpu.VMEM((rows, 128), F32)] * 2,
        5.4e-9 * rows * model * units,
        after,
        None,
        into,
    )


def narrow_kernel(gain, weight, *refs, sequences, full):
    active, refs = refs[:sequences], refs[sequences:]
    own, refs = refs[:sequences], refs[sequences:]
    other, refs = refs[:sequences], refs[sequences:]
    branch, total, columns, low = refs
    step = pl.program_id(0)
    span = active[0].shape[0]

    @pl.when(step == 0)
    def _():
        for s in range(sequences):
            mean, std = moments(own[s][...], other[s][...], full)
            columns[2 * s] = jnp.broadcast_to(as_column(mean), columns.shape[1:])
            columns[2 * s + 1] = jnp.broadcast_to(as_column(std), columns.shape[1:])
        total[...] = jnp.zeros_like(total)

    for s in range(sequences):
        low[s * span : (s + 1) * span, :] = normed_rows(
            active[s][...], columns[2 * s, :, 0:1], columns[2 * s + 1, :, 0:1], gain[...]
        ).astype(BF16)
    total[...] += dot(low[...], weight[...], 1, 0)

    @pl.when(step == pl.num_programs(0) - 1)
    def _():
        branch[...] = total[...].astype(BF16)


def narrow(active, own, other, gain, weight, full, after=()):
    sequences = len(active)
    span, units = active[0].shape
    model = weight.shape[1]
    tile = 512
    sums = (2, span)
    rows = sequences * span
    return call(
        partial(narrow_kernel, sequences=sequences, full=full),
        "narrow",
        (units // tile,),
        [
            (gain, (1, tile), lambda n: (0, n)),
            (weight, (tile, model), lambda n: (n, 0)),
        ]
        + [(array, (span, tile), lambda n: (0, n)) for array in active]
        + [(array, sums, None) for array in (*own, *other)],
        [((rows, model), BF16, (rows, model), None)],
        [
            pltpu.VMEM((rows, model), F32),
            pltpu.VMEM((2 * sequences, span, 128), F32),
            pltpu.VMEM((rows, tile), BF16),
        ],
        3.2e-9 * rows * model * units,
        after,
    )[0]


def wide_back_kernel(grads, weight, gain, *refs, sequences, full):
    active, refs = refs[:sequences], refs[sequences:]
    own, refs = refs[:sequences], refs[sequences:]
    other, refs = refs[:sequences], refs[sequences:]
    scaled, refs = refs[:sequences], refs[sequences:]
    sums, refs = refs[:sequences], refs[sequences:]
    gain_grad, columns, totals = refs
    step = pl.program_id(0)
    span = active[0].shape[0]

    @pl.when(step == 0)
    def _():
        for s in range(sequences):
            mean, std = moments(own[s][...], other[s][...], full)
            columns[2 * s] = jnp.broadcast_to(as_column(mean), columns.shape[1:])
            columns[2 * s + 1] = jnp.broadcast_to(as_column(std), columns.shape[1:])
        totals[...] = jnp.zeros_like(totals)

    every = dot(grads[...], weight[...], 1, 1)
    gain_part = 0.0
    for s in range(sequences):
        grad = every[s * span : (s + 1) * span]
        normal = (active[s][...].astype(F32) - columns[2 * s, :, 0:1]) * columns[2 * s + 1, :, 0:1]
        product = grad * normal
        gain_part += jnp.sum(product, axis=0, keepdims=True)
        grad = grad * gain[...]
        scaled[s][...] = grad.astype(BF16)
        product = product * gain[...]
        part, other_part = totals[2 * s], totals[2 * s + 1]
        for start in range(0, grad.shape[1], 128):
            part += grad[:, start : start + 128]
            other_part += product[:, start : start + 128]
        totals[2 * s] = part
        totals[2 * s + 1] = other_part
    gain_grad[...] = gain_part

    @pl.when(step == pl.num_programs(0) - 1)
    def _():
        for s in range(sequences):
            sums[s][...] = jnp.concatenate(
                [as_row(totals[2 * s]), as_row(totals[2 * s + 1])], axis=0
            )


def wide_back(grads, weight, active, own, other, gain, full, after=()):
    sequences = len(active)
    span, units = active[0].shape
    model = weight.shape[1]
    tile = 512
    sums = (2, span)
    across = (span, tile)
    tiled = lambda n: (0, n)
    made = call(
        partial(wide_back_kernel, sequences=sequences, full=full),
        "wide_back",
        (units // tile,),
        [
            (grads, (sequences * span, model), None),
            (weight, (tile, model), lambda n: (n, 0)),
            (gain, (1, tile), tiled),
        ]
        + [(array, across, tiled) for array in active]
        + [(array, sums, None) for array in (*own, *other)],
        [((span, units), BF16, across, tiled)] * sequences
        + [(sums, F32, sums, None)] * sequences
        + [((1, units), F32, (1, tile), tiled)],
        [pltpu.VMEM((2 * sequences, span, 128), F32)] * 2,
        3.5e-9 * sequences * span * model * units,
        after,
    )
    return made[:sequences], made[sequences : 2 * sequences], made[2 * sequences]


def pre_back_kernel(
    scaled, active, slope, own, other, own_back, other_back, weight, grads, branch, total, columns, *, full
):
    step = pl.program_id(0)

    @pl.when(step == 0)
    def _():
        mean, std = moments(own[...], other[...], full)
        back = (own_back[...] + other_back[...]) / full
        for n, row in enumerate((mean, std, back[0:1], back[1:2])):
            columns[n] = jnp.broadcast_to(as_column(row), columns.shape[1:])
        total[...] = jnp.zeros_like(total)

    std = columns[1, :, 0:1]
    normal = (active[...].astype(F32) - columns[0, :, 0:1]) * std
    grad = std * (scaled[...].astype(F32) - columns[2, :, 0:1] - normal * columns[3, :, 0:1])
    low = (grad * slope[...].astype(F32)).astype(BF16)
    grads[...] = low
    total[...] += dot(low, weight[...], 1, 1)

    @pl.when(step == pl.num_programs(0) - 1)
    def _():
        branch[...] = total[...].astype(BF16)


def pre_back(scaled, active, slope, own, other, own_back, other_back, weight, full, after=()):
    span, units = active.shape
    model = weight.shape[0]
    tile = 512
    sums = (2, span)
    across = (span, tile)
    tiled = lambda n: (0, n)
    return call(
        partial(pre_back_kernel, full=full),
        "pre_back",
        (units // tile,),
        [
            (scaled, across, tiled),
            (active, across, tiled),
            (slope, across, tiled),
            (own, sums, None),
            (other, sums, None),
            (own_back, sums, None),
            (other_back, sums, None),
            (weight, (model, tile), tiled),
        ],
        [((span, units), BF16, across, tiled), ((span, model), BF16, (span, model), None)],
        [pltpu.VMEM((span, model), F32), pltpu.VMEM((4, span, 128), F32)],
        4.6e-9 * span * model * units,
        after,
    )


def middle_kernel(
    grads, own, other, hidden, gain, weight, mixed, own_sums, other_sums, gain_attn,
    grad_hidden, low, scaled, sums, gain_grad, gain_attn_grad, *, full
):
    step = pl.program_id(0)

    @pl.when(step == 0)
    def _():
        gain_grad[...] = jnp.zeros_like(gain_grad)
        gain_attn_grad[...] = jnp.zeros_like(gain_attn_grad)

    normal, std = row_norm(hidden[...])
    grad = own[...].astype(F32) + other[...].astype(F32)
    gain_grad[...] += jnp.sum(grad * normal, axis=0, keepdims=True)
    part = grad * gain[...]
    back = std * (
        part
        - jnp.mean(part, axis=-1, keepdims=True)
        - normal * jnp.mean(part * normal, axis=-1, keepdims=True)
    )
    total = grads[...].astype(F32) + back
    grad_hidden[...] = total
    rows = total.astype(BF16)
    low[...] = rows
    inner = dot(rows, weight[...], 1, 0)
    mean, deviation = moments(own_sums[...], other_sums[...], full)
    normal = (mixed[...].astype(F32) - as_column(mean)) * as_column(deviation)
    gain_attn_grad[...] += jnp.sum(inner * normal, axis=0, keepdims=True)
    inner = inner * gain_attn[...]
    scaled[...] = inner
    sums[...] = jnp.concatenate([as_row(inner), as_row(inner * normal)], axis=0)


def middle(
    number, grads, own, other, hidden, gain, near_full, mixed, own_sums, other_sums, gain_attn, full, after=()
):
    span, model = hidden.shape
    width = mixed.shape[1]
    place = near_full.shape[1] // width - 1
    rows = min(256, span)
    below = number * (span // rows)
    by_row = lambda n: (n, 0)
    by_column = lambda n: (0, n)
    return call(
        partial(middle_kernel, full=full),
        "middle",
        (span // rows,),
        [
            (grads, (rows, model), lambda n: (n + below, 0)),
            (own, (rows, model), by_row),
            (other, (rows, model), by_row),
            (hidden, (rows, model), by_row),
            (gain, (1, model), None),
            (near_full, (model, width), lambda n: (0, place)),
            (mixed, (rows, width), by_row),
            (own_sums, (2, rows), by_column),
            (other_sums, (2, rows), by_column),
            (gain_attn, (1, width), None),
        ],
        [
            ((span, model), F32, (rows, model), by_row),
            ((span, model), BF16, (rows, model), by_row),
            ((span, width), F32, (rows, width), by_row),
            ((2, span), F32, (2, rows), by_column),
            ((1, model), F32, (1, model), None),
            ((1, width), F32, (1, width), None),
        ],
        [],
        1.2e-8 * span * width * model,
        after,
    )


def share_out_kernel(place, scaled, mixed, own, other, own_back, other_back, *outs, full):
    mean, std = moments(own[...], other[...], full)
    back = (own_back[...] + other_back[...]) / full
    mean, std, first, second = [as_column(row) for row in (mean, std, back[0:1], back[1:2])]
    share = outs[0].shape[1]
    for offset, out in enumerate(outs):
        at = pl.multiple_of(jnp.bitwise_xor(place[0], offset) * share, share)
        normal = (mixed[:, pl.ds(at, share)].astype(F32) - mean) * std
        out[...] = (std * (scaled[:, pl.ds(at, share)] - first - normal * second)).astype(BF16)


def share_out(place, scaled, mixed, own, other, own_back, other_back, full, groups, after=()):
    span, width = scaled.shape
    share = width // groups
    if share % 128:
        mean, std = moments(own, other, full)
        back = (own_back + other_back) / full
        mean, std, first, second = [row.reshape(-1, 1) for row in (mean, std, back[0], back[1])]
        normal = (mixed.astype(F32) - mean) * std
        grads = (std * (scaled - first - normal * second)).astype(BF16)
        return [
            lax.dynamic_slice_in_dim(grads, jnp.bitwise_xor(place[0], n) * share, share, 1)
            for n in range(groups)
        ]
    sums = (2, span)
    return call(
        partial(share_out_kernel, full=full),
        "share_out",
        (1,),
        [
            (scaled, (span, width), None),
            (mixed, (span, width), None),
            (own, sums, None),
            (other, sums, None),
            (own_back, sums, None),
            (other_back, sums, None),
        ],
        [((span, share), BF16, (span, share), None)] * groups,
        [],
        7.6e-6 * span * width,
        after,
        place,
    )


def first_back_kernel(order, grads, low, weight, gain, *refs):
    away, (kept, gain_grad, total) = refs[:4], refs[4:]
    step = pl.program_id(0)
    grad = dot(grads[...], weight[...], 1, 1)
    made = grad.astype(BF16)
    half = made.shape[1] // 2
    for n in range(2):

        @pl.when(step == n)
        def _(n=n):
            away[2 * n][...] = made[:, :half]
            away[2 * n + 1][...] = made[:, half:]

    @pl.when(step >= 2)
    def _():
        kept[...] = made

    @pl.when(step == 0)
    def _():
        total[...] = jnp.zeros_like(total)

    total[...] += jnp.sum(grad * low[...].astype(F32), axis=0, keepdims=True)

    @pl.when(step == pl.num_programs(0) - 1)
    def _():
        gain_grad[...] = total[...] / gain[...]


def first_back(order, grads, low, weight, gain, groups, after=()):
    count, width = grads.shape
    model = weight.shape[0]
    span = count // groups
    rows = (span, model)
    half = (span, model // 2)
    made = call(
        first_back_kernel,
        "first_back",
        (groups,),
        [
            (grads, (span, width), lambda n, p: (p[n], 0)),
            (low, rows, lambda n, p: (p[n], 0)),
            (weight, (model, width), None),
            (gain, (1, model), None),
        ],
        [(half, BF16, half, None)] * 4
        + [
            ((2 * span, model), BF16, rows, lambda n, p: (jnp.maximum(n - 2, 0), 0)),
            ((1, model), F32, (1, model), None),
        ],
        [pltpu.VMEM((1, model), F32)],
        4.5e-9 * count * model * width,
        after,
        order,
    )
    return made[:4], made[4], made[5]


def relay_kernel(array, out):
    out[...] = array[...]


def relay(array, after):
    rows = min(128, array.shape[0])
    block = (rows, array.shape[1])
    return call(
        relay_kernel,
        "relay",
        (array.shape[0] // rows,),
        [(array, block, lambda n: (n, 0))],
        [(array.shape, array.dtype, block, lambda n: (n, 0))],
        [],
        1,
        after,
    )[0]


def exchange(array, axis, size, offset):
    return lax.ppermute(array, axis, [(n, n ^ offset) for n in range(size)])


def add_kernel(*refs):
    total = refs[0][...].astype(F32)
    for ref in refs[1:-1]:
        total += ref[...].astype(F32)
    refs[-1][...] = total.astype(BF16)


def add(arrays, rows, after=(), width=None, us=None):
    width = width or arrays[0][0].shape[1]
    tile = 128

    def place(row, column):
        return lambda n: (n + row // tile, column // width)

    return call(
        add_kernel,
        "add",
        (rows // tile,),
        [(array, (tile, width), place(row, column)) for array, row, column in arrays],
        [((rows, width), BF16, (tile, width), lambda n: (n, 0))],
        [],
        us or 1.5e-6 * rows * width,
        after,
    )[0]


def add_halves_kernel(whole, left, right, *outs):
    half = left.shape[1]
    for n, (part, out) in enumerate(zip((left, right), outs)):
        total = whole[:, n * half : (n + 1) * half].astype(F32) + part[...].astype(F32)
        out[...] = total.astype(BF16)


def add_halves(whole, left, right, after=()):
    rows, width = left.shape
    tile = 128
    half = (tile, width)
    by_row = lambda n: (n, 0)
    return call(
        add_halves_kernel,
        "add_halves",
        (rows // tile,),
        [(whole, (tile, 2 * width), by_row), (left, half, by_row), (right, half, by_row)],
        [((rows, width), BF16, half, by_row)] * 2,
        [],
        3e-6 * rows * width,
        after,
    )


def join_halves_kernel(whole, *refs):
    pieces, out = refs[:-1], refs[-1]
    half = pieces[0].shape[1]
    for n in range(2):
        at = slice(n * half, (n + 1) * half)
        total = whole[:, at].astype(F32)
        for piece in pieces[n::2]:
            total += piece[...].astype(F32)
        out[:, at] = total.astype(BF16)


def join_halves(whole, got, far, after=()):
    rows, width = far[0].shape
    tile = 128
    half = (tile, width)
    below = rows // tile
    return call(
        join_halves_kernel,
        "join_halves",
        (rows // tile,),
        [(whole, (tile, 2 * width), lambda n: (n + below, 0))]
        + [(piece, half, lambda n: (n, 0)) for piece in (*got, *far)],
        [((rows, 2 * width), BF16, (tile, 2 * width), lambda n: (n, 0))],
        [],
        3e-6 * rows * width,
        after,
    )[0]


def result_kernel(own, other, *refs, tiles):
    hidden, out = refs[:-1], refs[-1]
    total = own[...].astype(F32) + other[...].astype(F32)
    for s, part in enumerate(hidden):

        @pl.when(pl.program_id(0) // tiles == s)
        def _(part=part):
            out[...] = (part[...] + total).astype(BF16)


def result_rows(own, other, hidden, after=(), us=None):
    span, model = hidden[0].shape
    rows = own.shape[0]
    tile = min(128, span)
    tiles = span // tile
    block = (tile, model)
    by_row = lambda n: (n, 0)
    return call(
        partial(result_kernel, tiles=tiles),
        "result",
        (rows // tile,),
        [(own, block, by_row), (other, block, by_row)]
        + [
            (array, block, lambda n, s=s: (jnp.clip(n - s * tiles, 0, tiles - 1), 0))
            for s, array in enumerate(hidden)
        ],
        [((rows, model), BF16, block, by_row)],
        [],
        us or 1.5e-6 * rows * model,
        after,
    )[0]


def input_kernel(tokens, gain, grads, *refs):
    out = refs[-1]
    pieces = [
        own[...].astype(F32) + other[...].astype(F32)
        for own, other in zip(refs[:-1:2], refs[1:-1:2])
    ]
    total = pieces[0] if len(pieces) == 1 else jnp.concatenate(pieces, axis=1)
    normal, std = row_norm(tokens[...].astype(F32))
    part = total * gain[...]
    first = std * (
        part
        - jnp.mean(part, axis=-1, keepdims=True)
        - normal * jnp.mean(part * normal, axis=-1, keepdims=True)
    )
    out[...] = (grads[...] + first).astype(BF16)


def input_rows(number, count, tokens, terms, gain, grads, into, after=()):
    span, model = grads.shape
    tile = min(128, span)
    block = (tile, model)
    by_row = lambda n: (n, 0)
    below = number * (span // tile)
    sums = [array for pair in terms for array in pair]
    return call(
        input_kernel,
        "input_grad",
        (span // tile,),
        [
            (tokens, block, lambda n: (n + below, 0)),
            (gain, (1, model), None),
            (grads, block, by_row),
        ]
        + [(array, (tile, array.shape[1]), by_row) for array in sums],
        [((count, span, model), BF16, (None, *block), lambda n: (number, n, 0))],
        [],
        2e-6 * span * model,
        after,
        None,
        None if into is None else [into],
    )[0]


class ScatterSum:
    def __init__(self, parts, groups, z_first=False):
        away, self.kept = parts
        self.groups, self.z_first = groups, z_first
        self.got = exchange(away, "seq", groups, 1)

    def mates(self, after=()):
        rows = self.kept.shape[0]
        pair = [(self.kept, 0, 0), (self.got, 0, 0)]
        if self.z_first:
            near = add(pair, rows, after)
            self.rows = lax.psum_scatter(near, "dp", scatter_dimension=0, tiled=True)
        else:
            near = add(pair, rows // 2, after)
            self.far = exchange(near, "seq", self.groups, 2)
        return near

    def own(self, after=(), us=None):
        half = self.kept.shape[0] // 2
        pieces = [(self.kept, half, 0), (self.got, half, 0), (self.far, 0, 0)]
        return add(pieces, half, after, None, us)

    def chips(self, after=(), us=None):
        if self.z_first:
            half = self.rows.shape[0] // 2
            far = exchange(self.rows[:half], "seq", self.groups, 2)
            self.out = self.rows[half:].astype(F32) + far.astype(F32)
            return self.out
        own = self.own(after, us)
        self.out = lax.psum_scatter(own, "dp", scatter_dimension=0, tiled=True).astype(F32)
        return own


def mp_sum(low, units):
    if units != 2:
        return lax.psum(low, "mp"), jnp.zeros_like(low)
    return low, exchange(low, "mp", 2, 1)


def mp_rows(sums, units):
    if units != 2:
        return lax.psum(sums, "mp"), jnp.zeros_like(sums)
    return sums, exchange(sums, "mp", 2, 1)


def axis_sum(array, axis, size):
    return sum([exchange(array, axis, size, offset) for offset in range(1, size)], array)


def in_order(pieces, place):
    stacked = jnp.stack(pieces)
    return [
        lax.dynamic_index_in_dim(stacked, jnp.bitwise_xor(place, n), 0, False)
        for n in range(len(pieces))
    ]


def pass_round(pieces, groups):
    return [pieces[0]] + [exchange(pieces[n], "seq", groups, n) for n in range(1, groups)]


def xpos_tables(count, lanes):
    positions = jnp.arange(count, dtype=F32)
    pair_index = jnp.arange(HALF, dtype=F32)
    frequency = 1.0 / 10000.0 ** (2.0 * pair_index / HEAD_DIM)
    angles = positions[:, None] * frequency[None, :]
    base_ratio = (2.0 * pair_index + 0.4 * HEAD_DIM) / (1.4 * HEAD_DIM)
    growth = base_ratio[None, :] ** ((positions[:, None] - count // 2) / XPOS_BASE)
    cosine, sine = jnp.cos(angles), jnp.sin(angles)
    tables = []
    for factor in (growth, 1.0 / growth):
        tables.append(jnp.tile(cosine * factor, (1, lanes // HALF)))
        tables.append(
            jnp.tile(jnp.concatenate([-sine * factor, sine * factor], axis=1), (1, lanes // HEAD_DIM))
        )
    return tables


def body(
    devices,
    groups,
    units,
    tokens,
    lengths,
    qkv_weight,
    out_weight,
    in_weight,
    down_weight,
    gain_in,
    gain_attn,
    gain_mid,
    gain_ffn,
    out_grad,
):
    sequences, span, model = tokens.shape
    each = range(sequences)
    data = ("dp", "seq")
    shards = devices * groups
    place = lax.axis_index("seq").astype(jnp.int32)
    local_width = qkv_weight.shape[2]
    heads_here = local_width // HEAD_DIM
    ffn_width = in_weight.shape[1]
    share = local_width // groups

    blocks = []
    for s in each:
        far = exchange(tokens[s], "seq", groups, 2)
        blocks.append([tokens[s], exchange(tokens[s], "seq", groups, 1), far])
    blocks[0].append(exchange(blocks[0][2], "seq", groups, 1))

    number = lax.axis_index("dp") * groups + place
    sizes = [gain_in.size, gain_mid.size, gain_attn.size, gain_ffn.size]
    cuts = [sum(sizes[:n]) for n in range(5)]
    chunk = qkv_weight.shape[1]
    by_device = qkv_weight.reshape(3, chunk, groups, share).transpose(2, 1, 0, 3)
    by_device = by_device.reshape(groups, chunk, 3 * share)
    flat = jnp.concatenate([gain_in, gain_mid, gain_attn.reshape(-1), gain_ffn.reshape(-1)])
    flat = jnp.pad(flat, (0, 16 * 3 * share - cuts[4])).reshape(16, 3 * share)
    pieces = [
        jnp.concatenate(
            [
                lax.dynamic_index_in_dim(by_device, jnp.bitwise_xor(place, n), 0, False),
                flat,
            ]
        )
        for n in range(groups)
    ]
    pieces = in_order(pass_round(pieces, groups), place)
    rows = jnp.concatenate([piece[:chunk] for piece in pieces], axis=0)
    heads_weight = lax.all_gather(rows, "dp", axis=0, tiled=True)

    flat = jnp.stack([piece[chunk:].reshape(-1)[: cuts[4]] for piece in pieces]).reshape(1, -1)
    row = lax.broadcasted_iota(jnp.int32, (devices, 1), 0)
    all_gains = jnp.where(row == lax.axis_index("dp"), flat, 0).astype(F32)
    all_gains = axis_sum(all_gains, "dp", devices).reshape(shards, cuts[4])
    pieces = [all_gains[:, cuts[n] : cuts[n + 1]] for n in range(4)]
    gain_one, gain_three = pieces[0].reshape(1, -1), pieces[1].reshape(1, -1)
    gain_two = pieces[2].reshape(shards, heads_here, -1).transpose(1, 0, 2).reshape(1, -1)
    gain_four = (
        pieces[3].reshape(shards, ffn_width // HEAD_DIM, -1).transpose(1, 0, 2).reshape(1, -1)
    )

    near_full = lax.all_gather(
        pack(in_weight, out_weight, [all_gains, blocks[0][2]]), data, axis=0, tiled=True
    )
    down_full = lax.all_gather(down_weight, data, axis=1, tiled=True)

    count = span * groups
    tables = xpos_tables(count, min(128, share))
    spot = place.reshape(1)
    metas = [jnp.stack([lengths[s], place]) for s in each]
    full_units = ffn_width * units

    first_low, projected = [], []
    mixed, logs, attended, att_sums, inner, branch = [], [], [], [], [], []
    last = ()
    for s in each:
        low, made = project(spot, blocks[s], gain_one, heads_weight, tables, last)
        first_low.append(low)
        projected.append(made)
        outs, log = attend(metas[s], made, groups)
        mixed.append(outs)
        logs.append(log)
        last = [log]
        if s == 0:
            far = relay(blocks[1][2], last)
            blocks[1].append(exchange(far, "seq", groups, 1))
            last = [far]
    passed = [pass_round(mixed[s], groups) for s in each]
    last = [*last, *passed[-1][1:]]
    for s in each:
        whole, sums = collect(spot, passed[s], last)
        attended.append(whole)
        att_sums.append(mp_rows(sums, units))
        last = [sums]
    last = [other for _, other in att_sums]
    for s in each:
        parts = 2 if s == sequences - 1 else 1
        low, terms = out_branch(attended[s], *att_sums[s], gain_two, near_full, model, parts, last)
        inner.append(low)
        branch.append([mp_sum(part, units) for part in terms])
        last = [terms[-1]]

    flat_tokens = tokens.reshape(sequences * span, model)
    flat_grads = out_grad.reshape(sequences * span, model)
    hidden, third_low, active, slope, act_sums = [], [], [], [], []
    for s in each:
        made = None
        for n, part in enumerate(branch[s]):
            made = widen(
                s, n, len(branch[s]), flat_tokens, *part, gain_three, near_full, ffn_width, made, last
            )
            last = [made[4]]
        hidden.append(made[0])
        third_low.append(made[1])
        active.append(made[2])
        slope.append(made[3])
        act_sums.append(mp_rows(made[4], units))
        last = [made[4]]

    own_sums, other_sums = [a for a, _ in act_sums], [b for _, b in act_sums]
    norm = (own_sums, other_sums, gain_four, full_units)
    down_parts = weight_grad(spot, [flat_grads], active, devices, groups, norm, False, last)
    down_sum = ScatterSum(down_parts, groups)
    last = [down_parts[0]]
    pre_low, third_terms = [], []
    scaled, back_sums, gain_four_grad = wide_back(
        flat_grads, down_full, active, own_sums, other_sums, gain_four, full_units, last
    )
    last = [back_sums[-1]]
    back_sums = [mp_rows(sums, units) for sums in back_sums]
    last = [down_sum.mates(last)] + [other for _, other in back_sums]
    for s in each:
        low, terms = pre_back(
            scaled[s], active[s], slope[s], *act_sums[s], *back_sums[s], near_full, full_units,
            last,
        )
        pre_low.append(low)
        third_terms.append(mp_sum(terms, units))
        last = [terms]

    gain_three_grad, gain_two_grad, gain_one_grad = 0.0, 0.0, 0.0
    order = jnp.bitwise_xor(place, jnp.array([3, 1, 2, 0], jnp.int32))
    grad_hidden, hidden_low, grads, projected_grads = [], [], [], []
    wide_terms = narrow(
        active, own_sums, other_sums, gain_four, down_full, full_units, last
    )
    last = [wide_terms]
    wide_terms = mp_sum(wide_terms, units)
    for s in each:
        made = middle(
            s, flat_grads, *third_terms[s], hidden[s], gain_three, near_full, attended[s],
            *att_sums[s], gain_two, model, last
        )
        grad_hidden.append(made[0])
        hidden_low.append(made[1])
        gain_three_grad += made[4]
        gain_two_grad += made[5]
        if s == 0:
            in_parts = weight_grad(
                spot, third_low, pre_low, devices, groups, None, Z_FIRST, [made[3]]
            )
            in_sum = ScatterSum(in_parts, groups, Z_FIRST)
            last = [down_sum.chips([in_parts[0], third_terms[1][1]])]
        else:
            last = [in_sum.mates([made[3]])]
        parts = share_out(
            spot, made[2], attended[s], *att_sums[s], *mp_rows(made[3], units), model, groups,
            last,
        )
        last = [parts[0]]
        grads.append(pass_round(parts, groups))
    for s in each:
        made = attend_back(
            metas[s], projected[s], grads[s], mixed[s], logs[s], tables, last,
            BACK_WEIGHT if s == 0 else 1,
        )
        projected_grads.append(made)
        last = [made]
        if s == 0:
            out_parts = weight_grad(
                spot, hidden_low, inner, devices, groups, None, False, last + grads[1][1:]
            )
            out_sum = ScatterSum(out_parts, groups)
            last = [out_sum.mates([out_parts[0], down_sum.out])]
        else:
            first_terms = mp_sum(join_halves(kept, got[2:], far, last), units)
            last = [first_terms[0]]
        away, kept, gain_part = first_back(
            order, made, first_low[s], heads_weight, gain_one, groups, last
        )
        gain_one_grad += gain_part
        got = [exchange(piece, "seq", groups, 1) for piece in away]
        if s == 0:
            last = [out_sum.chips([kept])]
            near = add_halves(kept, *got[:2], last)
            far = [exchange(piece, "seq", groups, 2) for piece in near]
            last = [near[0]]
        else:
            gain_one_sums = mp_rows(gain_one_grad, units)
            results = result_rows(*wide_terms, hidden, [kept], PAUSE)
            near = add_halves(kept, *got[:2], [results])
            last = [near[0], in_sum.rows]

    heads_part = heads_grad(first_low, projected_grads, last)
    heads_rows = lax.psum_scatter(heads_part, "dp", scatter_dimension=0, tiled=True)

    def input_grad(s, terms, into, after):
        return input_rows(
            s, sequences, flat_tokens, terms, gain_one, grad_hidden[s], into, after
        )

    gain_rows = jnp.concatenate(
        [
            (gain_one_sums[0] + gain_one_sums[1]).reshape(shards, -1),
            gain_three_grad.reshape(shards, -1),
            gain_two_grad.reshape(heads_here, shards, -1).transpose(1, 0, 2).reshape(shards, -1),
            gain_four_grad.reshape(ffn_width // HEAD_DIM, shards, -1)
            .transpose(1, 0, 2)
            .reshape(shards, -1),
        ],
        axis=1,
    )
    terms = []
    last = [heads_part, gain_one_sums[1]]
    for n, part in enumerate(near):
        far = exchange(part, "seq", groups, 2)
        column = n * (model // 2)
        own = add(
            [(kept, span, column), (got[2 + n], 0, 0), (far, 0, 0)],
            span,
            last,
            model // 2,
            None if n == 0 else LONG_PAUSE,
        )
        terms.append(mp_sum(own, units))
        if n == 0:
            gain_rows = relay(gain_rows, [own])
            grad_input = input_grad(0, [first_terms], None, [gain_rows])
            gain_rows = axis_sum(gain_rows, "dp", devices)
            last = [terms[0][1], gain_rows]
    gain_rows = axis_sum(relay(gain_rows, [own]), "seq", groups)
    in_sum.chips()
    pieces = [
        lax.dynamic_slice_in_dim(heads_rows, jnp.bitwise_xor(place, n) * chunk, chunk, 0)
        for n in range(groups)
    ]
    pieces = pass_round(pieces, groups)
    grad_input = input_grad(1, terms, grad_input, [gain_rows])
    rows = jnp.stack(in_order(pieces, place)).astype(F32)
    grad_qkv_w = rows.reshape(groups, chunk, 3, share).transpose(2, 1, 0, 3)
    grad_qkv_w = grad_qkv_w.reshape(3, chunk, local_width)
    gain_sums = lax.dynamic_index_in_dim(gain_rows, number, 0, False)
    one, three, two, four = [gain_sums[cuts[n] : cuts[n + 1]] for n in range(4)]
    return (
        results.reshape(sequences, span, model),
        grad_input,
        grad_qkv_w,
        out_sum.out.T,
        in_sum.out,
        down_sum.out.T,
        one,
        two.reshape(gain_attn.shape),
        three,
        four.reshape(gain_ffn.shape),
    )


def solution(mesh):
    sizes = mesh.shape
    data = ("dp", "seq")
    in_specs = (
        P("dp", "seq", None),
        P("dp"),
        P(None, data, "mp"),
        P("mp", data),
        P(data, "mp"),
        P("mp", data),
        P(data),
        P("mp", data),
        P(data),
        P("mp", data),
        P("dp", "seq", None),
    )
    out_specs = (
        P("dp", "seq", None),
        P("dp", "seq", None),
        P(None, data, "mp"),
        P("mp", data),
        P(data, "mp"),
        P("mp", data),
        P(data),
        P("mp", data),
        P(data),
        P("mp", data),
    )
    run = partial(body, sizes["dp"], sizes["seq"], sizes["mp"])
    return jax.shard_map(run, mesh=mesh, in_specs=in_specs, out_specs=out_specs, check_vma=False)
```

```python
from functools import partial

import jax
import jax.numpy as jnp
from jax import lax
from jax.experimental import pallas as pl
from jax.experimental.pallas import tpu as pltpu
from jax.sharding import PartitionSpec as P

HEAD_DIM = 64
HALF = HEAD_DIM // 2
XPOS_BASE = 512
EPSILON = 1e-05
NEGATIVE = -1e30
LOG2_E = 1.4426950408889634
SCORE_SCALE = 0.125
VMEM = 56 * 2**20
BF16 = jnp.bfloat16
KERNEL_RATE = 0.25e9
BACK_WEIGHT = 25
PAUSE = 300
MIDDLE_PAUSE = 450
LONG_PAUSE = 160


def lasting(us):
    return pl.CostEstimate(flops=int(us * KERNEL_RATE), bytes_accessed=0, transcendentals=0)


F32 = jnp.float32


def params(limit=VMEM):
    return pltpu.CompilerParams(vmem_limit_bytes=limit)


def dot(left, right, left_dim, right_dim):
    return lax.dot_general(
        left, right, (((left_dim,), (right_dim,)), ((), ())), preferred_element_type=F32
    )


def swap_halves(block):
    width = block.shape[1]
    if width % 128:
        pieces = []
        for start in range(0, width, HEAD_DIM):
            pieces += [block[:, start + HALF : start + HEAD_DIM], block[:, start : start + HALF]]
        return jnp.concatenate(pieces, axis=1)
    lane = lax.broadcasted_iota(jnp.int32, (block.shape[0], 128), 1) % HEAD_DIM
    pieces = []
    for start in range(0, width, 128):
        part = block[:, start : start + 128]
        pieces.append(
            jnp.where(lane < HALF, pltpu.roll(part, 128 - HALF, 1), pltpu.roll(part, HALF, 1))
        )
    return pieces[0] if len(pieces) == 1 else jnp.concatenate(pieces, axis=1)


def turned(block, cosine, sine, sign):
    lanes = cosine.shape[1]
    pieces = []
    for start in range(0, block.shape[1], lanes):
        part = block[:, start : start + lanes]
        pieces.append(part * cosine + sign * (swap_halves(part) * sine))
    return pieces[0] if len(pieces) == 1 else jnp.concatenate(pieces, axis=1)


def project_kernel(place, *refs, groups, share):
    blocks, refs = refs[:groups], refs[groups:]
    gain, weight, cos_q, sin_q, cos_k, sin_k, low, made, held = refs
    for offset, block in enumerate(blocks):

        @pl.when(pl.program_id(0) == offset)
        def _(block=block):
            held[...] = block[...]

    normal, _ = row_norm(held[...].astype(F32))
    rows = (normal * gain[...]).astype(BF16)
    low[...] = rows
    out = dot(rows, weight[...], 1, 0)
    queries = turned(out[:, :share], cos_q[...], sin_q[...], 1)
    keys = turned(out[:, share : 2 * share], cos_k[...], sin_k[...], 1)
    made[...] = jnp.concatenate([queries, keys, out[:, 2 * share :]], axis=1).astype(BF16)


def project(place, blocks, gain, weight, tables, after=()):
    groups = len(blocks)
    span, model = blocks[0].shape
    width = weight.shape[1]
    lanes = tables[0].shape[1]

    def here(n, p):
        return (jnp.bitwise_xor(n, p[0]), 0)

    return call(
        partial(project_kernel, groups=groups, share=width // 3),
        "project",
        (groups,),
        [(block, (span, model), None) for block in blocks]
        + [(gain, (1, model), None), (weight, (model, width), None)]
        + [(table, (span, lanes), here) for table in tables],
        [
            ((groups * span, model), BF16, (span, model), here),
            ((groups * span, width), BF16, (span, width), here),
        ],
        [pltpu.VMEM((span, model), BF16)],
        5e-9 * groups * span * model * width,
        after,
        place,
    )


def attend_kernel(meta, projected, *refs, groups, heads, block):
    outs, log_ref, vt_all, o_all = refs[:groups], refs[groups], refs[groups + 1], refs[groups + 2]
    step = pl.program_id(0)
    length, place = meta[0], meta[1]
    share = heads * HEAD_DIM
    span = outs[0].shape[0]

    def lanes(part, h):
        return slice(part * share + h * HEAD_DIM, part * share + (h + 1) * HEAD_DIM)

    @pl.when(step == 0)
    def _():
        for h in range(heads):
            vt_all[h] = projected[:, lanes(2, h)].T

    start = pl.multiple_of(step * block, block)
    queries = [projected[pl.ds(start, block), lanes(0, h)] for h in range(heads)]
    scale = SCORE_SCALE * LOG2_E

    def keys_block(index, carry, masked):
        at = pl.multiple_of(index * block, block)
        if masked:
            key_pos = at + lax.broadcasted_iota(jnp.int32, (block, block), 0)
            query_pos = start + lax.broadcasted_iota(jnp.int32, (block, block), 1)
            allowed = (key_pos <= query_pos) & (key_pos < length)
        new = []
        for h in range(heads):
            top, total, mixed = carry[h]
            scores = dot(projected[pl.ds(at, block), lanes(1, h)], queries[h], 1, 1)
            if masked:
                scores = jnp.where(allowed, scores, NEGATIVE)
            higher = jnp.maximum(top, jnp.max(scores, axis=0, keepdims=True))
            fade = jnp.exp2((top - higher) * scale)
            weights = jnp.exp2((scores - higher) * scale)
            total = total * fade + jnp.sum(weights, axis=0, keepdims=True)
            added = dot(vt_all[h, :, pl.ds(at, block)], weights.astype(BF16), 1, 0)
            new.append((higher, total, mixed * fade + added))
        return tuple(new)

    carry = tuple(
        (
            jnp.full((1, block), NEGATIVE, F32),
            jnp.zeros((1, block), F32),
            jnp.zeros((HEAD_DIM, block), F32),
        )
        for _ in range(heads)
    )
    whole = jnp.minimum(step, length // block)
    end = jnp.minimum(step + 1, (length + block - 1) // block)
    carry = lax.fori_loop(0, whole, lambda n, c: keys_block(n, c, False), carry)
    carry = lax.fori_loop(whole, end, lambda n, c: keys_block(n, c, True), carry)
    pieces = []
    for h in range(heads):
        top, total, mixed = carry[h]
        pieces.append((mixed / total).T)
        log_ref[h : h + 1, :] = top * scale + jnp.log2(total)
    o_all[pl.ds(start, block), :] = jnp.concatenate(pieces, axis=1).astype(BF16)

    @pl.when(step == pl.num_programs(0) - 1)
    def _():
        for offset, out in enumerate(outs):
            at = pl.multiple_of(jnp.bitwise_xor(place, offset) * span, span)
            out[...] = o_all[pl.ds(at, span), :]


def attend(meta, projected, groups, after=()):
    count, width = projected.shape
    share = width // 3
    span = count // groups
    heads = share // HEAD_DIM
    block = min(512, span)
    results = call(
        partial(attend_kernel, groups=groups, heads=heads, block=block),
        "attend",
        (count // block,),
        [(projected, (count, width), None)],
        [((span, share), BF16, (span, share), None)] * groups
        + [((heads, count), F32, (heads, block), lambda n, m: (0, n))],
        [pltpu.VMEM((heads, HEAD_DIM, count), BF16), pltpu.VMEM((count, share), BF16)],
        2.9e-8 * count * count * share,
        after,
        meta,
    )
    return results[:groups], results[groups]


def attend_back_kernel(meta, projected, *refs, groups, heads, block):
    grads, mixed = refs[:groups], refs[groups : 2 * groups]
    log_ref, cos_q, sin_q, cos_k, sin_k, out = refs[2 * groups : 2 * groups + 6]
    g_all, kt_all, dot_all, dqt_all, dk_sum, dv_sum = refs[2 * groups + 6 :]
    length, place = meta[0], meta[1]
    span = grads[0].shape[0]
    count = groups * span
    share = heads * HEAD_DIM
    scale = SCORE_SCALE * LOG2_E

    def lanes(part, h):
        return slice(part * share + h * HEAD_DIM, part * share + (h + 1) * HEAD_DIM)

    for h in range(heads):
        kt_all[h] = projected[:, lanes(1, h)].T
    for offset in range(groups):
        at = pl.multiple_of(jnp.bitwise_xor(place, offset) * span, span)
        g_all[pl.ds(at, span), :] = grads[offset][...]
        both = grads[offset][...].astype(F32) * mixed[offset][...].astype(F32)
        for h in range(heads):
            dot_all[h : h + 1, pl.ds(at, span)] = jnp.sum(
                both[:, lanes(0, h)].T, axis=0, keepdims=True
            )
    dqt_all[...] = jnp.zeros_like(dqt_all)
    query_blocks = count // block

    def keys_block(index, _):
        key_at = pl.multiple_of(index * block, block)
        keys = [projected[pl.ds(key_at, block), lanes(1, h)] for h in range(heads)]
        values = [projected[pl.ds(key_at, block), lanes(2, h)] for h in range(heads)]
        dk_sum[...] = jnp.zeros_like(dk_sum)
        dv_sum[...] = jnp.zeros_like(dv_sum)

        def query_block(index, _, masked):
            at = pl.multiple_of(index * block, block)
            if masked:
                key_pos = key_at + lax.broadcasted_iota(jnp.int32, (block, block), 0)
                query_pos = at + lax.broadcasted_iota(jnp.int32, (block, block), 1)
                allowed = (key_pos <= query_pos) & (key_pos < length)
            for h in range(heads):
                query = projected[pl.ds(at, block), lanes(0, h)]
                grad = g_all[pl.ds(at, block), lanes(0, h)]
                scores = dot(keys[h], query, 1, 1)
                weights = jnp.exp2(scores * scale - log_ref[h : h + 1, pl.ds(at, block)])
                if masked:
                    weights = jnp.where(allowed, weights, 0.0)
                grad_weights = dot(values[h], grad, 1, 1)
                grad_scores = weights * (grad_weights - dot_all[h : h + 1, pl.ds(at, block)])
                grad_scores = grad_scores.astype(BF16)
                dv_sum[h] += dot(weights.astype(BF16), grad, 1, 0)
                dk_sum[h] += dot(grad_scores, query, 1, 0)
                dqt_all[h, :, pl.ds(at, block)] += dot(
                    kt_all[h, :, pl.ds(key_at, block)], grad_scores, 1, 0
                )
            return 0

        crosses = key_at + block > length
        whole = jnp.where(crosses, query_blocks, index + 1)
        lax.fori_loop(index, whole, partial(query_block, masked=True), 0)
        lax.fori_loop(whole, query_blocks, partial(query_block, masked=False), 0)
        dk = jnp.concatenate([dk_sum[h] for h in range(heads)], axis=1) * SCORE_SCALE
        dv = jnp.concatenate([dv_sum[h] for h in range(heads)], axis=1)
        turn = (cos_k[pl.ds(key_at, block), :], sin_k[pl.ds(key_at, block), :])
        out[pl.ds(key_at, block), share : 2 * share] = turned(dk, *turn, -1).astype(BF16)
        out[pl.ds(key_at, block), 2 * share :] = dv.astype(BF16)
        return 0

    used = (length + block - 1) // block
    lax.fori_loop(0, used, keys_block, 0)

    def no_keys(index, _):
        at = pl.multiple_of(index * block, block)
        out[pl.ds(at, block), share:] = jnp.zeros((block, 2 * share), BF16)
        return 0

    lax.fori_loop(used, query_blocks, no_keys, 0)
    for index in range(query_blocks):
        at = slice(index * block, (index + 1) * block)
        dq = jnp.concatenate([dqt_all[h, :, at].T for h in range(heads)], axis=1) * SCORE_SCALE
        out[at, :share] = turned(dq, cos_q[at, :], sin_q[at, :], -1).astype(BF16)


def attend_back(meta, projected, grads, mixed, logs, tables, after=(), weight=1):
    groups = len(grads)
    count, width = projected.shape
    share = width // 3
    span = count // groups
    heads = share // HEAD_DIM
    block = min(512, span)
    return call(
        partial(attend_back_kernel, groups=groups, heads=heads, block=block),
        "attend_back",
        (1,),
        [(projected, (count, width), None)]
        + [(piece, (span, share), None) for piece in (*grads, *mixed)]
        + [(logs, logs.shape, None)]
        + [(table, table.shape, None) for table in tables],
        [((count, width), BF16, (count, width), None)],
        [
            pltpu.VMEM((count, share), BF16),
            pltpu.VMEM((heads, HEAD_DIM, count), BF16),
            pltpu.VMEM((heads, count), F32),
            pltpu.VMEM((heads, HEAD_DIM, count), F32),
            pltpu.VMEM((heads, block, HEAD_DIM), F32),
            pltpu.VMEM((heads, block, HEAD_DIM), F32),
        ],
        4.2e-8 * count * count * share * weight,
        after,
        meta,
    )[0]


def heads_grad_kernel(*refs, sequences):
    grads, lows, out = refs[:sequences], refs[sequences : 2 * sequences], refs[2 * sequences]
    total = dot(lows[0][...].T, grads[0][...], 1, 0)
    for s in range(1, sequences):
        total += dot(lows[s][...].T, grads[s][...], 1, 0)
    out[...] = total.astype(BF16)


def heads_grad(lows, grads, after=()):
    sequences = len(lows)
    count, model = lows[0].shape
    width = grads[0].shape[1]
    tile = 512
    return call(
        partial(heads_grad_kernel, sequences=sequences),
        "heads_grad",
        (model // tile,),
        [(grad, (count, width), None) for grad in grads]
        + [(low, (count, tile), lambda n: (0, n)) for low in lows],
        [((model, width), BF16, (tile, width), lambda n: (n, 0))],
        [],
        3e-9 * sequences * count * model * width,
        after,
    )[0]


def normed_rows(block, column_mean, column_std, gain):
    return (block.astype(F32) - column_mean) * column_std * gain


def moments(own, other, width):
    total = own + other
    mean = total[0:1] / width
    return mean, lax.rsqrt(total[1:2] / width - mean * mean + EPSILON)


def as_column(row):
    return jnp.broadcast_to(row, (128, row.shape[1])).T[:, 0:1]


def as_row(block):
    width = block.shape[1]
    part = block[:, 0:128]
    for start in range(128, width, 128):
        part = part + block[:, start : start + 128]
    return jnp.sum(part.T, axis=0, keepdims=True)


def weight_grad_kernel(place, *refs, sequences, devices, groups, chunk, offsets, normed, extra):
    lefts, refs = refs[:sequences], refs[sequences:]
    rights, refs = refs[:sequences], refs[sequences:]
    if normed:
        own_sums, other_sums, gain = refs[:sequences], refs[sequences : 2 * sequences], refs[2 * sequences]
        refs = refs[2 * sequences + 1 :]
    away, kept, turned_left = refs[extra : extra + 3]
    columns_ref = refs[extra + 3] if normed else None
    span = lefts[0].shape[0]

    @pl.when(pl.program_id(0) == 0)
    def _():
        row = 0
        for device, offset in offsets:
            target = jnp.bitwise_xor(place[0], offset)
            at = pl.multiple_of((device * groups + target) * chunk, chunk)
            for s in range(sequences):
                turned_left[row : row + chunk, s * span : (s + 1) * span] = lefts[s][
                    :, pl.ds(at, chunk)
                ].T
            row += chunk
        if normed:
            for s in range(sequences):
                mean, std = moments(own_sums[s][...], other_sums[s][...], normed)
                columns_ref[2 * s] = jnp.broadcast_to(as_column(mean), (span, 128))
                columns_ref[2 * s + 1] = jnp.broadcast_to(as_column(std), (span, 128))

    values = []
    for s in range(sequences):
        block = rights[s][...]
        if normed:
            block = normed_rows(
                block, columns_ref[2 * s, :, 0:1], columns_ref[2 * s + 1, :, 0:1], gain[...]
            ).astype(BF16)
        values.append(block)
    block = turned_left.shape[0] // 4
    parts = [away.at[:block], away.at[block:], kept.at[:block], kept.at[block:]]
    for n, part in enumerate(parts):
        rows = slice(n * block, (n + 1) * block)
        total = dot(turned_left[rows, :span], values[0], 1, 0)
        for s in range(1, sequences):
            total += dot(turned_left[rows, s * span : (s + 1) * span], values[s], 1, 0)
        part[...] = total.astype(BF16)


def weight_grad(place, lefts, rights, devices, groups, norm=None, z_first=False, after=()):
    sequences = len(rights)
    span = rights[0].shape[-2]
    width = lefts[0].shape[1]
    layers = rights[0].ndim == 3
    columns = rights[0].shape[0] * rights[0].shape[2] if layers else rights[0].shape[1]
    chunk = width // (devices * groups)
    tile = 512 if rights[0].shape[-1] % 512 == 0 else rights[0].shape[-1]
    half = width // 2
    if z_first:
        offsets = [(d, o) for core in (1, 0) for d in range(devices) for o in (2 + core, core)]
    else:
        offsets = [(d, o) for o in (3, 1, 2, 0) for d in range(devices)]
    if layers:
        tiles = rights[0].shape[2] // tile
        right_spec = pl.BlockSpec((None, span, tile), lambda n, p: (n // tiles, 0, n % tiles))
    else:
        right_spec = pl.BlockSpec((span, tile), lambda n, p: (0, n))
    if len(lefts) == sequences:
        in_specs = [pl.BlockSpec((span, width), lambda n, p: (0, 0))] * sequences
    else:
        lefts = lefts * sequences
        in_specs = [
            pl.BlockSpec((span, width), lambda n, p, s=s: (s, 0)) for s in range(sequences)
        ]
    in_specs += [right_spec] * sequences
    operands = [*lefts, *rights]
    scratch = [pltpu.VMEM((width, sequences * span), BF16)]
    full = 0
    if norm:
        own_sums, other_sums, gain, full = norm
        in_specs += [pl.BlockSpec((2, span), lambda n, p: (0, 0))] * (2 * sequences)
        in_specs += [pl.BlockSpec((1, tile), lambda n, p: (0, n))]
        operands += [*own_sums, *other_sums, gain]
        scratch += [pltpu.VMEM((2 * sequences, span, 128), F32)]
    in_specs += [pl.BlockSpec(memory_space=pl.ANY)] * len(after)
    return pl.pallas_call(
        partial(
            weight_grad_kernel,
            sequences=sequences,
            devices=devices,
            groups=groups,
            chunk=chunk,
            offsets=offsets,
            normed=full,
            extra=len(after),
        ),
        grid_spec=pltpu.PrefetchScalarGridSpec(
            num_scalar_prefetch=1,
            grid=(columns // tile,),
            in_specs=in_specs,
            out_specs=[pl.BlockSpec((half, tile), lambda n, p: (0, n))] * 2,
            scratch_shapes=scratch,
        ),
        out_shape=[jax.ShapeDtypeStruct((half, columns), BF16)] * 2,
        compiler_params=params(),
        cost_estimate=lasting(2.9e-9 * sequences * span * width * columns),
        name="weight_grad",
    )(place, *operands, *after)


def call(kernel, name, grid, ins, outs, scratch, us, after=(), scalars=None, into=None):
    into = into or []
    after = [*into, *after]
    extra = len(after)
    first = 0 if scalars is None else 1
    count = first + len(ins)

    def run(*refs):
        kernel(*refs[:count], *refs[count + extra :])

    def spec(block, index):
        if index is None:
            return pl.BlockSpec(block, lambda *_: (0,) * len(block))
        return pl.BlockSpec(block, index)

    return pl.pallas_call(
        run,
        grid_spec=pltpu.PrefetchScalarGridSpec(
            num_scalar_prefetch=first,
            grid=grid,
            in_specs=[spec(block, index) for _, block, index in ins]
            + [pl.BlockSpec(memory_space=pl.ANY)] * extra,
            out_specs=[spec(block, index) for _, _, block, index in outs],
            scratch_shapes=scratch,
        ),
        out_shape=[jax.ShapeDtypeStruct(shape, dtype) for shape, dtype, _, _ in outs],
        input_output_aliases={count + n: n for n in range(len(into))},
        compiler_params=params(),
        cost_estimate=lasting(us),
        name=name,
    )(*(() if scalars is None else (scalars,)), *[array for array, _, _ in ins], *after)


def pack_kernel(columns, rows, out):
    width = columns.shape[1]
    out[:, :width] = columns[...]
    out[:, width:] = rows[...].T


def pack(columns, rows, after=()):
    height, width = columns.shape
    total = width + rows.shape[0]
    return call(
        pack_kernel,
        "pack",
        (1,),
        [(columns, columns.shape, None), (rows, rows.shape, None)],
        [((height, total), BF16, (height, total), None)],
        [],
        1,
        after,
    )[0]


def collect_kernel(place, *refs, groups):
    pieces, (whole, sums) = refs[:groups], refs[groups:]
    share = pieces[0].shape[1]
    total, squares = 0.0, 0.0
    for offset, piece in enumerate(pieces):
        at = pl.multiple_of(jnp.bitwise_xor(place[0], offset) * share, share)
        block = piece[...]
        whole[:, pl.ds(at, share)] = block
        wide = block.astype(F32)
        total += as_row(wide)
        squares += as_row(wide * wide)
    sums[...] = jnp.concatenate([total, squares], axis=0)


def collect(place, pieces, after=()):
    groups = len(pieces)
    span, share = pieces[0].shape
    if share % 128:
        stacked = jnp.stack(pieces)
        whole = jnp.concatenate(
            [
                lax.dynamic_index_in_dim(stacked, jnp.bitwise_xor(place[0], n), 0, False)
                for n in range(groups)
            ],
            axis=1,
        )
        wide = whole.astype(F32)
        return whole, jnp.stack([jnp.sum(wide, axis=1), jnp.sum(wide * wide, axis=1)])
    width = groups * share
    return call(
        partial(collect_kernel, groups=groups),
        "collect",
        (1,),
        [(piece, (span, share), None) for piece in pieces],
        [((span, width), BF16, (span, width), None), ((2, span), F32, (2, span), None)],
        [],
        5e-6 * span * width,
        after,
        place,
    )


def out_kernel(mixed, own, other, gain, weight, inner, branch, *, full):
    mean, std = moments(own[...], other[...], full)
    low = normed_rows(mixed[...], as_column(mean), as_column(std), gain[...]).astype(BF16)
    inner[...] = low
    branch[...] = dot(low, weight[...], 1, 1).astype(BF16)


def out_branch(mixed, own, other, gain, near_full, full, parts=1, after=()):
    span, width = mixed.shape
    model = near_full.shape[0]
    place = near_full.shape[1] // width - 1
    rows = span // parts
    made = [None]
    branches = []
    for n in range(parts):
        made = call(
            partial(out_kernel, full=full),
            "out_branch",
            (1,),
            [
                (mixed, (rows, width), lambda _, n=n: (n, 0)),
                (own, (2, rows), lambda _, n=n: (0, n)),
                (other, (2, rows), lambda _, n=n: (0, n)),
                (gain, (1, width), None),
                (near_full, (model, width), lambda _: (0, place)),
            ],
            [
                ((span, width), BF16, (rows, width), lambda _, n=n: (n, 0)),
                ((rows, model), BF16, (rows, model), None),
            ],
            [],
            6e-9 * rows * width * model,
            after,
            None,
            made[:1] if n else None,
        )
        branches.append(made[1])
        after = [made[1]]
    return made[0], branches


def row_norm(block):
    mean = jnp.mean(block, axis=-1, keepdims=True)
    centered = block - mean
    std = lax.rsqrt(jnp.mean(centered * centered, axis=-1, keepdims=True) + EPSILON)
    return centered * std, std


def widen_kernel(tokens, own, other, gain, weight, hidden, low, active, slope, sums, total, squares):
    step = pl.program_id(0)

    @pl.when(step == 0)
    def _():
        block = tokens[...].astype(F32) + (own[...].astype(F32) + other[...].astype(F32))
        hidden[...] = block
        normal, _ = row_norm(block)
        low[...] = (normal * gain[...]).astype(BF16)
        total[...] = jnp.zeros_like(total)
        squares[...] = jnp.zeros_like(squares)

    pre = dot(low[...], weight[...], 1, 0)
    below = 0.5 + 0.5 * lax.erf(pre * 0.7071067811865476)
    value = pre * below
    active[...] = value.astype(BF16)
    slope[...] = (below + pre * (0.3989422804014327 * jnp.exp2(pre * pre * (-0.5 * LOG2_E)))).astype(
        BF16
    )
    part, square = total[...], squares[...]
    for start in range(0, value.shape[1], 128):
        piece = value[:, start : start + 128]
        part += piece
        square += piece * piece
    total[...] = part
    squares[...] = square

    @pl.when(step == pl.num_programs(0) - 1)
    def _():
        sums[...] = jnp.concatenate([as_row(total[...]), as_row(squares[...])], axis=0)


def widen(number, part, parts, tokens, own, other, gain, weight, units, into=None, after=()):
    rows, model = own.shape
    span = rows * parts
    tile = 512
    block = (rows, model)
    across = (rows, tile)
    here = lambda n: (part, 0)
    tiled = lambda n: (part, n)
    return call(
        widen_kernel,
        "widen",
        (units // tile,),
        [
            (tokens, block, lambda n: (number * parts + part, 0)),
            (own, block, None),
            (other, block, None),
            (gain, (1, model), None),
            (weight, (model, tile), lambda n: (0, n)),
        ],
        [
            ((span, model), F32, block, here),
            ((span, model), BF16, block, here),
            ((span, units), BF16, across, tiled),
            ((span, units), BF16, across, tiled),
            ((2, span), F32, (2, rows), lambda n: (0, part)),
        ],
        [pltpu.VMEM((rows, 128), F32)] * 2,
        5.4e-9 * rows * model * units,
        after,
        None,
        into,
    )


def narrow_kernel(gain, weight, *refs, sequences, full):
    active, refs = refs[:sequences], refs[sequences:]
    own, refs = refs[:sequences], refs[sequences:]
    other, refs = refs[:sequences], refs[sequences:]
    branch, total, columns, low = refs
    step = pl.program_id(0)
    span = active[0].shape[0]

    @pl.when(step == 0)
    def _():
        for s in range(sequences):
            mean, std = moments(own[s][...], other[s][...], full)
            columns[2 * s] = jnp.broadcast_to(as_column(mean), columns.shape[1:])
            columns[2 * s + 1] = jnp.broadcast_to(as_column(std), columns.shape[1:])
        total[...] = jnp.zeros_like(total)

    for s in range(sequences):
        low[s * span : (s + 1) * span, :] = normed_rows(
            active[s][...], columns[2 * s, :, 0:1], columns[2 * s + 1, :, 0:1], gain[...]
        ).astype(BF16)
    total[...] += dot(low[...], weight[...], 1, 0)

    @pl.when(step == pl.num_programs(0) - 1)
    def _():
        branch[...] = total[...].astype(BF16)


def narrow(active, own, other, gain, weight, full, after=()):
    sequences = len(active)
    span, units = active[0].shape
    model = weight.shape[1]
    tile = 512
    sums = (2, span)
    rows = sequences * span
    return call(
        partial(narrow_kernel, sequences=sequences, full=full),
        "narrow",
        (units // tile,),
        [
            (gain, (1, tile), lambda n: (0, n)),
            (weight, (tile, model), lambda n: (n, 0)),
        ]
        + [(array, (span, tile), lambda n: (0, n)) for array in active]
        + [(array, sums, None) for array in (*own, *other)],
        [((rows, model), BF16, (rows, model), None)],
        [
            pltpu.VMEM((rows, model), F32),
            pltpu.VMEM((2 * sequences, span, 128), F32),
            pltpu.VMEM((rows, tile), BF16),
        ],
        3.2e-9 * rows * model * units,
        after,
    )[0]


def wide_back_kernel(grads, weight, gain, *refs, sequences, full):
    active, refs = refs[:sequences], refs[sequences:]
    own, refs = refs[:sequences], refs[sequences:]
    other, refs = refs[:sequences], refs[sequences:]
    scaled, refs = refs[:sequences], refs[sequences:]
    sums, refs = refs[:sequences], refs[sequences:]
    gain_grad, columns, totals = refs
    step = pl.program_id(0)
    span = active[0].shape[0]

    @pl.when(step == 0)
    def _():
        for s in range(sequences):
            mean, std = moments(own[s][...], other[s][...], full)
            columns[2 * s] = jnp.broadcast_to(as_column(mean), columns.shape[1:])
            columns[2 * s + 1] = jnp.broadcast_to(as_column(std), columns.shape[1:])
        totals[...] = jnp.zeros_like(totals)

    every = dot(grads[...], weight[...], 1, 1)
    gain_part = 0.0
    for s in range(sequences):
        grad = every[s * span : (s + 1) * span]
        normal = (active[s][...].astype(F32) - columns[2 * s, :, 0:1]) * columns[2 * s + 1, :, 0:1]
        product = grad * normal
        gain_part += jnp.sum(product, axis=0, keepdims=True)
        grad = grad * gain[...]
        scaled[s][...] = grad.astype(BF16)
        product = product * gain[...]
        part, other_part = totals[2 * s], totals[2 * s + 1]
        for start in range(0, grad.shape[1], 128):
            part += grad[:, start : start + 128]
            other_part += product[:, start : start + 128]
        totals[2 * s] = part
        totals[2 * s + 1] = other_part
    gain_grad[...] = gain_part

    @pl.when(step == pl.num_programs(0) - 1)
    def _():
        for s in range(sequences):
            sums[s][...] = jnp.concatenate(
                [as_row(totals[2 * s]), as_row(totals[2 * s + 1])], axis=0
            )


def wide_back(grads, weight, active, own, other, gain, full, after=()):
    sequences = len(active)
    span, units = active[0].shape
    model = weight.shape[1]
    tile = 512
    sums = (2, span)
    across = (span, tile)
    tiled = lambda n: (0, n)
    made = call(
        partial(wide_back_kernel, sequences=sequences, full=full),
        "wide_back",
        (units // tile,),
        [
            (grads, (sequences * span, model), None),
            (weight, (tile, model), lambda n: (n, 0)),
            (gain, (1, tile), tiled),
        ]
        + [(array, across, tiled) for array in active]
        + [(array, sums, None) for array in (*own, *other)],
        [((span, units), BF16, across, tiled)] * sequences
        + [(sums, F32, sums, None)] * sequences
        + [((1, units), F32, (1, tile), tiled)],
        [pltpu.VMEM((2 * sequences, span, 128), F32)] * 2,
        3.5e-9 * sequences * span * model * units,
        after,
    )
    return made[:sequences], made[sequences : 2 * sequences], made[2 * sequences]


def pre_back_kernel(
    scaled, active, slope, own, other, own_back, other_back, weight, grads, branch, total, columns, *, full
):
    step = pl.program_id(0)

    @pl.when(step == 0)
    def _():
        mean, std = moments(own[...], other[...], full)
        back = (own_back[...] + other_back[...]) / full
        for n, row in enumerate((mean, std, back[0:1], back[1:2])):
            columns[n] = jnp.broadcast_to(as_column(row), columns.shape[1:])
        total[...] = jnp.zeros_like(total)

    std = columns[1, :, 0:1]
    normal = (active[...].astype(F32) - columns[0, :, 0:1]) * std
    grad = std * (scaled[...].astype(F32) - columns[2, :, 0:1] - normal * columns[3, :, 0:1])
    low = (grad * slope[...].astype(F32)).astype(BF16)
    grads[...] = low
    total[...] += dot(low, weight[...], 1, 1)

    @pl.when(step == pl.num_programs(0) - 1)
    def _():
        branch[...] = total[...].astype(BF16)


def pre_back(scaled, active, slope, own, other, own_back, other_back, weight, full, after=()):
    span, units = active.shape
    model = weight.shape[0]
    tile = 512
    sums = (2, span)
    across = (span, tile)
    tiled = lambda n: (0, n)
    return call(
        partial(pre_back_kernel, full=full),
        "pre_back",
        (units // tile,),
        [
            (scaled, across, tiled),
            (active, across, tiled),
            (slope, across, tiled),
            (own, sums, None),
            (other, sums, None),
            (own_back, sums, None),
            (other_back, sums, None),
            (weight, (model, tile), tiled),
        ],
        [((span, units), BF16, across, tiled), ((span, model), BF16, (span, model), None)],
        [pltpu.VMEM((span, model), F32), pltpu.VMEM((4, span, 128), F32)],
        4.6e-9 * span * model * units,
        after,
    )


def middle_kernel(
    grads, own, other, hidden, gain, weight, mixed, own_sums, other_sums, gain_attn,
    grad_hidden, low, scaled, sums, gain_grad, gain_attn_grad, *, full
):
    step = pl.program_id(0)

    @pl.when(step == 0)
    def _():
        gain_grad[...] = jnp.zeros_like(gain_grad)
        gain_attn_grad[...] = jnp.zeros_like(gain_attn_grad)

    normal, std = row_norm(hidden[...])
    grad = own[...].astype(F32) + other[...].astype(F32)
    gain_grad[...] += jnp.sum(grad * normal, axis=0, keepdims=True)
    part = grad * gain[...]
    back = std * (
        part
        - jnp.mean(part, axis=-1, keepdims=True)
        - normal * jnp.mean(part * normal, axis=-1, keepdims=True)
    )
    total = grads[...].astype(F32) + back
    grad_hidden[...] = total
    rows = total.astype(BF16)
    low[...] = rows
    inner = dot(rows, weight[...], 1, 0)
    mean, deviation = moments(own_sums[...], other_sums[...], full)
    normal = (mixed[...].astype(F32) - as_column(mean)) * as_column(deviation)
    gain_attn_grad[...] += jnp.sum(inner * normal, axis=0, keepdims=True)
    inner = inner * gain_attn[...]
    scaled[...] = inner
    sums[...] = jnp.concatenate([as_row(inner), as_row(inner * normal)], axis=0)


def middle(
    number, grads, own, other, hidden, gain, near_full, mixed, own_sums, other_sums, gain_attn, full, after=()
):
    span, model = hidden.shape
    width = mixed.shape[1]
    place = near_full.shape[1] // width - 1
    rows = min(256, span)
    below = number * (span // rows)
    by_row = lambda n: (n, 0)
    by_column = lambda n: (0, n)
    return call(
        partial(middle_kernel, full=full),
        "middle",
        (span // rows,),
        [
            (grads, (rows, model), lambda n: (n + below, 0)),
            (own, (rows, model), by_row),
            (other, (rows, model), by_row),
            (hidden, (rows, model), by_row),
            (gain, (1, model), None),
            (near_full, (model, width), lambda n: (0, place)),
            (mixed, (rows, width), by_row),
            (own_sums, (2, rows), by_column),
            (other_sums, (2, rows), by_column),
            (gain_attn, (1, width), None),
        ],
        [
            ((span, model), F32, (rows, model), by_row),
            ((span, model), BF16, (rows, model), by_row),
            ((span, width), F32, (rows, width), by_row),
            ((2, span), F32, (2, rows), by_column),
            ((1, model), F32, (1, model), None),
            ((1, width), F32, (1, width), None),
        ],
        [],
        1.2e-8 * span * width * model,
        after,
    )


def share_out_kernel(place, scaled, mixed, own, other, own_back, other_back, *outs, full):
    mean, std = moments(own[...], other[...], full)
    back = (own_back[...] + other_back[...]) / full
    mean, std, first, second = [as_column(row) for row in (mean, std, back[0:1], back[1:2])]
    share = outs[0].shape[1]
    for offset, out in enumerate(outs):
        at = pl.multiple_of(jnp.bitwise_xor(place[0], offset) * share, share)
        normal = (mixed[:, pl.ds(at, share)].astype(F32) - mean) * std
        out[...] = (std * (scaled[:, pl.ds(at, share)] - first - normal * second)).astype(BF16)


def share_out(
    place, scaled, mixed, own, other, own_back, other_back, full, groups, after=(), us=None
):
    span, width = scaled.shape
    share = width // groups
    if share % 128:
        mean, std = moments(own, other, full)
        back = (own_back + other_back) / full
        mean, std, first, second = [row.reshape(-1, 1) for row in (mean, std, back[0], back[1])]
        normal = (mixed.astype(F32) - mean) * std
        grads = (std * (scaled - first - normal * second)).astype(BF16)
        return [
            lax.dynamic_slice_in_dim(grads, jnp.bitwise_xor(place[0], n) * share, share, 1)
            for n in range(groups)
        ]
    sums = (2, span)
    return call(
        partial(share_out_kernel, full=full),
        "share_out",
        (1,),
        [
            (scaled, (span, width), None),
            (mixed, (span, width), None),
            (own, sums, None),
            (other, sums, None),
            (own_back, sums, None),
            (other_back, sums, None),
        ],
        [((span, share), BF16, (span, share), None)] * groups,
        [],
        us or 7.6e-6 * span * width,
        after,
        place,
    )


def first_back_kernel(order, grads, low, weight, gain, *refs):
    away, (kept, gain_grad, total) = refs[:4], refs[4:]
    step = pl.program_id(0)
    grad = dot(grads[...], weight[...], 1, 1)
    made = grad.astype(BF16)
    half = made.shape[1] // 2
    for n in range(2):

        @pl.when(step == n)
        def _(n=n):
            away[2 * n][...] = made[:, :half]
            away[2 * n + 1][...] = made[:, half:]

    @pl.when(step >= 2)
    def _():
        kept[...] = made

    @pl.when(step == 0)
    def _():
        total[...] = jnp.zeros_like(total)

    total[...] += jnp.sum(grad * low[...].astype(F32), axis=0, keepdims=True)

    @pl.when(step == pl.num_programs(0) - 1)
    def _():
        gain_grad[...] = total[...] / gain[...]


def first_back(order, grads, low, weight, gain, groups, after=()):
    count, width = grads.shape
    model = weight.shape[0]
    span = count // groups
    rows = (span, model)
    half = (span, model // 2)
    made = call(
        first_back_kernel,
        "first_back",
        (groups,),
        [
            (grads, (span, width), lambda n, p: (p[n], 0)),
            (low, rows, lambda n, p: (p[n], 0)),
            (weight, (model, width), None),
            (gain, (1, model), None),
        ],
        [(half, BF16, half, None)] * 4
        + [
            ((2 * span, model), BF16, rows, lambda n, p: (jnp.maximum(n - 2, 0), 0)),
            ((1, model), F32, (1, model), None),
        ],
        [pltpu.VMEM((1, model), F32)],
        4.5e-9 * count * model * width,
        after,
        order,
    )
    return made[:4], made[4], made[5]


def relay_kernel(array, out):
    out[...] = array[...]


def relay(array, after):
    rows = min(128, array.shape[0])
    block = (rows, array.shape[1])
    return call(
        relay_kernel,
        "relay",
        (array.shape[0] // rows,),
        [(array, block, lambda n: (n, 0))],
        [(array.shape, array.dtype, block, lambda n: (n, 0))],
        [],
        1,
        after,
    )[0]


def exchange(array, axis, size, offset):
    return lax.ppermute(array, axis, [(n, n ^ offset) for n in range(size)])


def add_kernel(*refs):
    total = refs[0][...].astype(F32)
    for ref in refs[1:-1]:
        total += ref[...].astype(F32)
    refs[-1][...] = total.astype(BF16)


def add(arrays, rows, after=(), width=None, us=None):
    width = width or arrays[0][0].shape[1]
    tile = 128

    def place(row, column):
        return lambda n: (n + row // tile, column // width)

    return call(
        add_kernel,
        "add",
        (rows // tile,),
        [(array, (tile, width), place(row, column)) for array, row, column in arrays],
        [((rows, width), BF16, (tile, width), lambda n: (n, 0))],
        [],
        us or 1.5e-6 * rows * width,
        after,
    )[0]


def add_halves_kernel(whole, left, right, *outs):
    half = left.shape[1]
    for n, (part, out) in enumerate(zip((left, right), outs)):
        total = whole[:, n * half : (n + 1) * half].astype(F32) + part[...].astype(F32)
        out[...] = total.astype(BF16)


def add_halves(whole, left, right, after=()):
    rows, width = left.shape
    tile = 128
    half = (tile, width)
    by_row = lambda n: (n, 0)
    return call(
        add_halves_kernel,
        "add_halves",
        (rows // tile,),
        [(whole, (tile, 2 * width), by_row), (left, half, by_row), (right, half, by_row)],
        [((rows, width), BF16, half, by_row)] * 2,
        [],
        3e-6 * rows * width,
        after,
    )


def join_halves_kernel(whole, *refs):
    pieces, out = refs[:-1], refs[-1]
    half = pieces[0].shape[1]
    for n in range(2):
        at = slice(n * half, (n + 1) * half)
        total = whole[:, at].astype(F32)
        for piece in pieces[n::2]:
            total += piece[...].astype(F32)
        out[:, at] = total.astype(BF16)


def join_halves(whole, got, far, after=()):
    rows, width = far[0].shape
    tile = 128
    half = (tile, width)
    below = rows // tile
    return call(
        join_halves_kernel,
        "join_halves",
        (rows // tile,),
        [(whole, (tile, 2 * width), lambda n: (n + below, 0))]
        + [(piece, half, lambda n: (n, 0)) for piece in (*got, *far)],
        [((rows, 2 * width), BF16, (tile, 2 * width), lambda n: (n, 0))],
        [],
        3e-6 * rows * width,
        after,
    )[0]


def result_kernel(own, other, *refs, tiles):
    hidden, out = refs[:-1], refs[-1]
    total = own[...].astype(F32) + other[...].astype(F32)
    for s, part in enumerate(hidden):

        @pl.when(pl.program_id(0) // tiles == s)
        def _(part=part):
            out[...] = (part[...] + total).astype(BF16)


def result_rows(own, other, hidden, after=(), us=None):
    span, model = hidden[0].shape
    rows = own.shape[0]
    tile = min(128, span)
    tiles = span // tile
    block = (tile, model)
    by_row = lambda n: (n, 0)
    return call(
        partial(result_kernel, tiles=tiles),
        "result",
        (rows // tile,),
        [(own, block, by_row), (other, block, by_row)]
        + [
            (array, block, lambda n, s=s: (jnp.clip(n - s * tiles, 0, tiles - 1), 0))
            for s, array in enumerate(hidden)
        ],
        [((rows, model), BF16, block, by_row)],
        [],
        us or 1.5e-6 * rows * model,
        after,
    )[0]


def input_kernel(tokens, gain, grads, *refs):
    out = refs[-1]
    pieces = [
        own[...].astype(F32) + other[...].astype(F32)
        for own, other in zip(refs[:-1:2], refs[1:-1:2])
    ]
    total = pieces[0] if len(pieces) == 1 else jnp.concatenate(pieces, axis=1)
    normal, std = row_norm(tokens[...].astype(F32))
    part = total * gain[...]
    first = std * (
        part
        - jnp.mean(part, axis=-1, keepdims=True)
        - normal * jnp.mean(part * normal, axis=-1, keepdims=True)
    )
    out[...] = (grads[...] + first).astype(BF16)


def input_rows(number, count, tokens, terms, gain, grads, into, after=()):
    span, model = grads.shape
    tile = min(128, span)
    block = (tile, model)
    by_row = lambda n: (n, 0)
    below = number * (span // tile)
    sums = [array for pair in terms for array in pair]
    return call(
        input_kernel,
        "input_grad",
        (span // tile,),
        [
            (tokens, block, lambda n: (n + below, 0)),
            (gain, (1, model), None),
            (grads, block, by_row),
        ]
        + [(array, (tile, array.shape[1]), by_row) for array in sums],
        [((count, span, model), BF16, (None, *block), lambda n: (number, n, 0))],
        [],
        2e-6 * span * model,
        after,
        None,
        None if into is None else [into],
    )[0]


class ScatterSum:
    def __init__(self, parts, groups, z_first=False):
        away, self.kept = parts
        self.groups, self.z_first = groups, z_first
        self.got = exchange(away, "seq", groups, 1)

    def mates(self, after=()):
        rows = self.kept.shape[0]
        pair = [(self.kept, 0, 0), (self.got, 0, 0)]
        if self.z_first:
            near = add(pair, rows, after)
            self.rows = lax.psum_scatter(near, "dp", scatter_dimension=0, tiled=True)
        else:
            near = add(pair, rows // 2, after)
            self.far = exchange(near, "seq", self.groups, 2)
        return near

    def own(self, after=(), us=None):
        half = self.kept.shape[0] // 2
        pieces = [(self.kept, half, 0), (self.got, half, 0), (self.far, 0, 0)]
        return add(pieces, half, after, None, us)

    def chips(self, after=(), us=None):
        if self.z_first:
            half = self.rows.shape[0] // 2
            far = exchange(self.rows[:half], "seq", self.groups, 2)
            self.out = self.rows[half:].astype(F32) + far.astype(F32)
            return self.out
        own = self.own(after, us)
        self.raw = lax.psum_scatter(own, "dp", scatter_dimension=0, tiled=True)
        self.out = self.raw.astype(F32)
        return own


def mp_sum(low, units):
    if units != 2:
        return lax.psum(low, "mp"), jnp.zeros_like(low)
    return low, exchange(low, "mp", 2, 1)


def mp_rows(sums, units):
    if units != 2:
        return lax.psum(sums, "mp"), jnp.zeros_like(sums)
    return sums, exchange(sums, "mp", 2, 1)


def axis_sum(array, axis, size):
    return sum([exchange(array, axis, size, offset) for offset in range(1, size)], array)


def in_order(pieces, place):
    stacked = jnp.stack(pieces)
    return [
        lax.dynamic_index_in_dim(stacked, jnp.bitwise_xor(place, n), 0, False)
        for n in range(len(pieces))
    ]


def pass_round(pieces, groups):
    return [pieces[0]] + [exchange(pieces[n], "seq", groups, n) for n in range(1, groups)]


def xpos_tables(count, lanes):
    positions = jnp.arange(count, dtype=F32)
    pair_index = jnp.arange(HALF, dtype=F32)
    frequency = 1.0 / 10000.0 ** (2.0 * pair_index / HEAD_DIM)
    angles = positions[:, None] * frequency[None, :]
    base_ratio = (2.0 * pair_index + 0.4 * HEAD_DIM) / (1.4 * HEAD_DIM)
    growth = base_ratio[None, :] ** ((positions[:, None] - count // 2) / XPOS_BASE)
    cosine, sine = jnp.cos(angles), jnp.sin(angles)
    tables = []
    for factor in (growth, 1.0 / growth):
        tables.append(jnp.tile(cosine * factor, (1, lanes // HALF)))
        tables.append(
            jnp.tile(jnp.concatenate([-sine * factor, sine * factor], axis=1), (1, lanes // HEAD_DIM))
        )
    return tables


def body(
    devices,
    groups,
    units,
    tokens,
    lengths,
    qkv_weight,
    out_weight,
    in_weight,
    down_weight,
    gain_in,
    gain_attn,
    gain_mid,
    gain_ffn,
    out_grad,
):
    sequences, span, model = tokens.shape
    each = range(sequences)
    data = ("dp", "seq")
    shards = devices * groups
    place = lax.axis_index("seq").astype(jnp.int32)
    local_width = qkv_weight.shape[2]
    heads_here = local_width // HEAD_DIM
    ffn_width = in_weight.shape[1]
    share = local_width // groups

    blocks = []
    for s in each:
        far = exchange(tokens[s], "seq", groups, 2)
        blocks.append([tokens[s], exchange(tokens[s], "seq", groups, 1), far])
    blocks[0].append(exchange(blocks[0][2], "seq", groups, 1))

    number = lax.axis_index("dp") * groups + place
    sizes = [gain_in.size, gain_mid.size, gain_attn.size, gain_ffn.size]
    cuts = [sum(sizes[:n]) for n in range(5)]
    chunk = qkv_weight.shape[1]
    by_device = qkv_weight.reshape(3, chunk, groups, share).transpose(2, 1, 0, 3)
    by_device = by_device.reshape(groups, chunk, 3 * share)
    flat = jnp.concatenate([gain_in, gain_mid, gain_attn.reshape(-1), gain_ffn.reshape(-1)])
    flat = jnp.pad(flat, (0, 16 * 3 * share - cuts[4])).reshape(16, 3 * share)
    pieces = [
        jnp.concatenate(
            [
                lax.dynamic_index_in_dim(by_device, jnp.bitwise_xor(place, n), 0, False),
                flat,
            ]
        )
        for n in range(groups)
    ]
    pieces = in_order(pass_round(pieces, groups), place)
    rows = jnp.concatenate([piece[:chunk] for piece in pieces], axis=0)
    rows = relay(rows, [blocks[s][0] for s in each])
    heads_weight = lax.all_gather(rows, "dp", axis=0, tiled=True)

    flat = jnp.stack([piece[chunk:].reshape(-1)[: cuts[4]] for piece in pieces]).reshape(1, -1)
    row = lax.broadcasted_iota(jnp.int32, (devices, 1), 0)
    all_gains = jnp.where(row == lax.axis_index("dp"), flat, 0).astype(F32)
    all_gains = axis_sum(all_gains, "dp", devices).reshape(shards, cuts[4])
    pieces = [all_gains[:, cuts[n] : cuts[n + 1]] for n in range(4)]
    gain_one, gain_three = pieces[0].reshape(1, -1), pieces[1].reshape(1, -1)
    gain_two = pieces[2].reshape(shards, heads_here, -1).transpose(1, 0, 2).reshape(1, -1)
    gain_four = (
        pieces[3].reshape(shards, ffn_width // HEAD_DIM, -1).transpose(1, 0, 2).reshape(1, -1)
    )

    near_full = lax.all_gather(
        pack(in_weight, out_weight, [all_gains, blocks[0][2]]), data, axis=0, tiled=True
    )
    down_full = lax.all_gather(down_weight, data, axis=1, tiled=True)

    count = span * groups
    tables = xpos_tables(count, min(128, share))
    spot = place.reshape(1)
    metas = [jnp.stack([lengths[s], place]) for s in each]
    full_units = ffn_width * units

    first_low, projected = [], []
    mixed, logs, attended, att_sums, inner, branch = [], [], [], [], [], []
    last = ()
    for s in each:
        low, made = project(spot, blocks[s], gain_one, heads_weight, tables, last)
        first_low.append(low)
        projected.append(made)
        outs, log = attend(metas[s], made, groups)
        mixed.append(outs)
        logs.append(log)
        last = [log]
        if s == 0:
            far = relay(blocks[1][2], last)
            blocks[1].append(exchange(far, "seq", groups, 1))
            last = [far]
    passed = [pass_round(mixed[s], groups) for s in each]
    last = [*last, *passed[-1][1:]]
    for s in each:
        whole, sums = collect(spot, passed[s], last)
        attended.append(whole)
        att_sums.append(mp_rows(sums, units))
        last = [sums]
    last = [other for _, other in att_sums]
    for s in each:
        parts = 2 if s == sequences - 1 else 1
        low, terms = out_branch(attended[s], *att_sums[s], gain_two, near_full, model, parts, last)
        inner.append(low)
        branch.append([mp_sum(part, units) for part in terms])
        last = [terms[-1]]

    flat_tokens = tokens.reshape(sequences * span, model)
    flat_grads = out_grad.reshape(sequences * span, model)
    hidden, third_low, active, slope, act_sums = [], [], [], [], []
    for s in each:
        made = None
        for n, part in enumerate(branch[s]):
            made = widen(
                s, n, len(branch[s]), flat_tokens, *part, gain_three, near_full, ffn_width, made, last
            )
            last = [made[4]]
        hidden.append(made[0])
        third_low.append(made[1])
        active.append(made[2])
        slope.append(made[3])
        act_sums.append(mp_rows(made[4], units))
        last = [made[4]]

    own_sums, other_sums = [a for a, _ in act_sums], [b for _, b in act_sums]
    norm = (own_sums, other_sums, gain_four, full_units)
    down_parts = weight_grad(spot, [flat_grads], active, devices, groups, norm, True, last)
    down_sum = ScatterSum(down_parts, groups, True)
    last = [down_parts[0]]
    pre_low, third_terms = [], []
    scaled, back_sums, gain_four_grad = wide_back(
        flat_grads, down_full, active, own_sums, other_sums, gain_four, full_units, last
    )
    last = [back_sums[-1]]
    back_sums = [mp_rows(sums, units) for sums in back_sums]
    last = [down_sum.mates(last)] + [other for _, other in back_sums]
    for s in each:
        low, terms = pre_back(
            scaled[s], active[s], slope[s], *act_sums[s], *back_sums[s], near_full, full_units,
            last,
        )
        pre_low.append(low)
        third_terms.append(mp_sum(terms, units))
        last = [terms]

    gain_three_grad, gain_two_grad, gain_one_grad = 0.0, 0.0, 0.0
    order = jnp.bitwise_xor(place, jnp.array([3, 1, 2, 0], jnp.int32))
    grad_hidden, hidden_low, grads, projected_grads = [], [], [], []
    wide_terms = narrow(
        active, own_sums, other_sums, gain_four, down_full, full_units, last
    )
    last = [wide_terms]
    wide_terms = mp_sum(wide_terms, units)
    for s in each:
        made = middle(
            s, flat_grads, *third_terms[s], hidden[s], gain_three, near_full, attended[s],
            *att_sums[s], gain_two, model, last
        )
        grad_hidden.append(made[0])
        hidden_low.append(made[1])
        gain_three_grad += made[4]
        gain_two_grad += made[5]
        if s == 0:
            in_parts = weight_grad(
                spot, third_low, pre_low, devices, groups, None, False, [made[3]]
            )
            in_sum = ScatterSum(in_parts, groups)
            last = [in_parts[0], third_terms[1][1]]
        else:
            last = [in_sum.mates([made[3]])]
        parts = share_out(
            spot, made[2], attended[s], *att_sums[s], *mp_rows(made[3], units), model, groups,
            last, MIDDLE_PAUSE if s == 0 else None,
        )
        last = [parts[0]]
        grads.append(pass_round(parts, groups))
    last += [down_sum.rows]
    out_parts = weight_grad(spot, hidden_low, inner, devices, groups, None, True, last)
    out_sum = ScatterSum(out_parts, groups, True)
    last = [out_parts[0], *grads[1][1:]]
    for s in each:
        made = attend_back(
            metas[s], projected[s], grads[s], mixed[s], logs[s], tables, last,
            BACK_WEIGHT if s == 0 else 1,
        )
        projected_grads.append(made)
        last = [made]
        if s == 0:
            last = [out_sum.mates(last)]
        else:
            first_terms = mp_sum(join_halves(kept, got[2:], far, last), units)
            last = [first_terms[0]]
        away, kept, gain_part = first_back(
            order, made, first_low[s], heads_weight, gain_one, groups, last
        )
        gain_one_grad += gain_part
        got = [exchange(piece, "seq", groups, 1) for piece in away]
        if s == 0:
            near = add_halves(kept, *got[:2], [kept])
            far = [exchange(piece, "seq", groups, 2) for piece in near]
            last = [in_sum.chips([near[0]])]
        else:
            gain_one_sums = mp_rows(gain_one_grad, units)
            results = result_rows(*wide_terms, hidden, [kept], PAUSE)
            near = add_halves(kept, *got[:2], [results])
            last = [near[0], in_sum.raw, out_sum.rows]

    heads_part = heads_grad(first_low, projected_grads, last)
    heads_rows = lax.psum_scatter(heads_part, "dp", scatter_dimension=0, tiled=True)

    def input_grad(s, terms, into, after):
        return input_rows(
            s, sequences, flat_tokens, terms, gain_one, grad_hidden[s], into, after
        )

    gain_rows = jnp.concatenate(
        [
            (gain_one_sums[0] + gain_one_sums[1]).reshape(shards, -1),
            gain_three_grad.reshape(shards, -1),
            gain_two_grad.reshape(heads_here, shards, -1).transpose(1, 0, 2).reshape(shards, -1),
            gain_four_grad.reshape(ffn_width // HEAD_DIM, shards, -1)
            .transpose(1, 0, 2)
            .reshape(shards, -1),
        ],
        axis=1,
    )
    terms = []
    last = [heads_part, gain_one_sums[1]]
    for n, part in enumerate(near):
        far = exchange(part, "seq", groups, 2)
        column = n * (model // 2)
        own = add(
            [(kept, span, column), (got[2 + n], 0, 0), (far, 0, 0)],
            span,
            last,
            model // 2,
            None if n == 0 else LONG_PAUSE,
        )
        terms.append(mp_sum(own, units))
        if n == 0:
            gain_rows = relay(gain_rows, [own])
            grad_input = input_grad(0, [first_terms], None, [gain_rows])
            gain_rows = axis_sum(gain_rows, "dp", devices)
            last = [terms[0][1], gain_rows, grad_input]
    gain_rows = axis_sum(relay(gain_rows, [own]), "seq", groups)
    down_sum.chips()
    out_sum.chips()
    pieces = [
        lax.dynamic_slice_in_dim(heads_rows, jnp.bitwise_xor(place, n) * chunk, chunk, 0)
        for n in range(groups)
    ]
    pieces = pass_round(pieces, groups)
    grad_input = input_grad(1, terms, grad_input, [gain_rows])
    rows = jnp.stack(in_order(pieces, place)).astype(F32)
    grad_qkv_w = rows.reshape(groups, chunk, 3, share).transpose(2, 1, 0, 3)
    grad_qkv_w = grad_qkv_w.reshape(3, chunk, local_width)
    gain_sums = lax.dynamic_index_in_dim(gain_rows, number, 0, False)
    one, three, two, four = [gain_sums[cuts[n] : cuts[n + 1]] for n in range(4)]
    return (
        results.reshape(sequences, span, model),
        grad_input,
        grad_qkv_w,
        out_sum.out.T,
        in_sum.out,
        down_sum.out.T,
        one,
        two.reshape(gain_attn.shape),
        three,
        four.reshape(gain_ffn.shape),
    )


def solution(mesh):
    sizes = mesh.shape
    data = ("dp", "seq")
    in_specs = (
        P("dp", "seq", None),
        P("dp"),
        P(None, data, "mp"),
        P("mp", data),
        P(data, "mp"),
        P("mp", data),
        P(data),
        P("mp", data),
        P(data),
        P("mp", data),
        P("dp", "seq", None),
    )
    out_specs = (
        P("dp", "seq", None),
        P("dp", "seq", None),
        P(None, data, "mp"),
        P("mp", data),
        P(data, "mp"),
        P("mp", data),
        P(data),
        P("mp", data),
        P(data),
        P("mp", data),
    )
    run = partial(body, sizes["dp"], sizes["seq"], sizes["mp"])
    return jax.shard_map(run, mesh=mesh, in_specs=in_specs, out_specs=out_specs, check_vma=False)
```

```python
from functools import partial

import jax
import jax.numpy as jnp
from jax import lax
from jax.experimental import pallas as pl
from jax.experimental.pallas import tpu as pltpu
from jax.sharding import PartitionSpec as P

HEAD_DIM = 64
HALF = HEAD_DIM // 2
XPOS_BASE = 512
EPSILON = 1e-05
NEGATIVE = -1e30
LOG2_E = 1.4426950408889634
SCORE_SCALE = 0.125
VMEM = 56 * 2**20
BF16 = jnp.bfloat16
KERNEL_RATE = 0.25e9
BACK_WEIGHT = 25
PAUSE = 300
MIDDLE_PAUSE = 450
LONG_PAUSE = 160


def lasting(us):
    return pl.CostEstimate(flops=int(us * KERNEL_RATE), bytes_accessed=0, transcendentals=0)


F32 = jnp.float32


def params(limit=VMEM):
    return pltpu.CompilerParams(vmem_limit_bytes=limit)


def dot(left, right, left_dim, right_dim):
    return lax.dot_general(
        left, right, (((left_dim,), (right_dim,)), ((), ())), preferred_element_type=F32
    )


def swap_halves(block):
    width = block.shape[1]
    if width % 128:
        pieces = []
        for start in range(0, width, HEAD_DIM):
            pieces += [block[:, start + HALF : start + HEAD_DIM], block[:, start : start + HALF]]
        return jnp.concatenate(pieces, axis=1)
    lane = lax.broadcasted_iota(jnp.int32, (block.shape[0], 128), 1) % HEAD_DIM
    pieces = []
    for start in range(0, width, 128):
        part = block[:, start : start + 128]
        pieces.append(
            jnp.where(lane < HALF, pltpu.roll(part, 128 - HALF, 1), pltpu.roll(part, HALF, 1))
        )
    return pieces[0] if len(pieces) == 1 else jnp.concatenate(pieces, axis=1)


def turned(block, cosine, sine, sign):
    lanes = cosine.shape[1]
    pieces = []
    for start in range(0, block.shape[1], lanes):
        part = block[:, start : start + lanes]
        pieces.append(part * cosine + sign * (swap_halves(part) * sine))
    return pieces[0] if len(pieces) == 1 else jnp.concatenate(pieces, axis=1)


def project_kernel(place, *refs, groups, share):
    blocks, refs = refs[:groups], refs[groups:]
    gain, weight, cos_q, sin_q, cos_k, sin_k, low, made, held = refs
    for offset, block in enumerate(blocks):

        @pl.when(pl.program_id(0) == offset)
        def _(block=block):
            held[...] = block[...]

    normal, _ = row_norm(held[...].astype(F32))
    rows = (normal * gain[...]).astype(BF16)
    low[...] = rows
    out = dot(rows, weight[...], 1, 0)
    queries = turned(out[:, :share], cos_q[...], sin_q[...], 1)
    keys = turned(out[:, share : 2 * share], cos_k[...], sin_k[...], 1)
    made[...] = jnp.concatenate([queries, keys, out[:, 2 * share :]], axis=1).astype(BF16)


def project(place, blocks, gain, weight, tables, after=()):
    groups = len(blocks)
    span, model = blocks[0].shape
    width = weight.shape[1]
    lanes = tables[0].shape[1]

    def here(n, p):
        return (jnp.bitwise_xor(n, p[0]), 0)

    return call(
        partial(project_kernel, groups=groups, share=width // 3),
        "project",
        (groups,),
        [(block, (span, model), None) for block in blocks]
        + [(gain, (1, model), None), (weight, (model, width), None)]
        + [(table, (span, lanes), here) for table in tables],
        [
            ((groups * span, model), BF16, (span, model), here),
            ((groups * span, width), BF16, (span, width), here),
        ],
        [pltpu.VMEM((span, model), BF16)],
        5e-9 * groups * span * model * width,
        after,
        place,
    )


def attend_kernel(meta, projected, *refs, groups, heads, block):
    outs, log_ref, vt_all, o_all = refs[:groups], refs[groups], refs[groups + 1], refs[groups + 2]
    step = pl.program_id(0)
    length, place = meta[0], meta[1]
    share = heads * HEAD_DIM
    span = outs[0].shape[0]

    def lanes(part, h):
        return slice(part * share + h * HEAD_DIM, part * share + (h + 1) * HEAD_DIM)

    @pl.when(step == 0)
    def _():
        for h in range(heads):
            vt_all[h] = projected[:, lanes(2, h)].T

    start = pl.multiple_of(step * block, block)
    queries = [projected[pl.ds(start, block), lanes(0, h)] for h in range(heads)]
    scale = SCORE_SCALE * LOG2_E

    def keys_block(index, carry, masked):
        at = pl.multiple_of(index * block, block)
        if masked:
            key_pos = at + lax.broadcasted_iota(jnp.int32, (block, block), 0)
            query_pos = start + lax.broadcasted_iota(jnp.int32, (block, block), 1)
            allowed = (key_pos <= query_pos) & (key_pos < length)
        new = []
        for h in range(heads):
            top, total, mixed = carry[h]
            scores = dot(projected[pl.ds(at, block), lanes(1, h)], queries[h], 1, 1)
            if masked:
                scores = jnp.where(allowed, scores, NEGATIVE)
            higher = jnp.maximum(top, jnp.max(scores, axis=0, keepdims=True))
            fade = jnp.exp2((top - higher) * scale)
            weights = jnp.exp2((scores - higher) * scale)
            total = total * fade + jnp.sum(weights, axis=0, keepdims=True)
            added = dot(vt_all[h, :, pl.ds(at, block)], weights.astype(BF16), 1, 0)
            new.append((higher, total, mixed * fade + added))
        return tuple(new)

    carry = tuple(
        (
            jnp.full((1, block), NEGATIVE, F32),
            jnp.zeros((1, block), F32),
            jnp.zeros((HEAD_DIM, block), F32),
        )
        for _ in range(heads)
    )
    whole = jnp.minimum(step, length // block)
    end = jnp.minimum(step + 1, (length + block - 1) // block)
    carry = lax.fori_loop(0, whole, lambda n, c: keys_block(n, c, False), carry)
    carry = lax.fori_loop(whole, end, lambda n, c: keys_block(n, c, True), carry)
    pieces = []
    for h in range(heads):
        top, total, mixed = carry[h]
        pieces.append((mixed / total).T)
        log_ref[h : h + 1, :] = top * scale + jnp.log2(total)
    o_all[pl.ds(start, block), :] = jnp.concatenate(pieces, axis=1).astype(BF16)

    @pl.when(step == pl.num_programs(0) - 1)
    def _():
        for offset, out in enumerate(outs):
            at = pl.multiple_of(jnp.bitwise_xor(place, offset) * span, span)
            out[...] = o_all[pl.ds(at, span), :]


def attend(meta, projected, groups, after=()):
    count, width = projected.shape
    share = width // 3
    span = count // groups
    heads = share // HEAD_DIM
    block = min(512, span)
    results = call(
        partial(attend_kernel, groups=groups, heads=heads, block=block),
        "attend",
        (count // block,),
        [(projected, (count, width), None)],
        [((span, share), BF16, (span, share), None)] * groups
        + [((heads, count), F32, (heads, block), lambda n, m: (0, n))],
        [pltpu.VMEM((heads, HEAD_DIM, count), BF16), pltpu.VMEM((count, share), BF16)],
        2.9e-8 * count * count * share,
        after,
        meta,
    )
    return results[:groups], results[groups]


def attend_back_kernel(meta, projected, *refs, groups, heads, block):
    grads, mixed = refs[:groups], refs[groups : 2 * groups]
    log_ref, cos_q, sin_q, cos_k, sin_k, out = refs[2 * groups : 2 * groups + 6]
    g_all, kt_all, dot_all, dqt_all, dk_sum, dv_sum = refs[2 * groups + 6 :]
    length, place = meta[0], meta[1]
    span = grads[0].shape[0]
    count = groups * span
    share = heads * HEAD_DIM
    scale = SCORE_SCALE * LOG2_E

    def lanes(part, h):
        return slice(part * share + h * HEAD_DIM, part * share + (h + 1) * HEAD_DIM)

    for h in range(heads):
        kt_all[h] = projected[:, lanes(1, h)].T
    for offset in range(groups):
        at = pl.multiple_of(jnp.bitwise_xor(place, offset) * span, span)
        g_all[pl.ds(at, span), :] = grads[offset][...]
        both = grads[offset][...].astype(F32) * mixed[offset][...].astype(F32)
        for h in range(heads):
            dot_all[h : h + 1, pl.ds(at, span)] = jnp.sum(
                both[:, lanes(0, h)].T, axis=0, keepdims=True
            )
    dqt_all[...] = jnp.zeros_like(dqt_all)
    query_blocks = count // block

    def keys_block(index, _):
        key_at = pl.multiple_of(index * block, block)
        keys = [projected[pl.ds(key_at, block), lanes(1, h)] for h in range(heads)]
        values = [projected[pl.ds(key_at, block), lanes(2, h)] for h in range(heads)]
        dk_sum[...] = jnp.zeros_like(dk_sum)
        dv_sum[...] = jnp.zeros_like(dv_sum)

        def query_block(index, _, masked):
            at = pl.multiple_of(index * block, block)
            if masked:
                key_pos = key_at + lax.broadcasted_iota(jnp.int32, (block, block), 0)
                query_pos = at + lax.broadcasted_iota(jnp.int32, (block, block), 1)
                allowed = (key_pos <= query_pos) & (key_pos < length)
            for h in range(heads):
                query = projected[pl.ds(at, block), lanes(0, h)]
                grad = g_all[pl.ds(at, block), lanes(0, h)]
                scores = dot(keys[h], query, 1, 1)
                weights = jnp.exp2(scores * scale - log_ref[h : h + 1, pl.ds(at, block)])
                if masked:
                    weights = jnp.where(allowed, weights, 0.0)
                grad_weights = dot(values[h], grad, 1, 1)
                grad_scores = weights * (grad_weights - dot_all[h : h + 1, pl.ds(at, block)])
                grad_scores = grad_scores.astype(BF16)
                dv_sum[h] += dot(weights.astype(BF16), grad, 1, 0)
                dk_sum[h] += dot(grad_scores, query, 1, 0)
                dqt_all[h, :, pl.ds(at, block)] += dot(
                    kt_all[h, :, pl.ds(key_at, block)], grad_scores, 1, 0
                )
            return 0

        crosses = key_at + block > length
        whole = jnp.where(crosses, query_blocks, index + 1)
        lax.fori_loop(index, whole, partial(query_block, masked=True), 0)
        lax.fori_loop(whole, query_blocks, partial(query_block, masked=False), 0)
        dk = jnp.concatenate([dk_sum[h] for h in range(heads)], axis=1) * SCORE_SCALE
        dv = jnp.concatenate([dv_sum[h] for h in range(heads)], axis=1)
        turn = (cos_k[pl.ds(key_at, block), :], sin_k[pl.ds(key_at, block), :])
        out[pl.ds(key_at, block), share : 2 * share] = turned(dk, *turn, -1).astype(BF16)
        out[pl.ds(key_at, block), 2 * share :] = dv.astype(BF16)
        return 0

    used = (length + block - 1) // block
    lax.fori_loop(0, used, keys_block, 0)

    def no_keys(index, _):
        at = pl.multiple_of(index * block, block)
        out[pl.ds(at, block), share:] = jnp.zeros((block, 2 * share), BF16)
        return 0

    lax.fori_loop(used, query_blocks, no_keys, 0)
    for index in range(query_blocks):
        at = slice(index * block, (index + 1) * block)
        dq = jnp.concatenate([dqt_all[h, :, at].T for h in range(heads)], axis=1) * SCORE_SCALE
        out[at, :share] = turned(dq, cos_q[at, :], sin_q[at, :], -1).astype(BF16)


def attend_back(meta, projected, grads, mixed, logs, tables, after=(), weight=1):
    groups = len(grads)
    count, width = projected.shape
    share = width // 3
    span = count // groups
    heads = share // HEAD_DIM
    block = min(512, span)
    return call(
        partial(attend_back_kernel, groups=groups, heads=heads, block=block),
        "attend_back",
        (1,),
        [(projected, (count, width), None)]
        + [(piece, (span, share), None) for piece in (*grads, *mixed)]
        + [(logs, logs.shape, None)]
        + [(table, table.shape, None) for table in tables],
        [((count, width), BF16, (count, width), None)],
        [
            pltpu.VMEM((count, share), BF16),
            pltpu.VMEM((heads, HEAD_DIM, count), BF16),
            pltpu.VMEM((heads, count), F32),
            pltpu.VMEM((heads, HEAD_DIM, count), F32),
            pltpu.VMEM((heads, block, HEAD_DIM), F32),
            pltpu.VMEM((heads, block, HEAD_DIM), F32),
        ],
        4.2e-8 * count * count * share * weight,
        after,
        meta,
    )[0]


def heads_grad_kernel(*refs, sequences):
    grads, lows, out = refs[:sequences], refs[sequences : 2 * sequences], refs[2 * sequences]
    total = dot(lows[0][...].T, grads[0][...], 1, 0)
    for s in range(1, sequences):
        total += dot(lows[s][...].T, grads[s][...], 1, 0)
    out[...] = total.astype(BF16)


def heads_grad(lows, grads, after=()):
    sequences = len(lows)
    count, model = lows[0].shape
    width = grads[0].shape[1]
    tile = 512
    return call(
        partial(heads_grad_kernel, sequences=sequences),
        "heads_grad",
        (model // tile,),
        [(grad, (count, width), None) for grad in grads]
        + [(low, (count, tile), lambda n: (0, n)) for low in lows],
        [((model, width), BF16, (tile, width), lambda n: (n, 0))],
        [],
        3e-9 * sequences * count * model * width,
        after,
    )[0]


def normed_rows(block, column_mean, column_std, gain):
    return (block.astype(F32) - column_mean) * column_std * gain


def moments(own, other, width):
    total = own + other
    mean = total[0:1] / width
    return mean, lax.rsqrt(total[1:2] / width - mean * mean + EPSILON)


def as_column(row):
    return jnp.broadcast_to(row, (128, row.shape[1])).T[:, 0:1]


def as_row(block):
    width = block.shape[1]
    part = block[:, 0:128]
    for start in range(128, width, 128):
        part = part + block[:, start : start + 128]
    return jnp.sum(part.T, axis=0, keepdims=True)


def weight_grad_kernel(place, *refs, sequences, devices, groups, chunk, offsets, normed, extra):
    lefts, refs = refs[:sequences], refs[sequences:]
    rights, refs = refs[:sequences], refs[sequences:]
    if normed:
        own_sums, other_sums, gain = refs[:sequences], refs[sequences : 2 * sequences], refs[2 * sequences]
        refs = refs[2 * sequences + 1 :]
    away, kept, turned_left = refs[extra : extra + 3]
    columns_ref = refs[extra + 3] if normed else None
    span = lefts[0].shape[0]

    @pl.when(pl.program_id(0) == 0)
    def _():
        row = 0
        for device, offset in offsets:
            target = jnp.bitwise_xor(place[0], offset)
            at = pl.multiple_of((device * groups + target) * chunk, chunk)
            for s in range(sequences):
                turned_left[row : row + chunk, s * span : (s + 1) * span] = lefts[s][
                    :, pl.ds(at, chunk)
                ].T
            row += chunk
        if normed:
            for s in range(sequences):
                mean, std = moments(own_sums[s][...], other_sums[s][...], normed)
                columns_ref[2 * s] = jnp.broadcast_to(as_column(mean), (span, 128))
                columns_ref[2 * s + 1] = jnp.broadcast_to(as_column(std), (span, 128))

    values = []
    for s in range(sequences):
        block = rights[s][...]
        if normed:
            block = normed_rows(
                block, columns_ref[2 * s, :, 0:1], columns_ref[2 * s + 1, :, 0:1], gain[...]
            ).astype(BF16)
        values.append(block)
    block = turned_left.shape[0] // 4
    parts = [away.at[:block], away.at[block:], kept.at[:block], kept.at[block:]]
    for n, part in enumerate(parts):
        rows = slice(n * block, (n + 1) * block)
        total = dot(turned_left[rows, :span], values[0], 1, 0)
        for s in range(1, sequences):
            total += dot(turned_left[rows, s * span : (s + 1) * span], values[s], 1, 0)
        part[...] = total.astype(BF16)


def weight_grad(place, lefts, rights, devices, groups, norm=None, z_first=False, after=()):
    sequences = len(rights)
    span = rights[0].shape[-2]
    width = lefts[0].shape[1]
    layers = rights[0].ndim == 3
    columns = rights[0].shape[0] * rights[0].shape[2] if layers else rights[0].shape[1]
    chunk = width // (devices * groups)
    tile = 512 if rights[0].shape[-1] % 512 == 0 else rights[0].shape[-1]
    half = width // 2
    if z_first:
        offsets = [(d, o) for core in (1, 0) for d in range(devices) for o in (2 + core, core)]
    else:
        offsets = [(d, o) for o in (3, 1, 2, 0) for d in range(devices)]
    if layers:
        tiles = rights[0].shape[2] // tile
        right_spec = pl.BlockSpec((None, span, tile), lambda n, p: (n // tiles, 0, n % tiles))
    else:
        right_spec = pl.BlockSpec((span, tile), lambda n, p: (0, n))
    if len(lefts) == sequences:
        in_specs = [pl.BlockSpec((span, width), lambda n, p: (0, 0))] * sequences
    else:
        lefts = lefts * sequences
        in_specs = [
            pl.BlockSpec((span, width), lambda n, p, s=s: (s, 0)) for s in range(sequences)
        ]
    in_specs += [right_spec] * sequences
    operands = [*lefts, *rights]
    scratch = [pltpu.VMEM((width, sequences * span), BF16)]
    full = 0
    if norm:
        own_sums, other_sums, gain, full = norm
        in_specs += [pl.BlockSpec((2, span), lambda n, p: (0, 0))] * (2 * sequences)
        in_specs += [pl.BlockSpec((1, tile), lambda n, p: (0, n))]
        operands += [*own_sums, *other_sums, gain]
        scratch += [pltpu.VMEM((2 * sequences, span, 128), F32)]
    in_specs += [pl.BlockSpec(memory_space=pl.ANY)] * len(after)
    return pl.pallas_call(
        partial(
            weight_grad_kernel,
            sequences=sequences,
            devices=devices,
            groups=groups,
            chunk=chunk,
            offsets=offsets,
            normed=full,
            extra=len(after),
        ),
        grid_spec=pltpu.PrefetchScalarGridSpec(
            num_scalar_prefetch=1,
            grid=(columns // tile,),
            in_specs=in_specs,
            out_specs=[pl.BlockSpec((half, tile), lambda n, p: (0, n))] * 2,
            scratch_shapes=scratch,
        ),
        out_shape=[jax.ShapeDtypeStruct((half, columns), BF16)] * 2,
        compiler_params=params(),
        cost_estimate=lasting(2.9e-9 * sequences * span * width * columns),
        name="weight_grad",
    )(place, *operands, *after)


def call(kernel, name, grid, ins, outs, scratch, us, after=(), scalars=None, into=None):
    into = into or []
    after = [*into, *after]
    extra = len(after)
    first = 0 if scalars is None else 1
    count = first + len(ins)

    def run(*refs):
        kernel(*refs[:count], *refs[count + extra :])

    def spec(block, index):
        if index is None:
            return pl.BlockSpec(block, lambda *_: (0,) * len(block))
        return pl.BlockSpec(block, index)

    return pl.pallas_call(
        run,
        grid_spec=pltpu.PrefetchScalarGridSpec(
            num_scalar_prefetch=first,
            grid=grid,
            in_specs=[spec(block, index) for _, block, index in ins]
            + [pl.BlockSpec(memory_space=pl.ANY)] * extra,
            out_specs=[spec(block, index) for _, _, block, index in outs],
            scratch_shapes=scratch,
        ),
        out_shape=[jax.ShapeDtypeStruct(shape, dtype) for shape, dtype, _, _ in outs],
        input_output_aliases={count + n: n for n in range(len(into))},
        compiler_params=params(),
        cost_estimate=lasting(us),
        name=name,
    )(*(() if scalars is None else (scalars,)), *[array for array, _, _ in ins], *after)


def pack_kernel(columns, rows, out):
    width = columns.shape[1]
    out[:, :width] = columns[...]
    out[:, width:] = rows[...].T


def pack(columns, rows, after=()):
    height, width = columns.shape
    total = width + rows.shape[0]
    return call(
        pack_kernel,
        "pack",
        (1,),
        [(columns, columns.shape, None), (rows, rows.shape, None)],
        [((height, total), BF16, (height, total), None)],
        [],
        1,
        after,
    )[0]


def collect_kernel(place, *refs, groups):
    pieces, (whole, sums) = refs[:groups], refs[groups:]
    share = pieces[0].shape[1]
    total, squares = 0.0, 0.0
    for offset, piece in enumerate(pieces):
        at = pl.multiple_of(jnp.bitwise_xor(place[0], offset) * share, share)
        block = piece[...]
        whole[:, pl.ds(at, share)] = block
        wide = block.astype(F32)
        total += as_row(wide)
        squares += as_row(wide * wide)
    sums[...] = jnp.concatenate([total, squares], axis=0)


def collect(place, pieces, after=()):
    groups = len(pieces)
    span, share = pieces[0].shape
    if share % 128:
        stacked = jnp.stack(pieces)
        whole = jnp.concatenate(
            [
                lax.dynamic_index_in_dim(stacked, jnp.bitwise_xor(place[0], n), 0, False)
                for n in range(groups)
            ],
            axis=1,
        )
        wide = whole.astype(F32)
        return whole, jnp.stack([jnp.sum(wide, axis=1), jnp.sum(wide * wide, axis=1)])
    width = groups * share
    return call(
        partial(collect_kernel, groups=groups),
        "collect",
        (1,),
        [(piece, (span, share), None) for piece in pieces],
        [((span, width), BF16, (span, width), None), ((2, span), F32, (2, span), None)],
        [],
        5e-6 * span * width,
        after,
        place,
    )


def out_kernel(mixed, own, other, gain, weight, inner, branch, *, full):
    mean, std = moments(own[...], other[...], full)
    low = normed_rows(mixed[...], as_column(mean), as_column(std), gain[...]).astype(BF16)
    inner[...] = low
    branch[...] = dot(low, weight[...], 1, 1).astype(BF16)


def out_branch(mixed, own, other, gain, near_full, full, parts=1, after=()):
    span, width = mixed.shape
    model = near_full.shape[0]
    place = near_full.shape[1] // width - 1
    rows = span // parts
    made = [None]
    branches = []
    for n in range(parts):
        made = call(
            partial(out_kernel, full=full),
            "out_branch",
            (1,),
            [
                (mixed, (rows, width), lambda _, n=n: (n, 0)),
                (own, (2, rows), lambda _, n=n: (0, n)),
                (other, (2, rows), lambda _, n=n: (0, n)),
                (gain, (1, width), None),
                (near_full, (model, width), lambda _: (0, place)),
            ],
            [
                ((span, width), BF16, (rows, width), lambda _, n=n: (n, 0)),
                ((rows, model), BF16, (rows, model), None),
            ],
            [],
            6e-9 * rows * width * model,
            after,
            None,
            made[:1] if n else None,
        )
        branches.append(made[1])
        after = [made[1]]
    return made[0], branches


def row_norm(block):
    mean = jnp.mean(block, axis=-1, keepdims=True)
    centered = block - mean
    std = lax.rsqrt(jnp.mean(centered * centered, axis=-1, keepdims=True) + EPSILON)
    return centered * std, std


def widen_kernel(tokens, own, other, gain, weight, hidden, low, active, slope, sums, total, squares):
    step = pl.program_id(0)

    @pl.when(step == 0)
    def _():
        block = tokens[...].astype(F32) + (own[...].astype(F32) + other[...].astype(F32))
        hidden[...] = block
        normal, _ = row_norm(block)
        low[...] = (normal * gain[...]).astype(BF16)
        total[...] = jnp.zeros_like(total)
        squares[...] = jnp.zeros_like(squares)

    pre = dot(low[...], weight[...], 1, 0)
    below = 0.5 + 0.5 * lax.erf(pre * 0.7071067811865476)
    value = pre * below
    active[...] = value.astype(BF16)
    slope[...] = (below + pre * (0.3989422804014327 * jnp.exp2(pre * pre * (-0.5 * LOG2_E)))).astype(
        BF16
    )
    part, square = total[...], squares[...]
    for start in range(0, value.shape[1], 128):
        piece = value[:, start : start + 128]
        part += piece
        square += piece * piece
    total[...] = part
    squares[...] = square

    @pl.when(step == pl.num_programs(0) - 1)
    def _():
        sums[...] = jnp.concatenate([as_row(total[...]), as_row(squares[...])], axis=0)


def widen(number, part, parts, tokens, own, other, gain, weight, units, into=None, after=()):
    rows, model = own.shape
    span = rows * parts
    tile = min(1024, units)
    block = (rows, model)
    across = (rows, tile)
    here = lambda n: (part, 0)
    tiled = lambda n: (part, n)
    return call(
        widen_kernel,
        "widen",
        (units // tile,),
        [
            (tokens, block, lambda n: (number * parts + part, 0)),
            (own, block, None),
            (other, block, None),
            (gain, (1, model), None),
            (weight, (model, tile), lambda n: (0, n)),
        ],
        [
            ((span, model), F32, block, here),
            ((span, model), BF16, block, here),
            ((span, units), BF16, across, tiled),
            ((span, units), BF16, across, tiled),
            ((2, span), F32, (2, rows), lambda n: (0, part)),
        ],
        [pltpu.VMEM((rows, 128), F32)] * 2,
        5.4e-9 * rows * model * units,
        after,
        None,
        into,
    )


def narrow_kernel(gain, weight, *refs, sequences, full):
    active, refs = refs[:sequences], refs[sequences:]
    own, refs = refs[:sequences], refs[sequences:]
    other, refs = refs[:sequences], refs[sequences:]
    branch, total, columns, low = refs
    step = pl.program_id(0)
    span = active[0].shape[0]

    @pl.when(step == 0)
    def _():
        for s in range(sequences):
            mean, std = moments(own[s][...], other[s][...], full)
            columns[2 * s] = jnp.broadcast_to(as_column(mean), columns.shape[1:])
            columns[2 * s + 1] = jnp.broadcast_to(as_column(std), columns.shape[1:])
        total[...] = jnp.zeros_like(total)

    for s in range(sequences):
        low[s * span : (s + 1) * span, :] = normed_rows(
            active[s][...], columns[2 * s, :, 0:1], columns[2 * s + 1, :, 0:1], gain[...]
        ).astype(BF16)
    total[...] += dot(low[...], weight[...], 1, 0)

    @pl.when(step == pl.num_programs(0) - 1)
    def _():
        branch[...] = total[...].astype(BF16)


def narrow(active, own, other, gain, weight, full, after=()):
    sequences = len(active)
    span, units = active[0].shape
    model = weight.shape[1]
    tile = min(1024, units)
    sums = (2, span)
    rows = sequences * span
    return call(
        partial(narrow_kernel, sequences=sequences, full=full),
        "narrow",
        (units // tile,),
        [
            (gain, (1, tile), lambda n: (0, n)),
            (weight, (tile, model), lambda n: (n, 0)),
        ]
        + [(array, (span, tile), lambda n: (0, n)) for array in active]
        + [(array, sums, None) for array in (*own, *other)],
        [((rows, model), BF16, (rows, model), None)],
        [
            pltpu.VMEM((rows, model), F32),
            pltpu.VMEM((2 * sequences, span, 128), F32),
            pltpu.VMEM((rows, tile), BF16),
        ],
        3.2e-9 * rows * model * units,
        after,
    )[0]


def wide_back_kernel(grads, weight, gain, *refs, sequences, full):
    active, refs = refs[:sequences], refs[sequences:]
    own, refs = refs[:sequences], refs[sequences:]
    other, refs = refs[:sequences], refs[sequences:]
    scaled, refs = refs[:sequences], refs[sequences:]
    sums, refs = refs[:sequences], refs[sequences:]
    gain_grad, columns, totals = refs
    step = pl.program_id(0)
    span = active[0].shape[0]

    @pl.when(step == 0)
    def _():
        for s in range(sequences):
            mean, std = moments(own[s][...], other[s][...], full)
            columns[2 * s] = jnp.broadcast_to(as_column(mean), columns.shape[1:])
            columns[2 * s + 1] = jnp.broadcast_to(as_column(std), columns.shape[1:])
        totals[...] = jnp.zeros_like(totals)

    every = dot(grads[...], weight[...], 1, 1)
    gain_part = 0.0
    for s in range(sequences):
        grad = every[s * span : (s + 1) * span]
        normal = (active[s][...].astype(F32) - columns[2 * s, :, 0:1]) * columns[2 * s + 1, :, 0:1]
        product = grad * normal
        gain_part += jnp.sum(product, axis=0, keepdims=True)
        grad = grad * gain[...]
        scaled[s][...] = grad.astype(BF16)
        product = product * gain[...]
        part, other_part = totals[2 * s], totals[2 * s + 1]
        for start in range(0, grad.shape[1], 128):
            part += grad[:, start : start + 128]
            other_part += product[:, start : start + 128]
        totals[2 * s] = part
        totals[2 * s + 1] = other_part
    gain_grad[...] = gain_part

    @pl.when(step == pl.num_programs(0) - 1)
    def _():
        for s in range(sequences):
            sums[s][...] = jnp.concatenate(
                [as_row(totals[2 * s]), as_row(totals[2 * s + 1])], axis=0
            )


def wide_back(grads, weight, active, own, other, gain, full, after=()):
    sequences = len(active)
    span, units = active[0].shape
    model = weight.shape[1]
    tile = min(1024, units)
    sums = (2, span)
    across = (span, tile)
    tiled = lambda n: (0, n)
    made = call(
        partial(wide_back_kernel, sequences=sequences, full=full),
        "wide_back",
        (units // tile,),
        [
            (grads, (sequences * span, model), None),
            (weight, (tile, model), lambda n: (n, 0)),
            (gain, (1, tile), tiled),
        ]
        + [(array, across, tiled) for array in active]
        + [(array, sums, None) for array in (*own, *other)],
        [((span, units), BF16, across, tiled)] * sequences
        + [(sums, F32, sums, None)] * sequences
        + [((1, units), F32, (1, tile), tiled)],
        [pltpu.VMEM((2 * sequences, span, 128), F32)] * 2,
        3.5e-9 * sequences * span * model * units,
        after,
    )
    return made[:sequences], made[sequences : 2 * sequences], made[2 * sequences]


def pre_back_kernel(
    scaled, active, slope, own, other, own_back, other_back, weight, grads, branch, total, columns, *, full
):
    step = pl.program_id(0)

    @pl.when(step == 0)
    def _():
        mean, std = moments(own[...], other[...], full)
        back = (own_back[...] + other_back[...]) / full
        for n, row in enumerate((mean, std, back[0:1], back[1:2])):
            columns[n] = jnp.broadcast_to(as_column(row), columns.shape[1:])
        total[...] = jnp.zeros_like(total)

    std = columns[1, :, 0:1]
    normal = (active[...].astype(F32) - columns[0, :, 0:1]) * std
    grad = std * (scaled[...].astype(F32) - columns[2, :, 0:1] - normal * columns[3, :, 0:1])
    low = (grad * slope[...].astype(F32)).astype(BF16)
    grads[...] = low
    total[...] += dot(low, weight[...], 1, 1)

    @pl.when(step == pl.num_programs(0) - 1)
    def _():
        branch[...] = total[...].astype(BF16)


def pre_back(scaled, active, slope, own, other, own_back, other_back, weight, full, after=()):
    span, units = active.shape
    model = weight.shape[0]
    tile = min(1024, units)
    sums = (2, span)
    across = (span, tile)
    tiled = lambda n: (0, n)
    return call(
        partial(pre_back_kernel, full=full),
        "pre_back",
        (units // tile,),
        [
            (scaled, across, tiled),
            (active, across, tiled),
            (slope, across, tiled),
            (own, sums, None),
            (other, sums, None),
            (own_back, sums, None),
            (other_back, sums, None),
            (weight, (model, tile), tiled),
        ],
        [((span, units), BF16, across, tiled), ((span, model), BF16, (span, model), None)],
        [pltpu.VMEM((span, model), F32), pltpu.VMEM((4, span, 128), F32)],
        4.6e-9 * span * model * units,
        after,
    )


def middle_kernel(
    grads, own, other, hidden, gain, weight, mixed, own_sums, other_sums, gain_attn,
    grad_hidden, low, scaled, sums, gain_grad, gain_attn_grad, *, full
):
    step = pl.program_id(0)

    @pl.when(step == 0)
    def _():
        gain_grad[...] = jnp.zeros_like(gain_grad)
        gain_attn_grad[...] = jnp.zeros_like(gain_attn_grad)

    normal, std = row_norm(hidden[...])
    grad = own[...].astype(F32) + other[...].astype(F32)
    gain_grad[...] += jnp.sum(grad * normal, axis=0, keepdims=True)
    part = grad * gain[...]
    back = std * (
        part
        - jnp.mean(part, axis=-1, keepdims=True)
        - normal * jnp.mean(part * normal, axis=-1, keepdims=True)
    )
    total = grads[...].astype(F32) + back
    grad_hidden[...] = total
    rows = total.astype(BF16)
    low[...] = rows
    inner = dot(rows, weight[...], 1, 0)
    mean, deviation = moments(own_sums[...], other_sums[...], full)
    normal = (mixed[...].astype(F32) - as_column(mean)) * as_column(deviation)
    gain_attn_grad[...] += jnp.sum(inner * normal, axis=0, keepdims=True)
    inner = inner * gain_attn[...]
    scaled[...] = inner
    sums[...] = jnp.concatenate([as_row(inner), as_row(inner * normal)], axis=0)


def middle(
    number, grads, own, other, hidden, gain, near_full, mixed, own_sums, other_sums, gain_attn, full, after=()
):
    span, model = hidden.shape
    width = mixed.shape[1]
    place = near_full.shape[1] // width - 1
    rows = min(256, span)
    below = number * (span // rows)
    by_row = lambda n: (n, 0)
    by_column = lambda n: (0, n)
    return call(
        partial(middle_kernel, full=full),
        "middle",
        (span // rows,),
        [
            (grads, (rows, model), lambda n: (n + below, 0)),
            (own, (rows, model), by_row),
            (other, (rows, model), by_row),
            (hidden, (rows, model), by_row),
            (gain, (1, model), None),
            (near_full, (model, width), lambda n: (0, place)),
            (mixed, (rows, width), by_row),
            (own_sums, (2, rows), by_column),
            (other_sums, (2, rows), by_column),
            (gain_attn, (1, width), None),
        ],
        [
            ((span, model), F32, (rows, model), by_row),
            ((span, model), BF16, (rows, model), by_row),
            ((span, width), F32, (rows, width), by_row),
            ((2, span), F32, (2, rows), by_column),
            ((1, model), F32, (1, model), None),
            ((1, width), F32, (1, width), None),
        ],
        [],
        1.2e-8 * span * width * model,
        after,
    )


def share_out_kernel(place, scaled, mixed, own, other, own_back, other_back, *outs, full):
    mean, std = moments(own[...], other[...], full)
    back = (own_back[...] + other_back[...]) / full
    mean, std, first, second = [as_column(row) for row in (mean, std, back[0:1], back[1:2])]
    share = outs[0].shape[1]
    for offset, out in enumerate(outs):
        at = pl.multiple_of(jnp.bitwise_xor(place[0], offset) * share, share)
        normal = (mixed[:, pl.ds(at, share)].astype(F32) - mean) * std
        out[...] = (std * (scaled[:, pl.ds(at, share)] - first - normal * second)).astype(BF16)


def share_out(
    place, scaled, mixed, own, other, own_back, other_back, full, groups, after=(), us=None
):
    span, width = scaled.shape
    share = width // groups
    if share % 128:
        mean, std = moments(own, other, full)
        back = (own_back + other_back) / full
        mean, std, first, second = [row.reshape(-1, 1) for row in (mean, std, back[0], back[1])]
        normal = (mixed.astype(F32) - mean) * std
        grads = (std * (scaled - first - normal * second)).astype(BF16)
        return [
            lax.dynamic_slice_in_dim(grads, jnp.bitwise_xor(place[0], n) * share, share, 1)
            for n in range(groups)
        ]
    sums = (2, span)
    return call(
        partial(share_out_kernel, full=full),
        "share_out",
        (1,),
        [
            (scaled, (span, width), None),
            (mixed, (span, width), None),
            (own, sums, None),
            (other, sums, None),
            (own_back, sums, None),
            (other_back, sums, None),
        ],
        [((span, share), BF16, (span, share), None)] * groups,
        [],
        us or 7.6e-6 * span * width,
        after,
        place,
    )


def first_back_kernel(order, grads, low, weight, gain, *refs):
    away, (kept, gain_grad, total) = refs[:4], refs[4:]
    step = pl.program_id(0)
    grad = dot(grads[...], weight[...], 1, 1)
    made = grad.astype(BF16)
    half = made.shape[1] // 2
    for n in range(2):

        @pl.when(step == n)
        def _(n=n):
            away[2 * n][...] = made[:, :half]
            away[2 * n + 1][...] = made[:, half:]

    @pl.when(step >= 2)
    def _():
        kept[...] = made

    @pl.when(step == 0)
    def _():
        total[...] = jnp.zeros_like(total)

    total[...] += jnp.sum(grad * low[...].astype(F32), axis=0, keepdims=True)

    @pl.when(step == pl.num_programs(0) - 1)
    def _():
        gain_grad[...] = total[...] / gain[...]


def first_back(order, grads, low, weight, gain, groups, after=()):
    count, width = grads.shape
    model = weight.shape[0]
    span = count // groups
    rows = (span, model)
    half = (span, model // 2)
    made = call(
        first_back_kernel,
        "first_back",
        (groups,),
        [
            (grads, (span, width), lambda n, p: (p[n], 0)),
            (low, rows, lambda n, p: (p[n], 0)),
            (weight, (model, width), None),
            (gain, (1, model), None),
        ],
        [(half, BF16, half, None)] * 4
        + [
            ((2 * span, model), BF16, rows, lambda n, p: (jnp.maximum(n - 2, 0), 0)),
            ((1, model), F32, (1, model), None),
        ],
        [pltpu.VMEM((1, model), F32)],
        4.5e-9 * count * model * width,
        after,
        order,
    )
    return made[:4], made[4], made[5]


def relay_kernel(array, out):
    out[...] = array[...]


def relay(array, after):
    rows = min(128, array.shape[0])
    block = (rows, array.shape[1])
    return call(
        relay_kernel,
        "relay",
        (array.shape[0] // rows,),
        [(array, block, lambda n: (n, 0))],
        [(array.shape, array.dtype, block, lambda n: (n, 0))],
        [],
        1,
        after,
    )[0]


def exchange(array, axis, size, offset):
    return lax.ppermute(array, axis, [(n, n ^ offset) for n in range(size)])


def add_kernel(*refs):
    total = refs[0][...].astype(F32)
    for ref in refs[1:-1]:
        total += ref[...].astype(F32)
    refs[-1][...] = total.astype(BF16)


def add(arrays, rows, after=(), width=None, us=None):
    width = width or arrays[0][0].shape[1]
    tile = 128

    def place(row, column):
        return lambda n: (n + row // tile, column // width)

    return call(
        add_kernel,
        "add",
        (rows // tile,),
        [(array, (tile, width), place(row, column)) for array, row, column in arrays],
        [((rows, width), BF16, (tile, width), lambda n: (n, 0))],
        [],
        us or 1.5e-6 * rows * width,
        after,
    )[0]


def add_halves_kernel(whole, left, right, *outs):
    half = left.shape[1]
    for n, (part, out) in enumerate(zip((left, right), outs)):
        total = whole[:, n * half : (n + 1) * half].astype(F32) + part[...].astype(F32)
        out[...] = total.astype(BF16)


def add_halves(whole, left, right, after=()):
    rows, width = left.shape
    tile = 128
    half = (tile, width)
    by_row = lambda n: (n, 0)
    return call(
        add_halves_kernel,
        "add_halves",
        (rows // tile,),
        [(whole, (tile, 2 * width), by_row), (left, half, by_row), (right, half, by_row)],
        [((rows, width), BF16, half, by_row)] * 2,
        [],
        3e-6 * rows * width,
        after,
    )


def join_halves_kernel(whole, *refs):
    pieces, out = refs[:-1], refs[-1]
    half = pieces[0].shape[1]
    for n in range(2):
        at = slice(n * half, (n + 1) * half)
        total = whole[:, at].astype(F32)
        for piece in pieces[n::2]:
            total += piece[...].astype(F32)
        out[:, at] = total.astype(BF16)


def join_halves(whole, got, far, after=()):
    rows, width = far[0].shape
    tile = 128
    half = (tile, width)
    below = rows // tile
    return call(
        join_halves_kernel,
        "join_halves",
        (rows // tile,),
        [(whole, (tile, 2 * width), lambda n: (n + below, 0))]
        + [(piece, half, lambda n: (n, 0)) for piece in (*got, *far)],
        [((rows, 2 * width), BF16, (tile, 2 * width), lambda n: (n, 0))],
        [],
        3e-6 * rows * width,
        after,
    )[0]


def result_kernel(own, other, *refs, tiles):
    hidden, out = refs[:-1], refs[-1]
    total = own[...].astype(F32) + other[...].astype(F32)
    for s, part in enumerate(hidden):

        @pl.when(pl.program_id(0) // tiles == s)
        def _(part=part):
            out[...] = (part[...] + total).astype(BF16)


def result_rows(own, other, hidden, after=(), us=None):
    span, model = hidden[0].shape
    rows = own.shape[0]
    tile = min(128, span)
    tiles = span // tile
    block = (tile, model)
    by_row = lambda n: (n, 0)
    return call(
        partial(result_kernel, tiles=tiles),
        "result",
        (rows // tile,),
        [(own, block, by_row), (other, block, by_row)]
        + [
            (array, block, lambda n, s=s: (jnp.clip(n - s * tiles, 0, tiles - 1), 0))
            for s, array in enumerate(hidden)
        ],
        [((rows, model), BF16, block, by_row)],
        [],
        us or 1.5e-6 * rows * model,
        after,
    )[0]


def input_kernel(tokens, gain, grads, *refs):
    out = refs[-1]
    pieces = [
        own[...].astype(F32) + other[...].astype(F32)
        for own, other in zip(refs[:-1:2], refs[1:-1:2])
    ]
    total = pieces[0] if len(pieces) == 1 else jnp.concatenate(pieces, axis=1)
    normal, std = row_norm(tokens[...].astype(F32))
    part = total * gain[...]
    first = std * (
        part
        - jnp.mean(part, axis=-1, keepdims=True)
        - normal * jnp.mean(part * normal, axis=-1, keepdims=True)
    )
    out[...] = (grads[...] + first).astype(BF16)


def input_rows(number, count, tokens, terms, gain, grads, into, after=()):
    span, model = grads.shape
    tile = min(128, span)
    block = (tile, model)
    by_row = lambda n: (n, 0)
    below = number * (span // tile)
    sums = [array for pair in terms for array in pair]
    return call(
        input_kernel,
        "input_grad",
        (span // tile,),
        [
            (tokens, block, lambda n: (n + below, 0)),
            (gain, (1, model), None),
            (grads, block, by_row),
        ]
        + [(array, (tile, array.shape[1]), by_row) for array in sums],
        [((count, span, model), BF16, (None, *block), lambda n: (number, n, 0))],
        [],
        2e-6 * span * model,
        after,
        None,
        None if into is None else [into],
    )[0]


def finish_kernel(own, far, out):
    out[...] = (own[...].astype(F32) + far[...].astype(F32)).T


def finish_rows(rows, far, after=()):
    chunk, width = far.shape
    tile = min(512, width)
    return call(
        finish_kernel,
        "finish",
        (width // tile,),
        [
            (rows, (chunk, tile), lambda n: (1, n)),
            (far, (chunk, tile), lambda n: (0, n)),
        ],
        [((width, chunk), F32, (tile, chunk), lambda n: (n, 0))],
        [],
        2e-6 * chunk * width,
        after,
    )[0]


class ScatterSum:
    def __init__(self, parts, groups, z_first=False):
        away, self.kept = parts
        self.groups, self.z_first = groups, z_first
        self.got = exchange(away, "seq", groups, 1)

    def mates(self, after=()):
        rows = self.kept.shape[0]
        pair = [(self.kept, 0, 0), (self.got, 0, 0)]
        if self.z_first:
            near = add(pair, rows, after)
            self.rows = lax.psum_scatter(near, "dp", scatter_dimension=0, tiled=True)
        else:
            near = add(pair, rows // 2, after)
            self.far = exchange(near, "seq", self.groups, 2)
        return near

    def own(self, after=(), us=None):
        half = self.kept.shape[0] // 2
        pieces = [(self.kept, half, 0), (self.got, half, 0), (self.far, 0, 0)]
        return add(pieces, half, after, None, us)

    def finish(self, after=()):
        half = self.rows.shape[0] // 2
        far = exchange(self.rows[:half], "seq", self.groups, 2)
        return finish_rows(self.rows, far, after)

    def chips(self, after=(), us=None):
        own = self.own(after, us)
        self.raw = lax.psum_scatter(own, "dp", scatter_dimension=0, tiled=True)
        self.out = self.raw.astype(F32)
        return own


def mp_sum(low, units):
    if units != 2:
        return lax.psum(low, "mp"), jnp.zeros_like(low)
    return low, exchange(low, "mp", 2, 1)


def mp_rows(sums, units):
    if units != 2:
        return lax.psum(sums, "mp"), jnp.zeros_like(sums)
    return sums, exchange(sums, "mp", 2, 1)


def axis_sum(array, axis, size):
    return sum([exchange(array, axis, size, offset) for offset in range(1, size)], array)


def in_order(pieces, place):
    stacked = jnp.stack(pieces)
    return [
        lax.dynamic_index_in_dim(stacked, jnp.bitwise_xor(place, n), 0, False)
        for n in range(len(pieces))
    ]


def pass_round(pieces, groups):
    return [pieces[0]] + [exchange(pieces[n], "seq", groups, n) for n in range(1, groups)]


def xpos_tables(count, lanes):
    positions = jnp.arange(count, dtype=F32)
    pair_index = jnp.arange(HALF, dtype=F32)
    frequency = 1.0 / 10000.0 ** (2.0 * pair_index / HEAD_DIM)
    angles = positions[:, None] * frequency[None, :]
    base_ratio = (2.0 * pair_index + 0.4 * HEAD_DIM) / (1.4 * HEAD_DIM)
    growth = base_ratio[None, :] ** ((positions[:, None] - count // 2) / XPOS_BASE)
    cosine, sine = jnp.cos(angles), jnp.sin(angles)
    tables = []
    for factor in (growth, 1.0 / growth):
        tables.append(jnp.tile(cosine * factor, (1, lanes // HALF)))
        tables.append(
            jnp.tile(jnp.concatenate([-sine * factor, sine * factor], axis=1), (1, lanes // HEAD_DIM))
        )
    return tables


def body(
    devices,
    groups,
    units,
    tokens,
    lengths,
    qkv_weight,
    out_weight,
    in_weight,
    down_weight,
    gain_in,
    gain_attn,
    gain_mid,
    gain_ffn,
    out_grad,
):
    sequences, span, model = tokens.shape
    each = range(sequences)
    data = ("dp", "seq")
    shards = devices * groups
    place = lax.axis_index("seq").astype(jnp.int32)
    local_width = qkv_weight.shape[2]
    heads_here = local_width // HEAD_DIM
    ffn_width = in_weight.shape[1]
    share = local_width // groups

    blocks = []
    for s in each:
        far = exchange(tokens[s], "seq", groups, 2)
        blocks.append([tokens[s], exchange(tokens[s], "seq", groups, 1), far])
    blocks[0].append(exchange(blocks[0][2], "seq", groups, 1))

    number = lax.axis_index("dp") * groups + place
    sizes = [gain_in.size, gain_mid.size, gain_attn.size, gain_ffn.size]
    cuts = [sum(sizes[:n]) for n in range(5)]
    chunk = qkv_weight.shape[1]
    by_device = qkv_weight.reshape(3, chunk, groups, share).transpose(2, 1, 0, 3)
    by_device = by_device.reshape(groups, chunk, 3 * share)
    flat = jnp.concatenate([gain_in, gain_mid, gain_attn.reshape(-1), gain_ffn.reshape(-1)])
    flat = jnp.pad(flat, (0, 16 * 3 * share - cuts[4])).reshape(16, 3 * share)
    pieces = [
        jnp.concatenate(
            [
                lax.dynamic_index_in_dim(by_device, jnp.bitwise_xor(place, n), 0, False),
                flat,
            ]
        )
        for n in range(groups)
    ]
    pieces = in_order(pass_round(pieces, groups), place)
    rows = jnp.concatenate([piece[:chunk] for piece in pieces], axis=0)
    rows = relay(rows, [blocks[s][0] for s in each])
    heads_weight = lax.all_gather(rows, "dp", axis=0, tiled=True)

    flat = jnp.stack([piece[chunk:].reshape(-1)[: cuts[4]] for piece in pieces]).reshape(1, -1)
    row = lax.broadcasted_iota(jnp.int32, (devices, 1), 0)
    all_gains = jnp.where(row == lax.axis_index("dp"), flat, 0).astype(F32)
    all_gains = axis_sum(all_gains, "dp", devices).reshape(shards, cuts[4])
    pieces = [all_gains[:, cuts[n] : cuts[n + 1]] for n in range(4)]
    gain_one, gain_three = pieces[0].reshape(1, -1), pieces[1].reshape(1, -1)
    gain_two = pieces[2].reshape(shards, heads_here, -1).transpose(1, 0, 2).reshape(1, -1)
    gain_four = (
        pieces[3].reshape(shards, ffn_width // HEAD_DIM, -1).transpose(1, 0, 2).reshape(1, -1)
    )

    near_full = lax.all_gather(
        pack(in_weight, out_weight, [all_gains, blocks[0][2]]), data, axis=0, tiled=True
    )
    down_full = lax.all_gather(down_weight, data, axis=1, tiled=True)

    count = span * groups
    tables = xpos_tables(count, min(128, share))
    spot = place.reshape(1)
    metas = [jnp.stack([lengths[s], place]) for s in each]
    full_units = ffn_width * units

    first_low, projected = [], []
    mixed, logs, attended, att_sums, inner, branch = [], [], [], [], [], []
    last = ()
    for s in each:
        low, made = project(spot, blocks[s], gain_one, heads_weight, tables, last)
        first_low.append(low)
        projected.append(made)
        outs, log = attend(metas[s], made, groups)
        mixed.append(outs)
        logs.append(log)
        last = [log]
        if s == 0:
            far = relay(blocks[1][2], last)
            blocks[1].append(exchange(far, "seq", groups, 1))
            last = [far]
    passed = [pass_round(mixed[s], groups) for s in each]
    last = [*last, *passed[-1][1:]]
    for s in each:
        whole, sums = collect(spot, passed[s], last)
        attended.append(whole)
        att_sums.append(mp_rows(sums, units))
        last = [sums]
    last = [other for _, other in att_sums]
    for s in each:
        parts = 2 if s == sequences - 1 else 1
        low, terms = out_branch(attended[s], *att_sums[s], gain_two, near_full, model, parts, last)
        inner.append(low)
        branch.append([mp_sum(part, units) for part in terms])
        last = [terms[-1]]

    flat_tokens = tokens.reshape(sequences * span, model)
    flat_grads = out_grad.reshape(sequences * span, model)
    hidden, third_low, active, slope, act_sums = [], [], [], [], []
    for s in each:
        made = None
        for n, part in enumerate(branch[s]):
            made = widen(
                s, n, len(branch[s]), flat_tokens, *part, gain_three, near_full, ffn_width, made, last
            )
            last = [made[4]]
        hidden.append(made[0])
        third_low.append(made[1])
        active.append(made[2])
        slope.append(made[3])
        act_sums.append(mp_rows(made[4], units))
        last = [made[4]]

    own_sums, other_sums = [a for a, _ in act_sums], [b for _, b in act_sums]
    norm = (own_sums, other_sums, gain_four, full_units)
    down_parts = weight_grad(spot, [flat_grads], active, devices, groups, norm, True, last)
    down_sum = ScatterSum(down_parts, groups, True)
    last = [down_parts[0]]
    pre_low, third_terms = [], []
    scaled, back_sums, gain_four_grad = wide_back(
        flat_grads, down_full, active, own_sums, other_sums, gain_four, full_units, last
    )
    last = [back_sums[-1]]
    back_sums = [mp_rows(sums, units) for sums in back_sums]
    last = [down_sum.mates(last)] + [other for _, other in back_sums]
    for s in each:
        low, terms = pre_back(
            scaled[s], active[s], slope[s], *act_sums[s], *back_sums[s], near_full, full_units,
            last,
        )
        pre_low.append(low)
        third_terms.append(mp_sum(terms, units))
        last = [terms]

    gain_three_grad, gain_two_grad, gain_one_grad = 0.0, 0.0, 0.0
    order = jnp.bitwise_xor(place, jnp.array([3, 1, 2, 0], jnp.int32))
    grad_hidden, hidden_low, grads, projected_grads = [], [], [], []
    wide_terms = narrow(
        active, own_sums, other_sums, gain_four, down_full, full_units, last
    )
    last = [wide_terms]
    wide_terms = mp_sum(wide_terms, units)
    for s in each:
        made = middle(
            s, flat_grads, *third_terms[s], hidden[s], gain_three, near_full, attended[s],
            *att_sums[s], gain_two, model, last
        )
        grad_hidden.append(made[0])
        hidden_low.append(made[1])
        gain_three_grad += made[4]
        gain_two_grad += made[5]
        if s == 0:
            in_parts = weight_grad(
                spot, third_low, pre_low, devices, groups, None, False, [made[3]]
            )
            in_sum = ScatterSum(in_parts, groups)
            last = [in_parts[0], third_terms[1][1]]
        else:
            last = [in_sum.mates([made[3]])]
        parts = share_out(
            spot, made[2], attended[s], *att_sums[s], *mp_rows(made[3], units), model, groups,
            last, MIDDLE_PAUSE if s == 0 else None,
        )
        last = [parts[0]]
        grads.append(pass_round(parts, groups))
    last += [down_sum.rows]
    out_parts = weight_grad(spot, hidden_low, inner, devices, groups, None, True, last)
    out_sum = ScatterSum(out_parts, groups, True)
    last = [out_parts[0], *grads[1][1:]]
    for s in each:
        made = attend_back(
            metas[s], projected[s], grads[s], mixed[s], logs[s], tables, last,
            BACK_WEIGHT if s == 0 else 1,
        )
        projected_grads.append(made)
        last = [made]
        if s == 0:
            last = [out_sum.mates(last)]
        else:
            first_terms = mp_sum(join_halves(kept, got[2:], far, last), units)
            last = [first_terms[0]]
        away, kept, gain_part = first_back(
            order, made, first_low[s], heads_weight, gain_one, groups, last
        )
        gain_one_grad += gain_part
        got = [exchange(piece, "seq", groups, 1) for piece in away]
        if s == 0:
            near = add_halves(kept, *got[:2], [kept])
            far = [exchange(piece, "seq", groups, 2) for piece in near]
            last = [in_sum.chips([near[0]])]
        else:
            gain_one_sums = mp_rows(gain_one_grad, units)
            results = result_rows(*wide_terms, hidden, [kept], PAUSE)
            near = add_halves(kept, *got[:2], [results])
            last = [near[0], in_sum.raw, out_sum.rows]

    heads_part = heads_grad(first_low, projected_grads, last)
    heads_rows = lax.psum_scatter(heads_part, "dp", scatter_dimension=0, tiled=True)

    def input_grad(s, terms, into, after):
        return input_rows(
            s, sequences, flat_tokens, terms, gain_one, grad_hidden[s], into, after
        )

    gain_rows = jnp.concatenate(
        [
            (gain_one_sums[0] + gain_one_sums[1]).reshape(shards, -1),
            gain_three_grad.reshape(shards, -1),
            gain_two_grad.reshape(heads_here, shards, -1).transpose(1, 0, 2).reshape(shards, -1),
            gain_four_grad.reshape(ffn_width // HEAD_DIM, shards, -1)
            .transpose(1, 0, 2)
            .reshape(shards, -1),
        ],
        axis=1,
    )
    terms = []
    last = [heads_part, gain_one_sums[1]]
    for n, part in enumerate(near):
        far = exchange(part, "seq", groups, 2)
        column = n * (model // 2)
        own = add(
            [(kept, span, column), (got[2 + n], 0, 0), (far, 0, 0)],
            span,
            last,
            model // 2,
            None if n == 0 else LONG_PAUSE,
        )
        terms.append(mp_sum(own, units))
        if n == 0:
            gain_rows = relay(gain_rows, [own])
            grad_input = input_grad(0, [first_terms], None, [gain_rows])
            gain_rows = axis_sum(gain_rows, "dp", devices)
            last = [terms[0][1], gain_rows, grad_input]
    gain_rows = relay(gain_rows, [own])
    grad_down = down_sum.finish([gain_rows])
    grad_out = out_sum.finish([grad_down])
    gain_rows = axis_sum(gain_rows, "seq", groups)
    pieces = [
        lax.dynamic_slice_in_dim(heads_rows, jnp.bitwise_xor(place, n) * chunk, chunk, 0)
        for n in range(groups)
    ]
    pieces = pass_round(pieces, groups)
    grad_input = input_grad(1, terms, grad_input, [gain_rows, grad_out])
    rows = jnp.stack(in_order(pieces, place)).astype(F32)
    grad_qkv_w = rows.reshape(groups, chunk, 3, share).transpose(2, 1, 0, 3)
    grad_qkv_w = grad_qkv_w.reshape(3, chunk, local_width)
    gain_sums = lax.dynamic_index_in_dim(gain_rows, number, 0, False)
    one, three, two, four = [gain_sums[cuts[n] : cuts[n + 1]] for n in range(4)]
    return (
        results.reshape(sequences, span, model),
        grad_input,
        grad_qkv_w,
        grad_out,
        in_sum.out,
        grad_down,
        one,
        two.reshape(gain_attn.shape),
        three,
        four.reshape(gain_ffn.shape),
    )


def solution(mesh):
    sizes = mesh.shape
    data = ("dp", "seq")
    in_specs = (
        P("dp", "seq", None),
        P("dp"),
        P(None, data, "mp"),
        P("mp", data),
        P(data, "mp"),
        P("mp", data),
        P(data),
        P("mp", data),
        P(data),
        P("mp", data),
        P("dp", "seq", None),
    )
    out_specs = (
        P("dp", "seq", None),
        P("dp", "seq", None),
        P(None, data, "mp"),
        P("mp", data),
        P(data, "mp"),
        P("mp", data),
        P(data),
        P("mp", data),
        P(data),
        P("mp", data),
    )
    run = partial(body, sizes["dp"], sizes["seq"], sizes["mp"])
    return jax.shard_map(run, mesh=mesh, in_specs=in_specs, out_specs=out_specs, check_vma=False)
```
